32 devices in a mesh: dp: 16 (over z, y, x), mp: 2 (over core).
Axes of the slice: x: 2, y: 2, z: 4, core: 2. Of those that a mesh axis runs over, the one named last changes fastest.
Arguments:
- series: bfloat16 [896, 32, 336], P('mp', 'dp'), may hold values from -6 to 6
- groups: int32 [32], P('dp'), may hold values from 0 to 2
- counts: int32 [32], P('dp'), may hold values from 574 to 862, as said below
- cotangent: bfloat16 [896, 32, 512], P('mp', 'dp'), may hold values from -18 to 18
- embed_weight: float32 [3, 336, 512], replicated, may hold values from -0.3125 to 0.3125
- embed_moment: float32 [3, 336, 512], replicated, may hold values from -6 to 6
- embed_error: float32 [16, 3, 336, 512], P('dp'), may hold values from -80 to 80
- embed_start: float32 [512, 8], replicated, may hold values from -6 to 6
- attend_weight: float32 [512, 3, 512], P(None, None, 'mp'), may hold values from -0.25 to 0.25
- attend_moment: float32 [512, 3, 512], P(None, None, 'mp'), may hold values from -6 to 6
- attend_error: float32 [16, 512, 3, 512], P('dp', None, None, 'mp'), may hold values from -80 to 80
- attend_start: float32 [3, 512, 8], P(None, 'mp'), may hold values from -6 to 6
- mixer_weight: float32 [512, 512], P('mp'), may hold values from -2 to 2
- mixer_moment: float32 [512, 512], P('mp'), may hold values from -6 to 6
- mixer_error: float32 [16, 512, 512], P('dp', 'mp'), may hold values from -80 to 80
- mixer_start: float32 [2, 512, 8], P('mp'), may hold values from -6 to 6
- inner_weight: float32 [512, 2048], P(None, 'mp'), may hold values from -0.25 to 0.25
- inner_moment: float32 [512, 2048], P(None, 'mp'), may hold values from -6 to 6
- inner_error: float32 [16, 512, 2048], P('dp', None, 'mp'), may hold values from -80 to 80
- inner_start: float32 [2048, 8], P('mp'), may hold values from -6 to 6
- outer_weight: float32 [2048, 512], P('mp'), may hold values from -0.125 to 0.125
- outer_moment: float32 [2048, 512], P('mp'), may hold values from -6 to 6
- outer_error: float32 [16, 2048, 512], P('dp', 'mp'), may hold values from -80 to 80
- outer_start: float32 [2, 512, 8], P('mp'), may hold values from -6 to 6
- embed_bias: float32 [3, 512], replicated, may hold values from -1.75 to 1.75
- embed_bias_moment: float32 [3, 512], replicated, may hold values from -6 to 6
- query_bias: float32 [2, 512], P(None, 'mp'), may hold values from -1.75 to 1.75
- query_bias_moment: float32 [2, 512], P(None, 'mp'), may hold values from -6 to 6
- inner_bias: float32 [2048], P('mp'), may hold values from -1.75 to 1.75
- inner_bias_moment: float32 [2048], P('mp'), may hold values from -6 to 6
- norm_gains: float32 [2, 512], replicated, may hold values from 0.5 to 1.5
- gains_moment: float32 [2, 512], replicated, may hold values from -6 to 6
- shared_biases: float32 [4, 512], replicated, may hold values from -1.75 to 1.75
- biases_moment: float32 [4, 512], replicated, may hold values from -6 to 6
Outputs:
- output: float32 [896, 32, 512], P('mp', 'dp')
- series_grad: float32 [896, 32, 336], P('mp', 'dp')
- embed_weight_new: float32 [3, 336, 512], replicated
- embed_moment_new: float32 [3, 336, 512], replicated
- embed_error_new: float32 [16, 3, 336, 512], P('dp')
- embed_left: float32 [3, 336, 8], replicated
- embed_right: float32 [512, 8], replicated
- attend_weight_new: float32 [512, 3, 512], P(None, None, 'mp')
- attend_moment_new: float32 [512, 3, 512], P(None, None, 'mp')
- attend_error_new: float32 [16, 512, 3, 512], P('dp', None, None, 'mp')
- attend_left: float32 [2, 512, 8], P('mp')
- attend_right: float32 [3, 512, 8], P(None, 'mp')
- mixer_weight_new: float32 [512, 512], P('mp')
- mixer_moment_new: float32 [512, 512], P('mp')
- mixer_error_new: float32 [16, 512, 512], P('dp', 'mp')
- mixer_left: float32 [512, 8], P('mp')
- mixer_right: float32 [2, 512, 8], P('mp')
- inner_weight_new: float32 [512, 2048], P(None, 'mp')
- inner_moment_new: float32 [512, 2048], P(None, 'mp')
- inner_error_new: float32 [16, 512, 2048], P('dp', None, 'mp')
- inner_left: float32 [2, 512, 8], P('mp')
- inner_right: float32 [2048, 8], P('mp')
- outer_weight_new: float32 [2048, 512], P('mp')
- outer_moment_new: float32 [2048, 512], P('mp')
- outer_error_new: float32 [16, 2048, 512], P('dp', 'mp')
- outer_left: float32 [2048, 8], P('mp')
- outer_right: float32 [2, 512, 8], P('mp')
- embed_bias_moment_new: float32 [3, 512], replicated
- embed_bias_new: float32 [3, 512], replicated
- query_bias_moment_new: float32 [2, 512], P(None, 'mp')
- query_bias_new: float32 [2, 512], P(None, 'mp')
- inner_bias_moment_new: float32 [2048], P('mp')
- inner_bias_new: float32 [2048], P('mp')
- gains_moment_new: float32 [2, 512], replicated
- norm_gains_new: float32 [2, 512], replicated
- biases_moment_new: float32 [4, 512], replicated
- shared_biases_new: float32 [4, 512], replicated
The draws below stay inside these ranges and needn't reach their ends.
Inputs may be any that keep to these rules, and one draw needn't show every extreme that they name: `counts`: some window has exactly 862 live variates.
All inputs are finite; a program needn't handle non-finite values.
Results may differ from the reference program's by a relative error of at most 0.02.
Values may be sent and summed in bfloat16 or wider, within the bound.
A program may use at most 256 MiB of HBM per device.

```python
import math
import jax
import jax.numpy as jnp
from jax import lax

D = 512
HEADS = 8
HEAD_DIM = 64
FF = 2048
NVAR = 862
VSLOT = 896
LMAX = 336
GROUPS = 3
RANK = 8
WIN_DEV = 2
WINS = 32
N_DP = 16
N_MP = 2


def draw_counts(key, part):
    key = jax.random.fold_in(key, 11)
    first_key, second_key = jax.random.split(key)
    drawn = jax.random.randint(first_key, (WINS,), NVAR * 2 // 3, NVAR + 1, dtype=jnp.int32)
    chosen = jax.random.randint(second_key, (), 0, WINS, dtype=jnp.int32)
    return jnp.where(jnp.arange(WINS, dtype=jnp.int32) == chosen, NVAR, drawn).astype(jnp.int32)


def draw_cotangent(key, part):
    key = jax.random.fold_in(key, 23)
    ramp = jnp.arange(WINS, dtype=jnp.float32) / max(WINS - 1, 1)
    factor = 1.0 + 2.0 * ramp
    base = jnp.clip(jax.random.normal(key, (VSLOT, WINS, D), jnp.float32), -6.0, 6.0)
    return (base * factor[None, :, None]).astype(jnp.bfloat16)


def plant(values, stream_key, least, top_value):
    longest = values.shape.index(max(values.shape))
    spots = []
    for shift in (0, 1):
        where = [jax.random.randint(jax.random.fold_in(stream_key, axis), (), 0, length) for axis, length in enumerate(values.shape)]
        where[longest] = (where[longest] + shift) % values.shape[longest]
        spots.append(tuple(where))
    return values.at[spots[0]].set(least).at[spots[1]].set(top_value)


def shard_levels(rng, extent, cuts, least, top_value):
    gain = 1.0
    for axis_at, parts in cuts:
        steps = jax.random.uniform(jax.random.fold_in(jax.random.fold_in(rng, 6), axis_at), (parts,), jnp.float32, least / len(cuts), top_value / len(cuts))
        gain = gain * jnp.repeat(jnp.exp(steps), extent[axis_at] // parts).reshape((-1,) + (1,) * (len(extent) - 1 - axis_at))
    return gain


def bell_draw(stream_key, dims, scale, bound, pieces=(), held_as=jnp.bfloat16):
    values = scale * jax.random.normal(stream_key, dims, jnp.float32)
    if pieces:
        values = values * shard_levels(stream_key, dims, pieces, -0.22, 0.18)
    return jnp.clip(values, -bound, bound).astype(held_as)


def setup_inputs(seed: int = 0) -> dict:
    seeds = jax.random.split(jax.random.key(seed), 35)
    return {
        "series": bell_draw(seeds[0], (VSLOT, WINS, LMAX), 1.0, 6.0, ((0, 2), (1, 16))),
        "groups": plant(jax.random.randint(seeds[1], (WINS,), 0, 3), jax.random.fold_in(seeds[1], 1), 0, 2).astype(jnp.int32),
        "counts": draw_counts(jax.random.fold_in(seeds[34], 71), 0),
        "cotangent": draw_cotangent(jax.random.fold_in(seeds[34], 71), 0),
        "embed_weight": bell_draw(seeds[4], (GROUPS, LMAX, D), LMAX ** -0.5, 0.3125, (), jnp.float32),
        "embed_moment": bell_draw(seeds[5], (GROUPS, LMAX, D), (0.1 * (WIN_DEV * VSLOT) ** 0.5 * N_DP ** -0.5), 6.0, (), jnp.float32),
        "embed_error": bell_draw(seeds[6], (N_DP, GROUPS, LMAX, D), (0.3 * (WIN_DEV * VSLOT) ** 0.5), 80.0, ((0, 16),), jnp.float32),
        "embed_start": bell_draw(seeds[7], (D, RANK), 1.0, 6.0, (), jnp.float32),
        "attend_weight": bell_draw(seeds[8], (D, 3, D), D ** -0.5, 0.25, ((2, 2),), jnp.float32),
        "attend_moment": bell_draw(seeds[9], (D, 3, D), (0.1 * (WIN_DEV * VSLOT) ** 0.5 * N_DP ** -0.5), 6.0, ((2, 2),), jnp.float32),
        "attend_error": bell_draw(seeds[10], (N_DP, D, 3, D), (0.3 * (WIN_DEV * VSLOT) ** 0.5), 80.0, ((0, 16), (3, 2)), jnp.float32),
        "attend_start": bell_draw(seeds[11], (3, D, RANK), 1.0, 6.0, ((1, 2),), jnp.float32),
        "mixer_weight": bell_draw(seeds[12], (D, D), (max(D * 16 // VSLOT, 1)) ** -0.5, 2.0, ((0, 2),), jnp.float32),
        "mixer_moment": bell_draw(seeds[13], (D, D), (0.1 * (WIN_DEV * VSLOT) ** 0.5 * N_DP ** -0.5), 6.0, ((0, 2),), jnp.float32),
        "mixer_error": bell_draw(seeds[14], (N_DP, D, D), (0.3 * (WIN_DEV * VSLOT) ** 0.5), 80.0, ((0, 16), (1, 2)), jnp.float32),
        "mixer_start": bell_draw(seeds[15], (N_MP, D, RANK), 1.0, 6.0, ((0, 2),), jnp.float32),
        "inner_weight": bell_draw(seeds[16], (D, FF), D ** -0.5, 0.25, ((1, 2),), jnp.float32),
        "inner_moment": bell_draw(seeds[17], (D, FF), (0.1 * (WIN_DEV * VSLOT) ** 0.5 * N_DP ** -0.5), 6.0, ((1, 2),), jnp.float32),
        "inner_error": bell_draw(seeds[18], (N_DP, D, FF), (0.3 * (WIN_DEV * VSLOT) ** 0.5), 80.0, ((0, 16), (2, 2)), jnp.float32),
        "inner_start": bell_draw(seeds[19], (FF, RANK), 1.0, 6.0, ((0, 2),), jnp.float32),
        "outer_weight": bell_draw(seeds[20], (FF, D), FF ** -0.5, 0.125, ((0, 2),), jnp.float32),
        "outer_moment": bell_draw(seeds[21], (FF, D), (0.1 * (WIN_DEV * VSLOT) ** 0.5 * N_DP ** -0.5), 6.0, ((0, 2),), jnp.float32),
        "outer_error": bell_draw(seeds[22], (N_DP, FF, D), (0.3 * (WIN_DEV * VSLOT) ** 0.5), 80.0, ((0, 16), (1, 2)), jnp.float32),
        "outer_start": bell_draw(seeds[23], (N_MP, D, RANK), 1.0, 6.0, ((0, 2),), jnp.float32),
        "embed_bias": bell_draw(seeds[24], (GROUPS, D), 0.3, 1.75, (), jnp.float32),
        "embed_bias_moment": bell_draw(seeds[25], (GROUPS, D), (0.1 * (WIN_DEV * VSLOT) ** 0.5 * N_DP ** -0.5), 6.0, (), jnp.float32),
        "query_bias": bell_draw(seeds[26], (2, D), 0.3, 1.75, ((1, 2),), jnp.float32),
        "query_bias_moment": bell_draw(seeds[27], (2, D), (0.1 * (WIN_DEV * VSLOT) ** 0.5 * N_DP ** -0.5), 6.0, ((1, 2),), jnp.float32),
        "inner_bias": bell_draw(seeds[28], (FF,), 0.3, 1.75, ((0, 2),), jnp.float32),
        "inner_bias_moment": bell_draw(seeds[29], (FF,), (0.1 * (WIN_DEV * VSLOT) ** 0.5 * N_DP ** -0.5), 6.0, ((0, 2),), jnp.float32),
        "norm_gains": jnp.clip(1.0 + 0.1 * jax.random.normal(seeds[30], (2, D), jnp.float32), 0.5, 1.5),
        "gains_moment": bell_draw(seeds[31], (2, D), (0.1 * (WIN_DEV * VSLOT) ** 0.5 * N_DP ** -0.5), 6.0, (), jnp.float32),
        "shared_biases": bell_draw(seeds[32], (4, D), 0.3, 1.75, (), jnp.float32),
        "biases_moment": bell_draw(seeds[33], (4, D), (0.1 * (WIN_DEV * VSLOT) ** 0.5 * N_DP ** -0.5), 6.0, (), jnp.float32),
    }


@jax.custom_vjp
def low(v):
    return lax.optimization_barrier(v.astype(jnp.bfloat16)).astype(jnp.float32)

@jax.custom_vjp
def low_back(v):
    return v

def low_keep(v):
    return (low(v), None)

def low_pass(kept, grad):
    return (grad,)

def back_keep(v):
    return (v, None)

def back_low(kept, grad):
    return (low(grad),)
low.defvjp(low_keep, low_pass)
low_back.defvjp(back_keep, back_low)
highest = lax.Precision.HIGHEST
momentum_decay = 0.9
norm_epsilon = 1e-05
base_rate = 0.03

def lookbacks(groups):
    return jnp.where(groups == 0, LMAX * 2 // 7, jnp.where(groups == 1, LMAX * 4 // 7, LMAX)).astype(jnp.int32)

def gelu_exact(values):
    return values * 0.5 * (1.0 + jax.scipy.special.erf(values * 0.7071067811865476))

def layer_norm(values, norm_gain, norm_shift):
    centered = values - lax.optimization_barrier(jnp.mean(values, axis=-1, keepdims=True))
    spread = lax.optimization_barrier(jnp.mean(centered * centered, axis=-1, keepdims=True))
    return centered * lax.rsqrt(spread + norm_epsilon) * norm_gain + norm_shift

def forward(parameters, series, groups, counts):
    embed_weight, attend_weight, mixer_weight, inner_weight, outer_weight, embed_bias, query_bias, inner_bias, norm_gains, shared_biases = parameters
    row_total = series.shape[0]
    windows = series.shape[1]
    columns = jnp.arange(LMAX, dtype=jnp.int32)
    in_window = (columns[None, :] >= LMAX - lookbacks(groups)[:, None]).astype(jnp.float32)
    picked = (groups[:, None] == jnp.arange(GROUPS, dtype=jnp.int32)[None, :]).astype(jnp.float32)
    embed_table = jnp.einsum('wg,gld->wld', picked, low(embed_weight), precision=highest)
    hidden = jnp.einsum('swl,wld->swd', series * in_window[None], embed_table, precision=highest)
    hidden = low_back(hidden + jnp.dot(picked, embed_bias, precision=highest)[None])
    tokens = low(hidden)
    triple_bias = jnp.stack([query_bias[0], jnp.zeros((D,), jnp.float32), query_bias[1]])
    projected = jnp.einsum('swd,dke->swke', tokens, low(attend_weight), precision=highest) + triple_bias
    projected = low(low_back(projected)).reshape(row_total, windows, 3, HEADS, HEAD_DIM)
    scores = jnp.einsum('swhe,twhe->whst', projected[:, :, 0], projected[:, :, 1], precision=highest) * HEAD_DIM ** (-0.5)
    scores = low_back(scores)
    key_live = jnp.arange(row_total, dtype=jnp.int32)[None, :] < counts[:, None]
    scores = jnp.where(key_live[:, None, None, :], scores, -1e+30)
    softmax_weights = low(jax.nn.softmax(scores, axis=-1))
    context = jnp.einsum('whst,twhe->swhe', softmax_weights, projected[:, :, 2], precision=highest)
    context = low(low_back(context.reshape(row_total, windows, D)))
    attended = low_back(jnp.einsum('swe,ed->swd', context, low(mixer_weight), precision=highest))
    normed = layer_norm(hidden + attended + shared_biases[2], norm_gains[0], shared_biases[0])
    preact = jnp.einsum('swd,df->swf', low(normed), low(inner_weight), precision=highest) + inner_bias
    preact = low_back(preact)
    feed_out = jnp.einsum('swf,fd->swd', low(gelu_exact(preact)), low(outer_weight), precision=highest)
    return layer_norm(normed + low_back(feed_out) + shared_biases[3], norm_gains[1], shared_biases[1])

def orthonormal(left_factor):
    columns = []
    for column in range(left_factor.shape[1]):
        vector = left_factor[:, column]
        for earlier in columns:
            vector = vector - jnp.sum(earlier * vector) * earlier
        columns.append(vector * lax.rsqrt(jnp.sum(vector * vector) + 1e-12))
    return jnp.stack(columns, axis=1)

def compress(stacked, anchor):
    left_factor = lax.optimization_barrier(jnp.sum(jnp.einsum('rnm,mk->rnk', stacked, anchor, precision=highest), axis=0)) / N_DP
    left_factor = orthonormal(left_factor)
    right_factor = lax.optimization_barrier(jnp.sum(jnp.einsum('rnm,nk->rmk', stacked, left_factor, precision=highest), axis=0)) / N_DP
    approx = jnp.dot(left_factor, right_factor.T, precision=highest)
    return (left_factor, right_factor, approx, stacked - approx[None])

def split_windows(array):
    return jnp.swapaxes(array.reshape(array.shape[0], N_DP, WIN_DEV, array.shape[2]), 0, 1)

def join_windows(array):
    return jnp.swapaxes(array, 0, 1).reshape(array.shape[1], N_DP * WIN_DEV, array.shape[3])

def rows_split(stacked):
    return jnp.swapaxes(stacked.reshape(N_DP, N_MP, stacked.shape[1] // N_MP, stacked.shape[2]), 0, 1)

def rows_join(shards):
    return jnp.swapaxes(shards, 0, 1).reshape(N_DP, -1, shards.shape[3])

def cols_split(stacked):
    return jnp.transpose(stacked.reshape(N_DP, stacked.shape[1], N_MP, stacked.shape[2] // N_MP), (2, 0, 1, 3))

def cols_join(shards):
    return jnp.transpose(shards, (1, 2, 0, 3)).reshape(N_DP, shards.shape[2], -1)

def renew(weight, moment, update, step_rate):
    new_moment = momentum_decay * moment + update
    return (weight - step_rate * new_moment, new_moment)

def reference(series, groups, counts, cotangent, embed_weight, embed_moment, embed_error, embed_start, attend_weight, attend_moment, attend_error, attend_start, mixer_weight, mixer_moment, mixer_error, mixer_start, inner_weight, inner_moment, inner_error, inner_start, outer_weight, outer_moment, outer_error, outer_start, embed_bias, embed_bias_moment, query_bias, query_bias_moment, inner_bias, inner_bias_moment, norm_gains, gains_moment, shared_biases, biases_moment):
    parameters = (embed_weight, attend_weight, mixer_weight, inner_weight, outer_weight, embed_bias, query_bias, inner_bias, norm_gains, shared_biases)

    def per_replica(stacked):
        local_series, local_groups, local_counts, local_cotangent = stacked
        live_rows = (jnp.arange(VSLOT, dtype=jnp.int32)[:, None] < local_counts[None, :]).astype(jnp.float32)

        def run(values, inputs):
            return forward(values, inputs, local_groups, local_counts)
        result, pullback = jax.vjp(run, parameters, local_series.astype(jnp.float32))
        gradients, series_gradient = pullback(local_cotangent.astype(jnp.float32) * live_rows[:, :, None])
        return (result, series_gradient, gradients)
    results, series_grads, gradients = lax.map(per_replica, (split_windows(series), groups.reshape(N_DP, WIN_DEV), counts.reshape(N_DP, WIN_DEV), split_windows(cotangent)))
    output = join_windows(results)
    series_grad = join_windows(series_grads)
    step_rate = base_rate * math.sqrt(N_DP * 7 / (WIN_DEV * VSLOT))
    mixer_rate = step_rate * math.sqrt(D / max(D * 16 // VSLOT, 1))
    slice_width = D // N_MP
    inner_slice = FF // N_MP
    embed_left, embed_right, embed_approx, embed_residue = compress((gradients[0] + embed_error).reshape(N_DP, GROUPS * LMAX, D), embed_start)
    embed_new, embed_moment_new = renew(embed_weight, embed_moment, embed_approx.reshape(GROUPS, LMAX, D), step_rate)
    attend_stack = jnp.transpose((gradients[1] + attend_error).reshape(N_DP, D, 3, N_MP, slice_width), (3, 0, 1, 2, 4)).reshape(N_MP, N_DP, D, 3 * slice_width)
    attend_anchor = jnp.transpose(attend_start.reshape(3, N_MP, slice_width, RANK), (1, 0, 2, 3)).reshape(N_MP, 3 * slice_width, RANK)
    attend_left, attend_right, attend_approx, attend_residue = jax.vmap(compress)(attend_stack, attend_anchor)
    attend_approx = jnp.transpose(attend_approx.reshape(N_MP, D, 3, slice_width), (1, 2, 0, 3)).reshape(D, 3, D)
    attend_residue = jnp.transpose(attend_residue.reshape(N_MP, N_DP, D, 3, slice_width), (1, 2, 3, 0, 4)).reshape(N_DP, D, 3, D)
    attend_right = jnp.transpose(attend_right.reshape(N_MP, 3, slice_width, RANK), (1, 0, 2, 3)).reshape(3, D, RANK)
    attend_new, attend_moment_new = renew(attend_weight, attend_moment, attend_approx, step_rate)
    mixer_left, mixer_right, mixer_approx, mixer_residue = jax.vmap(compress)(rows_split(gradients[2] + mixer_error), mixer_start)
    mixer_new, mixer_moment_new = renew(mixer_weight, mixer_moment, mixer_approx.reshape(D, D), mixer_rate)
    inner_left, inner_right, inner_approx, inner_residue = jax.vmap(compress)(cols_split(gradients[3] + inner_error), inner_start.reshape(N_MP, inner_slice, RANK))
    inner_approx = jnp.transpose(inner_approx, (1, 0, 2)).reshape(D, FF)
    inner_new, inner_moment_new = renew(inner_weight, inner_moment, inner_approx, step_rate)
    outer_left, outer_right, outer_approx, outer_residue = jax.vmap(compress)(rows_split(gradients[4] + outer_error), outer_start)
    outer_new, outer_moment_new = renew(outer_weight, outer_moment, outer_approx.reshape(FF, D), step_rate)
    means = [lax.optimization_barrier(jnp.sum(gradients[position], axis=0)) / N_DP for position in range(5, 10)]
    embed_bias_new, embed_bias_moment_new = renew(embed_bias, embed_bias_moment, means[0], step_rate)
    query_bias_new, query_bias_moment_new = renew(query_bias, query_bias_moment, means[1], step_rate)
    inner_bias_new, inner_bias_moment_new = renew(inner_bias, inner_bias_moment, means[2], step_rate)
    norm_gains_new, gains_moment_new = renew(norm_gains, gains_moment, means[3], step_rate)
    shared_biases_new, biases_moment_new = renew(shared_biases, biases_moment, means[4], step_rate)
    return (output, series_grad, embed_new, embed_moment_new, embed_residue.reshape(N_DP, GROUPS, LMAX, D), embed_left.reshape(GROUPS, LMAX, RANK), embed_right, attend_new, attend_moment_new, attend_residue, attend_left, attend_right, mixer_new, mixer_moment_new, rows_join(mixer_residue), mixer_left.reshape(D, RANK), mixer_right, inner_new, inner_moment_new, cols_join(inner_residue), inner_left, inner_right.reshape(FF, RANK), outer_new, outer_moment_new, rows_join(outer_residue), outer_left.reshape(FF, RANK), outer_right, embed_bias_moment_new, embed_bias_new, query_bias_moment_new, query_bias_new, inner_bias_moment_new, inner_bias_new, gains_moment_new, norm_gains_new, biases_moment_new, shared_biases_new)
```

```python
import functools
import math

import jax
import jax.numpy as jnp
from jax import lax
from jax.experimental import pallas as pl
from jax.experimental.pallas import tpu as pltpu
from jax.sharding import PartitionSpec as P

HEADS = 8
momentum_decay = 0.9
norm_epsilon = 1e-05
base_rate = 0.03
inverse_root_two = 0.7071067811865476
inverse_root_tau = 0.3989422804014327
log2_e = 1.4426950408889634
ln_two = 0.6931471805599453
f32 = jnp.float32
bf16 = jnp.bfloat16
VMEM = pltpu.VMEM
VM = pl.BlockSpec(memory_space=pltpu.VMEM)
SM = pl.BlockSpec(memory_space=pltpu.SMEM)
MIB = 1024 * 1024


def dot_nn(a, b):
    return lax.dot_general(a, b, (((1,), (0,)), ((), ())), preferred_element_type=f32)


def dot_nt(a, b):
    return lax.dot_general(a, b, (((1,), (1,)), ((), ())), preferred_element_type=f32)


def dot_tn(a, b):
    return lax.dot_general(a, b, (((0,), (0,)), ((), ())), preferred_element_type=f32)


def split_two(x):
    high = x.astype(bf16)
    return high, (x - high.astype(f32)).astype(bf16)


def three_way(x, lane):
    high = x.astype(bf16).astype(f32)
    rest = x - high
    middle = rest.astype(bf16).astype(f32)
    last = rest - middle
    place = lax.rem(lane, 3)
    return jnp.where(place == 0, high, jnp.where(place == 1, middle, last)).astype(bf16)


def row_number(rows, position):
    half = rows // 2
    index = lax.broadcasted_iota(jnp.int32, (rows, 128), 0)
    return jnp.where(index < half, index + position * half, index - half + (1 - position) * half)


def attend_forward(
    scalars, series_own, series_other, table, embed_bias, own, other, query_bias,
    hidden_ref, token_ref, query_ref, key_ref, value_ref, context_ref, lse_ref,
):
    rows, width = hidden_ref.shape
    half = rows // 2
    part = own.shape[2]
    head_dim = width // HEADS
    for index, block in enumerate((series_own, series_other)):
        values = dot_nn(block[...], table[...]) + embed_bias[...]
        hidden_ref[pl.ds(index * half, half), :] = values
        token_ref[pl.ds(index * half, half), :] = values.astype(bf16)
    scale = head_dim**-0.5 * log2_e
    tokens = token_ref[...]
    for index, block in enumerate((own, other)):
        columns = pl.ds(index * part, part)
        query_ref[:, columns] = (
            (dot_nn(tokens, block[0]) + query_bias[0:1, columns]) * scale
        ).astype(bf16)
        key_ref[:, columns] = dot_nn(tokens, block[1]).astype(bf16)
        value_ref[:, columns] = (dot_nn(tokens, block[2]) + query_bias[1:2, columns]).astype(bf16)
    lane = lax.broadcasted_iota(jnp.int32, (rows, 128), 1)
    dead = row_number(rows, scalars[0]) >= scalars[1]
    extra_query = jnp.where(lane == 0, 1.0, 0.0).astype(bf16)
    extra_key = jnp.where((lane == 0) & dead, -1e30, 0.0).astype(bf16)
    ones = jnp.ones((rows, 128), bf16)
    lse_ref[...] = jnp.zeros_like(lse_ref)

    def pair(index, carry):
        columns = pl.ds(pl.multiple_of(index * 128, 128), 128)
        queries = query_ref[:, columns]
        keys = jnp.concatenate([key_ref[:, columns], extra_key], axis=1)
        values = jnp.concatenate([value_ref[:, columns], ones], axis=1)
        found = []
        for side in range(2):
            mine = (lane >= head_dim) if side else (lane < head_dim)
            query = jnp.concatenate(
                [jnp.where(mine, queries, jnp.zeros_like(queries)), extra_query], axis=1
            )
            scores = dot_nt(query, keys)
            peak = jnp.max(scores, axis=1, keepdims=True)
            soft = jnp.exp2(scores - peak).astype(bf16)
            mixed = dot_nn(soft, values)
            total = mixed[:, 128:]
            found.append(mixed[:, :128] / total)
            log_total = jnp.broadcast_to(peak, (rows, 128)) + jnp.log2(total)
            lse_ref[...] = jnp.where(lane // 3 == index * 2 + side, log_total, lse_ref[...])
        context_ref[:, columns] = jnp.where(lane < head_dim, found[0], found[1]).astype(bf16)
        return carry

    lax.fori_loop(0, width // 128, pair, 0)


def norm_rows(values, gain, shift):
    centered = values - jnp.mean(values, axis=-1, keepdims=True)
    inverse = lax.rsqrt(jnp.mean(centered * centered, axis=-1, keepdims=True) + norm_epsilon)
    unit = centered * inverse
    return unit * gain + shift, unit, inverse


def norm_rows_back(upstream, unit, inverse, gain):
    scaled = upstream * gain
    return inverse * (
        scaled
        - jnp.mean(scaled, axis=-1, keepdims=True)
        - unit * jnp.mean(scaled * unit, axis=-1, keepdims=True)
    )


def feed_forward(
    scalars, context_ref, hidden_ref, mixer_own, mixer_other, inner_own, inner_other,
    outer_own, outer_other, inner_bias, gains, biases, cot_own, cot_other,
    output_ref, active_ref, preact_ref, normed_ref, feed_ref, attend_ref, resid_ref,
    context_grad_ref, delta_ref, sums_ref, inner_sum_ref, slope_ref,
):
    tile, width = hidden_ref.shape
    step = pl.program_id(0)
    steps = pl.num_programs(0)
    part = mixer_own.shape[0]
    inner_part = inner_own.shape[1]
    rows = tile * steps
    half = rows // 2
    chunk = 512
    context = context_ref[...]
    attended = dot_nn(context[:, :part], mixer_own[...]) + dot_nn(
        context[:, part:], mixer_other[...]
    )
    normed, unit_one, inverse_one = norm_rows(
        hidden_ref[...] + attended + biases[2:3, :], gains[0:1, :], biases[0:1, :]
    )
    normed_low = normed.astype(bf16)
    normed_ref[...] = normed_low
    for index, block in enumerate((inner_own, inner_other)):
        for start in range(0, inner_part, chunk):
            columns = pl.ds(index * inner_part + start, chunk)
            preact = dot_nn(normed_low, block[:, pl.ds(start, chunk)]) + inner_bias[0:1, columns]
            phi = 0.5 + 0.5 * lax.erf(preact * inverse_root_two)
            active_ref[:, columns] = (preact * phi).astype(bf16)
            slope_ref[:, columns] = (
                phi + preact * jnp.exp2(preact * preact * (-0.5 * log2_e)) * inverse_root_tau
            ).astype(bf16)
    feed_out = dot_nn(active_ref[:, :inner_part], outer_own[...]) + dot_nn(
        active_ref[:, inner_part:], outer_other[...]
    )
    output, unit_two, inverse_two = norm_rows(
        normed + feed_out + biases[3:4, :], gains[1:2, :], biases[1:2, :]
    )
    output_ref[...] = output
    index = lax.broadcasted_iota(jnp.int32, (tile, width), 0) + step * tile
    position = scalars[0]
    number = jnp.where(index < half, index + position * half, index - half + (1 - position) * half)
    cot = jnp.where(step < steps // 2, cot_own[...], cot_other[...]).astype(f32)
    upstream = jnp.where(number < scalars[1], cot, 0.0)
    resid_two = norm_rows_back(upstream, unit_two, inverse_two, gains[1:2, :])
    feed_grad = resid_two.astype(bf16)
    feed_ref[...] = feed_grad
    for index, block in enumerate((outer_own, outer_other)):
        for start in range(0, inner_part, chunk):
            columns = pl.ds(index * inner_part + start, chunk)
            grad = dot_nt(feed_grad, block[pl.ds(start, chunk), :])
            preact_ref[:, columns] = (grad * slope_ref[:, columns].astype(f32)).astype(bf16)
    normed_grad = (
        resid_two
        + dot_nt(preact_ref[:, :inner_part], inner_own[...])
        + dot_nt(preact_ref[:, inner_part:], inner_other[...])
    )
    resid_one = norm_rows_back(normed_grad, unit_one, inverse_one, gains[0:1, :])
    resid_ref[...] = resid_one
    attend_grad = resid_one.astype(bf16)
    attend_ref[...] = attend_grad
    context_grad = jnp.concatenate(
        [dot_nt(attend_grad, mixer_own[...]), dot_nt(attend_grad, mixer_other[...])], axis=1
    ).astype(bf16)
    context_grad_ref[...] = context_grad
    high, low = split_two(context_grad.astype(f32) * context.astype(f32))
    head_dim = width // HEADS
    head = lax.broadcasted_iota(jnp.int32, (width, 128), 0) // head_dim
    lane = lax.broadcasted_iota(jnp.int32, (width, 128), 1)
    chooser = jnp.where(lane // 3 == head, -1.0, 0.0).astype(bf16)
    delta = dot_nn(high, chooser) + dot_nn(low, chooser)
    delta_ref[...] = three_way(delta, lax.broadcasted_iota(jnp.int32, (tile, 128), 1))

    @pl.when(step == 0)
    def _():
        sums_ref[...] = jnp.zeros_like(sums_ref)
        inner_sum_ref[...] = jnp.zeros_like(inner_sum_ref)

    def add(row, values):
        sums_ref[row : row + 1, :] += jnp.sum(values, axis=0, keepdims=True)

    add(1, normed_grad * unit_one)
    add(2, upstream * unit_two)
    add(3, normed_grad)
    add(4, upstream)
    add(5, resid_one)
    add(6, resid_two)
    inner_sum_ref[0:1, :] += jnp.sum(preact_ref[...].astype(f32), axis=0, keepdims=True)


def attend_backward(
    scalars, query_ref, key_ref, value_ref, lse_ref, context_grad_ref, delta_ref,
    dquery_ref, dkey_ref, dvalue_ref,
):
    rows, width = query_ref.shape
    head_dim = width // HEADS
    lane = lax.broadcasted_iota(jnp.int32, (rows, 128), 1)
    dead = row_number(rows, scalars[0]) >= scalars[1]
    extra_query = jnp.where(lane == 127, jnp.ones((rows, 128), bf16), three_way(-lse_ref[...], lane))
    extra_key = jnp.where((lane == 127) & dead, -1e30, 0.0)
    extra_grad = delta_ref[...]

    def pair(index, carry):
        columns = pl.ds(pl.multiple_of(index * 128, 128), 128)
        queries = query_ref[:, columns]
        keys = key_ref[:, columns]
        values = value_ref[:, columns]
        grads = context_grad_ref[:, columns]
        dquery = dkey = dvalue = None
        for side in range(2):
            mine = (lane >= head_dim) if side else (lane < head_dim)
            hot = lane // 3 == index * 2 + side
            nothing = jnp.zeros_like(queries)
            query = jnp.where(mine, queries, nothing)
            grad = jnp.where(mine, grads, nothing)
            key = jnp.where(mine, keys, nothing)
            soft = jnp.exp2(
                dot_nt(
                    jnp.concatenate([keys, jnp.where(hot, 1.0, extra_key).astype(bf16)], axis=1),
                    jnp.concatenate([query, extra_query], axis=1),
                )
            )
            centered = dot_nt(
                jnp.concatenate([values, jnp.where(hot, 1.0, 0.0).astype(bf16)], axis=1),
                jnp.concatenate([grad, extra_grad], axis=1),
            )
            score_grad = (soft * centered).astype(bf16)
            one = dot_nn(soft.astype(bf16), grad)
            two = dot_nn(score_grad, query)
            three = dot_tn(key, score_grad)
            dvalue = one if dvalue is None else dvalue + one
            dkey = two if dkey is None else dkey + two
            dquery = three if dquery is None else dquery + three
        dvalue_ref[:, columns] = dvalue.astype(bf16)
        dkey_ref[:, columns] = (dkey * ln_two).astype(bf16)
        dquery_ref[:, columns] = (dquery.T * head_dim**-0.5).astype(bf16)
        return carry

    lax.fori_loop(0, width // 128, pair, 0)


def input_backward(
    dquery_ref, dkey_ref, dvalue_ref, token_ref, resid_ref, own, other, table,
    series_own, series_other, sums_ref,
    attend_own, attend_other, series_grad_ref, table_grad_ref, sums_out, query_sum_ref,
):
    rows, width = token_ref.shape
    half = rows // 2
    part = own.shape[2]
    tokens = token_ref[...]
    total = resid_ref[...]
    for kind, grad_ref in enumerate((dquery_ref, dkey_ref, dvalue_ref)):
        low = grad_ref[...]
        attend_own[kind] = dot_tn(tokens, low[:, :part])
        attend_other[kind] = dot_tn(tokens, low[:, part:]).astype(bf16)
        total = total + dot_nt(low[:, :part], own[kind]) + dot_nt(low[:, part:], other[kind])
        if kind != 1:
            row = kind // 2
            query_sum_ref[row : row + 1, :] = jnp.sum(low.astype(f32), axis=0, keepdims=True)
    low = total.astype(bf16)
    series_grad_ref[...] = dot_nt(low, table[...])
    table_grad_ref[...] = (
        dot_tn(series_own[...], low[:half]) + dot_tn(series_other[...], low[half:])
    ).astype(bf16)
    sums_out[...] = sums_ref[...]
    sums_out[0:1, :] = jnp.sum(low.astype(f32), axis=0, keepdims=True)


def left_factors(embed, outer, attend, inner, mixer, s_embed, s_outer, s_attend, s_inner, s_mixer, out):
    def product(start, matrix):
        start_high, start_low = split_two(start)
        high, low = split_two(matrix)
        four = jnp.concatenate([start_high, start_low], axis=0)
        both = dot_nt(four, high)
        return both[:8] + both[8:] + dot_nt(start_high, low)

    out[:, 0:1024] = jnp.concatenate(
        [product(s_embed[...], embed[...]), jnp.zeros((8, 1024 - embed.shape[0]), f32)], axis=1
    )
    out[:, 1024:2048] = product(s_outer[...], outer[...])
    out[:, 2048:2560] = (
        product(s_attend[0], attend[0])
        + product(s_attend[1], attend[1])
        + product(s_attend[2], attend[2])
    )
    out[:, 2560:3072] = product(s_inner[...], inner[...])
    out[:, 3072:3328] = product(s_mixer[...], mixer[...])


def orthonormal_rows(vectors):
    rank = vectors.shape[0]
    row = lax.broadcasted_iota(jnp.int32, vectors.shape, 0)
    for index in range(rank):
        pivot = vectors[index : index + 1, :]
        inner = jnp.sum(vectors * pivot, axis=1, keepdims=True)
        size = inner[index : index + 1, :] + 1e-12
        reduced = vectors - pivot * (inner / size)
        vectors = jnp.where(
            row > index, reduced, jnp.where(row == index, vectors * lax.rsqrt(size), vectors)
        )
    return vectors


def right_factors(replicas, summed, embed, outer, attend, inner, mixer, left_ref, out):
    def product(basis, matrix):
        basis_high, basis_low = split_two(basis)
        high, low = split_two(matrix)
        both = dot_nn(jnp.concatenate([basis_high, basis_low], axis=0), high)
        return both[:8] + both[8:] + dot_nn(basis_high, low)

    share = 1.0 / replicas
    bases = []
    for start, size in ((0, 1024), (1024, 1024), (2048, 512), (2560, 512), (3072, 256)):
        basis = orthonormal_rows(summed[:, start : start + size] * share)
        left_ref[:, start : start + size] = basis
        bases.append(basis)
    out[:, 0:512] = product(bases[0][:, : embed.shape[0]], embed[...])
    out[:, 512:1024] = product(bases[1], outer[...])
    out[:, 1024:1280] = product(bases[2], attend[0])
    out[:, 1280:1536] = product(bases[2], attend[1])
    out[:, 1536:1792] = product(bases[2], attend[2])
    out[:, 1792:2816] = product(bases[3], inner[...])
    out[:, 2816:3328] = product(bases[4], mixer[...])
    out[:, 3328:] = jnp.zeros((8, out.shape[1] - 3328), f32)


def sum_replicas(replicas, in_ref, out_ref, parts, send_one, recv_one, send_two, recv_two):
    me = lax.axis_index("dp")
    barrier = pltpu.get_barrier_semaphore()
    chunk = in_ref.shape[1] // replicas

    def peer(offset):
        return lax.rem(me + offset, replicas)

    def columns(index):
        return pl.ds(pl.multiple_of(index * chunk, 128), chunk)

    def greet(offset, carry):
        pl.semaphore_signal(
            barrier, inc=1, device_id={"dp": peer(offset)}, device_id_type=pl.DeviceIdType.MESH
        )
        return carry

    lax.fori_loop(1, replicas, greet, 0)
    pl.semaphore_wait(barrier, replicas - 1)

    def scatter(offset):
        other = peer(offset)
        return pltpu.make_async_remote_copy(
            src_ref=in_ref.at[:, columns(other)],
            dst_ref=parts.at[offset],
            send_sem=send_one.at[offset],
            recv_sem=recv_one.at[offset],
            device_id={"dp": other},
            device_id_type=pl.DeviceIdType.MESH,
        )

    def spread(offset):
        return pltpu.make_async_remote_copy(
            src_ref=out_ref.at[:, columns(me)],
            dst_ref=out_ref.at[:, columns(me)],
            send_sem=send_two.at[offset],
            recv_sem=recv_two.at[offset],
            device_id={"dp": peer(offset)},
            device_id_type=pl.DeviceIdType.MESH,
        )

    def gathered(offset):
        source = lax.rem(me - offset + replicas, replicas)
        return pltpu.make_async_remote_copy(
            src_ref=out_ref.at[:, columns(source)],
            dst_ref=out_ref.at[:, columns(source)],
            send_sem=send_two.at[offset],
            recv_sem=recv_two.at[offset],
            device_id={"dp": peer(offset)},
            device_id_type=pl.DeviceIdType.MESH,
        )

    def each(what):
        def body(offset, carry):
            what(offset)
            return carry

        lax.fori_loop(1, replicas, body, 0)

    each(lambda offset: scatter(offset).start())
    total = in_ref[:, columns(me)]

    def collect(offset, total):
        scatter(offset).wait_recv()
        return total + parts[offset]

    out_ref[:, columns(me)] = lax.fori_loop(1, replicas, collect, total)
    each(lambda offset: spread(offset).start())
    each(lambda offset: gathered(offset).wait_recv())
    each(lambda offset: scatter(offset).wait_send())
    each(lambda offset: spread(offset).wait_send())


def all_sum(values, replicas, collective_id):
    width = values.shape[1]
    chunk = width // replicas
    padded = max(128, -(-chunk // 128) * 128)
    full = padded * replicas
    if full != width:
        values = jnp.pad(values, ((0, 0), (0, full - width)))
    out = pl.pallas_call(
        functools.partial(sum_replicas, replicas),
        out_shape=jax.ShapeDtypeStruct((8, full), f32),
        in_specs=[VM],
        out_specs=VM,
        scratch_shapes=[
            pltpu.VMEM((replicas, 8, padded), f32),
            pltpu.SemaphoreType.DMA((replicas,)),
            pltpu.SemaphoreType.DMA((replicas,)),
            pltpu.SemaphoreType.DMA((replicas,)),
            pltpu.SemaphoreType.DMA((replicas,)),
        ],
        compiler_params=pltpu.CompilerParams(
            collective_id=collective_id, has_side_effects=True, vmem_limit_bytes=8 * MIB
        ),
        name=f"sum_replicas_{collective_id}",
    )(values)
    return out[:, :width]


def call(kernel, outs, args, *, grid=None, in_specs=None, out_specs=None, scratch=(), limit=56, name=None, aliases=None):
    kwargs = {}
    if grid is not None:
        kwargs["grid"] = grid
    return pl.pallas_call(
        kernel,
        out_shape=outs,
        in_specs=in_specs if in_specs is not None else [VM] * len(args),
        out_specs=out_specs if out_specs is not None else jax.tree.map(lambda _: VM, outs),
        scratch_shapes=list(scratch),
        compiler_params=pltpu.CompilerParams(vmem_limit_bytes=limit * MIB),
        name=name,
        **kwargs,
    )(*args)


def sds(shape, dtype=f32):
    return jax.ShapeDtypeStruct(shape, dtype)


def renew_all(step_rate, mixer_rate, args):
    def kernel(
        left, r_embed, r_outer, r_attend, r_inner, r_mixer, *refs
    ):
        matrices, weights, moments = refs[0:5], refs[5:10], refs[10:15]
        errors, new_weights, new_moments = refs[15:20], refs[20:25], refs[25:30]
        step = pl.program_id(0)

        def approx(basis, right):
            left_high, left_low = split_two(basis)
            right_high, right_low = split_two(right)
            return dot_tn(
                jnp.concatenate([left_high, left_low, left_high, left_low], axis=0),
                jnp.concatenate([right_high, right_high, right_low, right_low], axis=0),
            )

        def write(index, where, update, rate):
            errors[index][where] = matrices[index][where] - update
            moment = momentum_decay * moments[index][where] + update
            new_moments[index][where] = moment
            new_weights[index][where] = weights[index][where] - rate * moment

        every = (slice(None), slice(None))
        size = matrices[0].shape[0]
        write(0, every, approx(left[:, 0:size], r_embed[...]), step_rate)
        block = matrices[1].shape[0]
        write(
            1, every,
            approx(left[:, pl.ds(pl.multiple_of(1024 + step * block, 128), block)], r_outer[...]),
            step_rate,
        )
        block = matrices[2].shape[1]
        basis = left[:, pl.ds(pl.multiple_of(2048 + step * block, 128), block)]
        for kind in range(3):
            write(
                2, (kind, slice(None), slice(None)),
                approx(basis, r_attend[:, kind * 256 : (kind + 1) * 256]), step_rate,
            )
        block = matrices[3].shape[0]
        write(
            3, every,
            approx(left[:, pl.ds(pl.multiple_of(2560 + step * block, 128), block)], r_inner[...]),
            step_rate,
        )
        write(4, every, approx(left[:, 3072:3328], r_mixer[...]), mixer_rate)

    steps = 4
    left, right, matrices, weights, moments = args
    full = pl.BlockSpec((8, left.shape[1]), lambda i: (0, 0))
    column = lambda a: pl.BlockSpec((a.shape[0], a.shape[1] // steps), lambda i: (0, i))
    row = lambda a: pl.BlockSpec((a.shape[0] // steps, a.shape[1]), lambda i: (i, 0))
    middle = lambda a: pl.BlockSpec((a.shape[0], a.shape[1] // steps, a.shape[2]), lambda i: (0, i, 0))
    r_embed, r_outer, r_attend, r_inner, r_mixer = (
        right[:, 0:512], right[:, 512:1024], right[:, 1024:1792], right[:, 1792:2816], right[:, 2816:3328],
    )
    whole = lambda a: pl.BlockSpec(a.shape, lambda i: (0, 0))
    specs = [column(matrices[0]), row(matrices[1]), middle(matrices[2]), row(matrices[3]), column(matrices[4])]
    outs = [sds(a.shape) for a in matrices] * 3
    found = call(
        kernel, outs,
        (left, r_embed, r_outer, r_attend, r_inner, r_mixer, *matrices, *weights, *moments),
        grid=(steps,),
        in_specs=[full, column(r_embed), whole(r_outer), whole(r_attend), whole(r_inner), column(r_mixer)] + specs * 3,
        out_specs=specs * 3,
        name="renew_all",
    )
    return found[0:5], found[5:10], found[10:15]


def renew(weight, moment, update, step_rate):
    new_moment = momentum_decay * moment + update
    return (weight - step_rate * new_moment, new_moment)


def local(
    series, groups, counts, cotangent,
    embed_weight, embed_moment, embed_error, embed_start,
    attend_weight, attend_moment, attend_error, attend_start,
    mixer_weight, mixer_moment, mixer_error, mixer_start,
    inner_weight, inner_moment, inner_error, inner_start,
    outer_weight, outer_moment, outer_error, outer_start,
    embed_bias, embed_bias_moment, query_bias, query_bias_moment,
    inner_bias, inner_bias_moment, norm_gains, gains_moment, shared_biases, biases_moment,
):
    replicas = lax.axis_size("dp")
    position = lax.axis_index("mp")
    half, windows, history = series.shape
    rows = 2 * half
    group_count, _, width = embed_weight.shape
    part = attend_weight.shape[2]
    inner_part = inner_weight.shape[1]

    def swap(values):
        return lax.ppermute(values, "mp", [(0, 1), (1, 0)])

    def mine(values, axis):
        return lax.dynamic_index_in_dim(values, position, axis, keepdims=False)

    def theirs(values, axis):
        return lax.dynamic_index_in_dim(values, 1 - position, axis, keepdims=False)

    series_other = swap(theirs(series, 1))
    attend_own = attend_weight.transpose(1, 0, 2).astype(bf16)
    attend_other = swap(attend_own)
    small = jnp.concatenate([query_bias, inner_bias.reshape(inner_part // part, part)], axis=0)
    small_other = swap(small)
    mixer_own = mixer_weight.astype(bf16)
    mixer_other = swap(mixer_own)
    inner_own = inner_weight.astype(bf16)
    inner_other = swap(inner_own)
    outer_own = outer_weight.astype(bf16)
    outer_other = swap(outer_own)
    cot_other = swap(theirs(cotangent, 1))
    series_own = mine(series, 1)
    cot_own = mine(cotangent, 1)

    group = mine(groups, 0)
    count = mine(counts, 0)
    lookback = jnp.where(
        group == 0, history * 2 // 7, jnp.where(group == 1, history * 4 // 7, history)
    ).astype(jnp.int32)
    in_window = (jnp.arange(history, dtype=jnp.int32) >= history - lookback)[:, None]
    table = jnp.where(
        in_window, lax.dynamic_index_in_dim(embed_weight, group, 0, keepdims=False), 0.0
    ).astype(bf16)
    bias_row = lax.dynamic_slice_in_dim(embed_bias, group, 1, 0)
    query_bias_full = jnp.concatenate([query_bias, small_other[:2]], axis=1)
    inner_bias_full = jnp.concatenate([inner_bias, small_other[2:].reshape(inner_part)])[None]
    scalars = jnp.stack([position.astype(jnp.int32), count])

    low = sds((rows, width), bf16)
    full = sds((rows, width))
    hidden, tokens, queries, keys, values, context, lse = call(
        attend_forward,
        [full, low, low, low, low, low, sds((rows, 128))],
        (scalars, series_own, series_other, table, bias_row, attend_own, attend_other, query_bias_full),
        in_specs=[SM] + [VM] * 7,
        name="attend_forward",
    )
    steps = 4
    tile = rows // steps
    rowed = lambda n: pl.BlockSpec((tile, n), lambda i: (i, 0))
    whole = lambda a: pl.BlockSpec(a.shape, lambda i: (0, 0))
    first = pl.BlockSpec((tile, width), lambda i: (jnp.minimum(i, steps // 2 - 1), 0))
    second = pl.BlockSpec((tile, width), lambda i: (jnp.maximum(i - steps // 2, 0), 0))
    hidden_units = 2 * inner_part
    output, active, preact_grad, normed_low, feed_grad, attend_out, resid_one, context_grad, delta, sums, inner_sums = call(
        feed_forward,
        [
            full, sds((rows, hidden_units), bf16), sds((rows, hidden_units), bf16), low, low, low,
            full, low, sds((rows, 128), bf16), sds((8, width)), sds((8, hidden_units)),
        ],
        (scalars, context, hidden, mixer_own, mixer_other, inner_own, inner_other, outer_own,
         outer_other, inner_bias_full, norm_gains, shared_biases, cot_own, cot_other),
        grid=(steps,),
        in_specs=[SM, rowed(width), rowed(width), whole(mixer_own), whole(mixer_own), whole(inner_own),
                  whole(inner_own), whole(outer_own), whole(outer_own), whole(inner_bias_full),
                  whole(norm_gains), whole(shared_biases), first, second],
        out_specs=[rowed(width), rowed(hidden_units), rowed(hidden_units), rowed(width), rowed(width),
                   rowed(width), rowed(width), rowed(width), rowed(128),
                   pl.BlockSpec((8, width), lambda i: (0, 0)),
                   pl.BlockSpec((8, hidden_units), lambda i: (0, 0))],
        scratch=[pltpu.VMEM((tile, hidden_units), bf16)],
        name="feed_forward",
    )
    output_other = swap(output[half:])
    outer_far = swap(dot_tn(active[:, inner_part:], feed_grad).astype(bf16))
    inner_far = swap(dot_tn(normed_low, preact_grad[:, inner_part:]).astype(bf16))
    mixer_far = swap(dot_tn(context[:, part:], attend_out).astype(bf16))
    dquery, dkey, dvalue = call(
        attend_backward,
        [low, low, low],
        (scalars, queries, keys, values, lse, context_grad, delta),
        in_specs=[SM] + [VM] * 6,
        name="attend_backward",
    )
    attend_near, attend_far, series_grad, table_grad, sums, query_sums = call(
        input_backward,
        [
            sds((3, width, part)), sds((3, width, part), bf16), sds((rows, history)),
            sds((history, width), bf16), sds((8, width)), sds((2, width)),
        ],
        (dquery, dkey, dvalue, tokens, resid_one, attend_own, attend_other, table, series_own,
         series_other, sums),
        name="input_backward",
    )
    attend_far = swap(attend_far)
    table_far = swap(table_grad)
    series_grad_other = swap(series_grad[half:])
    small_far = swap(
        jnp.concatenate(
            [sums[:7], query_sums[:, part:].reshape(1, width), inner_sums[0, inner_part:].reshape(-1, width)],
            axis=0,
        )
    )
    far_group = theirs(groups, 0)

    outer_matrix = dot_tn(active[:, :inner_part], feed_grad) + outer_far.astype(f32) + outer_error[0]
    inner_matrix = dot_tn(normed_low, preact_grad[:, :inner_part]) + inner_far.astype(f32) + inner_error[0]
    mixer_matrix = dot_tn(context[:, :part], attend_out) + mixer_far.astype(f32) + mixer_error[0]
    attend_matrix = attend_near + attend_far.astype(f32) + attend_error[0].transpose(1, 0, 2)
    group_ids = jnp.arange(group_count, dtype=jnp.int32)[:, None, None]
    embed_grad = jnp.where(group_ids == group, table_grad.astype(f32)[None], 0.0) + jnp.where(
        group_ids == far_group, table_far.astype(f32)[None], 0.0
    )
    lookbacks = jnp.where(
        group_ids == 0, history * 2 // 7, jnp.where(group_ids == 1, history * 4 // 7, history)
    )
    seen = jnp.arange(history, dtype=jnp.int32)[None, :, None] >= history - lookbacks
    embed_matrix = (jnp.where(seen, embed_grad, 0.0) + embed_error[0]).reshape(
        group_count * history, width
    )
    common = sums[:7] + small_far[:7]
    ids = jnp.arange(group_count, dtype=jnp.int32)[:, None]
    embed_bias_grad = jnp.where(ids == group, sums[0:1], 0.0) + jnp.where(
        ids == far_group, small_far[0:1], 0.0
    )
    query_bias_grad = query_sums[:, :part] + small_far[7].reshape(2, part)
    inner_bias_grad = inner_sums[0, :inner_part] + small_far[8:].reshape(inner_part)
    vectors = jnp.concatenate(
        [
            embed_bias_grad.reshape(-1), common[1:7].reshape(-1), query_bias_grad.reshape(-1), inner_bias_grad,
        ]
    ).reshape(8, -1)

    matrices = (embed_matrix, outer_matrix, attend_matrix, inner_matrix, mixer_matrix)
    starts = (
        embed_start.T, outer_start[0].T, attend_start.transpose(0, 2, 1), inner_start.T, mixer_start[0].T,
    )
    left_part = call(left_factors, sds((8, 3328)), (*matrices, *starts), name="left_factors")
    summed = all_sum(jnp.concatenate([left_part, vectors], axis=1), replicas, 1)
    left, right_part = call(
        functools.partial(right_factors, replicas),
        [sds((8, 3328)), sds((8, 4096))],
        (summed, *matrices),
        name="right_factors",
    )
    right = all_sum(right_part, replicas, 2)[:, :3328] / replicas

    step_rate = base_rate * math.sqrt(replicas * 7 / (windows * rows))
    mixer_rate = step_rate * math.sqrt(width / max(width * 16 // rows, 1))
    embed_flat = (group_count * history, width)
    errors, weights, moments = renew_all(
        step_rate, mixer_rate,
        (
            left, right, matrices,
            (embed_weight.reshape(embed_flat), outer_weight, attend_weight.transpose(1, 0, 2), inner_weight, mixer_weight),
            (embed_moment.reshape(embed_flat), outer_moment, attend_moment.transpose(1, 0, 2), inner_moment, mixer_moment),
        ),
    )
    means = (summed[:, 3328:] / replicas).reshape(-1)
    cut = []
    place = 0
    for like in (embed_bias, norm_gains, shared_biases, query_bias, inner_bias):
        cut.append(means[place : place + like.size].reshape(like.shape))
        place += like.size
    embed_bias_new, embed_bias_moment_new = renew(embed_bias, embed_bias_moment, cut[0], step_rate)
    norm_gains_new, gains_moment_new = renew(norm_gains, gains_moment, cut[1], step_rate)
    shared_biases_new, biases_moment_new = renew(shared_biases, biases_moment, cut[2], step_rate)
    query_bias_new, query_bias_moment_new = renew(query_bias, query_bias_moment, cut[3], step_rate)
    inner_bias_new, inner_bias_moment_new = renew(inner_bias, inner_bias_moment, cut[4], step_rate)

    def both(own, other):
        return jnp.where(
            position == 0, jnp.stack([own, other], axis=1), jnp.stack([other, own], axis=1)
        )

    turned = lambda a: a.transpose(1, 0, 2)
    return (
        both(output[:half], output_other),
        both(series_grad[:half], series_grad_other),
        weights[0].reshape(embed_weight.shape),
        moments[0].reshape(embed_weight.shape),
        errors[0].reshape(embed_error.shape),
        left[:, : group_count * history].reshape(8, group_count, history).transpose(1, 2, 0),
        right[:, 0:512].T,
        turned(weights[2]),
        turned(moments[2]),
        turned(errors[2])[None],
        left[:, 2048:2560].T[None],
        right[:, 1024:1792].reshape(8, 3, part).transpose(1, 2, 0),
        weights[4],
        moments[4],
        errors[4][None],
        left[:, 3072:3328].T,
        right[:, 2816:3328].T[None],
        weights[3],
        moments[3],
        errors[3][None],
        left[:, 2560:3072].T[None],
        right[:, 1792:2816].T,
        weights[1],
        moments[1],
        errors[1][None],
        left[:, 1024:2048].T,
        right[:, 512:1024].T[None],
        embed_bias_moment_new,
        embed_bias_new,
        query_bias_moment_new,
        query_bias_new,
        inner_bias_moment_new,
        inner_bias_new,
        gains_moment_new,
        norm_gains_new,
        biases_moment_new,
        shared_biases_new,
    )


def solution(mesh):
    return jax.shard_map(
        local,
        mesh=mesh,
        in_specs=(
            P("mp", "dp", None),
            P("dp"),
            P("dp"),
            P("mp", "dp", None),
            P(),
            P(),
            P("dp", None, None, None),
            P(),
            P(None, None, "mp"),
            P(None, None, "mp"),
            P("dp", None, None, "mp"),
            P(None, "mp", None),
            P("mp", None),
            P("mp", None),
            P("dp", "mp", None),
            P("mp", None, None),
            P(None, "mp"),
            P(None, "mp"),
            P("dp", None, "mp"),
            P("mp", None),
            P("mp", None),
            P("mp", None),
            P("dp", "mp", None),
            P("mp", None, None),
            P(),
            P(),
            P(None, "mp"),
            P(None, "mp"),
            P("mp"),
            P("mp"),
            P(),
            P(),
            P(),
            P(),
        ),
        out_specs=(
            P("mp", "dp", None),
            P("mp", "dp", None),
            P(),
            P(),
            P("dp", None, None, None),
            P(),
            P(),
            P(None, None, "mp"),
            P(None, None, "mp"),
            P("dp", None, None, "mp"),
            P("mp", None, None),
            P(None, "mp", None),
            P("mp", None),
            P("mp", None),
            P("dp", "mp", None),
            P("mp", None),
            P("mp", None, None),
            P(None, "mp"),
            P(None, "mp"),
            P("dp", None, "mp"),
            P("mp", None, None),
            P("mp", None),
            P("mp", None),
            P("mp", None),
            P("dp", "mp", None),
            P("mp", None),
            P("mp", None, None),
            P(),
            P(),
            P(None, "mp"),
            P(None, "mp"),
            P("mp"),
            P("mp"),
            P(),
            P(),
            P(),
            P(),
        ),
        check_vma=False,
    )
```

```python
import functools
import math

import jax
import jax.numpy as jnp
from jax import lax
from jax.experimental import pallas as pl
from jax.experimental.pallas import tpu as pltpu
from jax.sharding import PartitionSpec as P

HEADS = 8
momentum_decay = 0.9
norm_epsilon = 1e-05
base_rate = 0.03
inverse_root_two = 0.7071067811865476
inverse_root_tau = 0.3989422804014327
log2_e = 1.4426950408889634
ln_two = 0.6931471805599453
f32 = jnp.float32
bf16 = jnp.bfloat16
VMEM = pltpu.VMEM
VM = pl.BlockSpec(memory_space=pltpu.VMEM)
SM = pl.BlockSpec(memory_space=pltpu.SMEM)
MIB = 1024 * 1024


def dot_nn(a, b):
    return lax.dot_general(a, b, (((1,), (0,)), ((), ())), preferred_element_type=f32)


def dot_nt(a, b):
    return lax.dot_general(a, b, (((1,), (1,)), ((), ())), preferred_element_type=f32)


def dot_tn(a, b):
    return lax.dot_general(a, b, (((0,), (0,)), ((), ())), preferred_element_type=f32)


def split_two(x):
    high = x.astype(bf16)
    return high, (x - high.astype(f32)).astype(bf16)


def three_way(x, lane):
    high = x.astype(bf16).astype(f32)
    rest = x - high
    middle = rest.astype(bf16).astype(f32)
    last = rest - middle
    place = lax.rem(lane, 3)
    return jnp.where(place == 0, high, jnp.where(place == 1, middle, last)).astype(bf16)


LIMITS = (20, 24, 32, 48, 40, 40, 24, 20, 56)
TILES = 4


def place_and_count(counts):
    position = lax.axis_index("mp")
    return position, counts[position]


def row_number(rows, position):
    half = rows // 2
    index = lax.broadcasted_iota(jnp.int32, (rows, 128), 0)
    return jnp.where(index < half, index + position * half, index - half + (1 - position) * half)


def lookback_of(group, history):
    return jnp.where(
        group == 0, history * 2 // 7, jnp.where(group == 1, history * 4 // 7, history)
    ).astype(jnp.int32)


def split_pair(pair_ref, mine, theirs, columns):
    position = lax.axis_index("mp")

    @pl.when(position == 0)
    def _():
        mine[:, columns] = pair_ref[:, 0, :]
        theirs[:, columns] = pair_ref[:, 1, :]

    @pl.when(position != 0)
    def _():
        mine[:, columns] = pair_ref[:, 1, :]
        theirs[:, columns] = pair_ref[:, 0, :]


def join_pair(mine, theirs, pair_ref):
    position = lax.axis_index("mp")

    @pl.when(position == 0)
    def _():
        pair_ref[:, 0, :] = mine[...]
        pair_ref[:, 1, :] = theirs[...]

    @pl.when(position != 0)
    def _():
        pair_ref[:, 1, :] = mine[...]
        pair_ref[:, 0, :] = theirs[...]


def prepare_attention(
    groups, series, attend, embed, embed_bias, query_bias, inner_bias,
    send, series_own, table, bias_row, small,
):
    half, _, history = series.shape
    depth = attend.shape[1] // 2
    send[:half, 256:] = jnp.zeros((half, send.shape[1] - 256), bf16)
    split_pair(series, series_own, send.at[:half], slice(0, history))
    for kind in range(3):
        rows = slice(half + kind * depth, half + (kind + 1) * depth)
        send[rows, :256] = attend[kind, :depth, :].astype(bf16)
        send[rows, 256:] = attend[kind, depth:, :].astype(bf16)
    group = groups[lax.axis_index("mp")]
    chosen = embed[group]
    row = lax.broadcasted_iota(jnp.int32, chosen.shape, 0)
    table[...] = jnp.where(row >= history - lookback_of(group, history), chosen, 0.0).astype(bf16)
    row = lax.broadcasted_iota(jnp.int32, embed_bias.shape, 0)
    bias_row[...] = jnp.sum(jnp.where(row == group, embed_bias[...], 0.0), axis=0, keepdims=True)
    small[...] = jnp.zeros_like(small)
    small[0:2, : query_bias.shape[1]] = query_bias[...]
    small[2:3, :] = inner_bias[...]


def prepare_feed(cotangent, mixer, inner, outer, send, cot_own):
    half = cotangent.shape[0]
    m, d = mixer.shape[0], inner.shape[0]
    o = outer.shape[0]
    send[:m] = mixer[...].astype(bf16)
    send[m : m + d] = inner[:, :512].astype(bf16)
    send[m + d : m + 2 * d] = inner[:, 512:].astype(bf16)
    send[m + 2 * d : m + 2 * d + o] = outer[...].astype(bf16)
    split_pair(cotangent, cot_own, send.at[m + 2 * d + o :], slice(None))


def attend_block(pack, half, kind):
    start = half + kind * 256
    return jnp.concatenate([pack[start : start + 256, :256], pack[start : start + 256, 256:]], axis=0)


def attend_forward(
    counts, series_own, table, embed_bias, own, other, small, small_other,
    hidden_ref, token_ref, query_ref, key_ref, value_ref, context_ref, lse_ref,
):
    rows, width = hidden_ref.shape
    half, history = series_own.shape
    part = width // 2
    head_dim = width // HEADS
    position, count = place_and_count(counts)
    for index, block in enumerate((series_own[...], other[:half, :history])):
        values = dot_nn(block, table[...]) + embed_bias[...]
        hidden_ref[pl.ds(index * half, half), :] = values
        token_ref[pl.ds(index * half, half), :] = values.astype(bf16)
    scale = head_dim**-0.5 * log2_e
    tokens = token_ref[...]
    for index, (pack, bias) in enumerate(((own, small), (other, small_other))):
        columns = pl.ds(index * part, part)
        query_ref[:, columns] = (
            (dot_nn(tokens, attend_block(pack, half, 0)) + bias[0:1, :part]) * scale
        ).astype(bf16)
        key_ref[:, columns] = dot_nn(tokens, attend_block(pack, half, 1)).astype(bf16)
        value_ref[:, columns] = (
            dot_nn(tokens, attend_block(pack, half, 2)) + bias[1:2, :part]
        ).astype(bf16)
    lane = lax.broadcasted_iota(jnp.int32, (rows, 128), 1)
    dead = row_number(rows, position) >= count
    extra_query = jnp.where(lane == 0, 1.0, 0.0).astype(bf16)
    extra_key = jnp.where((lane == 0) & dead, -1e30, 0.0).astype(bf16)
    ones = jnp.ones((rows, 128), bf16)
    lse_ref[...] = jnp.zeros_like(lse_ref)

    def pair(index, carry):
        columns = pl.ds(pl.multiple_of(index * 128, 128), 128)
        queries = query_ref[:, columns]
        keys = jnp.concatenate([key_ref[:, columns], extra_key], axis=1)
        values = jnp.concatenate([value_ref[:, columns], ones], axis=1)
        found = []
        for side in range(2):
            mine = (lane >= head_dim) if side else (lane < head_dim)
            query = jnp.concatenate(
                [jnp.where(mine, queries, jnp.zeros_like(queries)), extra_query], axis=1
            )
            scores = dot_nt(query, keys)
            peak = jnp.max(scores, axis=1, keepdims=True)
            soft = jnp.exp2(scores - peak).astype(bf16)
            mixed = dot_nn(soft, values)
            total = mixed[:, 128:]
            found.append(mixed[:, :128] / total)
            log_total = jnp.broadcast_to(peak, (rows, 128)) + jnp.log2(total)
            lse_ref[...] = jnp.where(lane // 3 == index * 2 + side, log_total, lse_ref[...])
        context_ref[:, columns] = jnp.where(lane < head_dim, found[0], found[1]).astype(bf16)
        return carry

    lax.fori_loop(0, width // 128, pair, 0)


def norm_rows(values, gain, shift):
    centered = values - jnp.mean(values, axis=-1, keepdims=True)
    inverse = lax.rsqrt(jnp.mean(centered * centered, axis=-1, keepdims=True) + norm_epsilon)
    unit = centered * inverse
    return unit * gain + shift, unit, inverse


def norm_rows_back(upstream, unit, inverse, gain):
    scaled = upstream * gain
    return inverse * (
        scaled
        - jnp.mean(scaled, axis=-1, keepdims=True)
        - unit * jnp.mean(scaled * unit, axis=-1, keepdims=True)
    )


def feed_forward(
    tiles, counts, context_ref, hidden_ref, own, other, small, small_other, gains, biases, cot_own,
    output_ref, output_send, active_ref, preact_ref, normed_ref, feed_ref, attend_ref, resid_ref,
    context_grad_ref, delta_ref, sums_ref, inner_sum_ref, grads_send, slope_ref,
):
    rows, width = hidden_ref.shape
    tile = rows // tiles
    half = rows // 2
    part = width // 2
    units = active_ref.shape[1]
    inner_part = units // 2
    chunk = 512
    position, count = place_and_count(counts)
    sums_ref[...] = jnp.zeros_like(sums_ref)
    inner_sum_ref[...] = jnp.zeros_like(inner_sum_ref)
    at_inner = part
    at_outer = part + inner_part
    at_cot = at_outer + inner_part

    def inner_chunk(index):
        pack = (own, other)[index * chunk // inner_part]
        start = at_inner + (index * chunk % inner_part) // chunk * width
        return pack[start : start + width, :]

    def outer_chunk(index):
        pack = (own, other)[index * chunk // inner_part]
        start = at_outer + index * chunk % inner_part
        return pack[start : start + chunk, :]

    head_dim = width // HEADS
    head = lax.broadcasted_iota(jnp.int32, (width, 128), 0) // head_dim
    lane = lax.broadcasted_iota(jnp.int32, (width, 128), 1)
    chooser = jnp.where(lane // 3 == head, -1.0, 0.0).astype(bf16)

    def add(row, values):
        sums_ref[row : row + 1, :] += jnp.sum(values, axis=0, keepdims=True)

    def one_tile(step, carry):
        place = pl.ds(pl.multiple_of(step * tile, tile), tile)
        context = context_ref[place, :]
        attended = dot_nn(context[:, :part], own[:part, :]) + dot_nn(
            context[:, part:], other[:part, :]
        )
        normed, unit_one, inverse_one = norm_rows(
            hidden_ref[place, :] + attended + biases[2:3, :], gains[0:1, :], biases[0:1, :]
        )
        normed_low = normed.astype(bf16)
        normed_ref[place, :] = normed_low
        for index in range(units // chunk):
            columns = slice(index * chunk, (index + 1) * chunk)
            bias = (small, small_other)[index * chunk // inner_part]
            start = index * chunk % inner_part
            preact = dot_nn(normed_low, inner_chunk(index)) + bias[2:3, start : start + chunk]
            phi = 0.5 + 0.5 * lax.erf(preact * inverse_root_two)
            active_ref[place, columns] = (preact * phi).astype(bf16)
            slope_ref[:, columns] = (
                phi + preact * jnp.exp2(preact * preact * (-0.5 * log2_e)) * inverse_root_tau
            ).astype(bf16)
        feed_out = dot_nn(active_ref[place, :inner_part], own[at_outer:at_cot, :]) + dot_nn(
            active_ref[place, inner_part:], other[at_outer:at_cot, :]
        )
        output, unit_two, inverse_two = norm_rows(
            normed + feed_out + biases[3:4, :], gains[1:2, :], biases[1:2, :]
        )
        index = lax.broadcasted_iota(jnp.int32, (tile, width), 0)

        @pl.when(step < tiles // 2)
        def _():
            output_ref[place, :] = output
        far = step - tiles // 2
        far_place = pl.ds(pl.multiple_of(jnp.maximum(far, 0) * tile, tile), tile)
        near_place = pl.ds(pl.multiple_of(jnp.minimum(step, tiles // 2 - 1) * tile, tile), tile)

        @pl.when(step >= tiles // 2)
        def _():
            output_send[far_place, :] = output
        cot = jnp.where(
            step < tiles // 2,
            cot_own[near_place, :],
            other[pl.ds(pl.multiple_of(at_cot + jnp.maximum(far, 0) * tile, 32), tile), :],
        ).astype(f32)
        first = jnp.where(
            step < tiles // 2,
            position * half + step * tile,
            (1 - position) * half + far * tile,
        )
        upstream = jnp.where(index + first < count, cot, 0.0)
        resid_two = norm_rows_back(upstream, unit_two, inverse_two, gains[1:2, :])
        feed_grad = resid_two.astype(bf16)
        feed_ref[place, :] = feed_grad
        for index in range(units // chunk):
            columns = slice(index * chunk, (index + 1) * chunk)
            grad = dot_nt(feed_grad, outer_chunk(index))
            preact_ref[place, columns] = (grad * slope_ref[:, columns].astype(f32)).astype(bf16)
        normed_grad = resid_two
        for index in range(units // chunk):
            columns = slice(index * chunk, (index + 1) * chunk)
            normed_grad = normed_grad + dot_nt(preact_ref[place, columns], inner_chunk(index))
        resid_one = norm_rows_back(normed_grad, unit_one, inverse_one, gains[0:1, :])
        resid_ref[place, :] = resid_one
        attend_grad = resid_one.astype(bf16)
        attend_ref[place, :] = attend_grad
        context_grad = jnp.concatenate(
            [dot_nt(attend_grad, own[:part, :]), dot_nt(attend_grad, other[:part, :])], axis=1
        ).astype(bf16)
        context_grad_ref[place, :] = context_grad
        high, low = split_two(context_grad.astype(f32) * context.astype(f32))
        delta = dot_nn(high, chooser) + dot_nn(low, chooser)
        delta_ref[place, :] = three_way(delta, lax.broadcasted_iota(jnp.int32, (tile, 128), 1))
        add(1, normed_grad * unit_one)
        add(2, upstream * unit_two)
        add(3, normed_grad)
        add(4, upstream)
        add(5, resid_one)
        add(6, resid_two)
        inner_sum_ref[0:1, :] += jnp.sum(preact_ref[place, :].astype(f32), axis=0, keepdims=True)
        return carry

    lax.fori_loop(0, tiles, one_tile, 0)
    grads_send[:inner_part, :] = dot_tn(active_ref[:, inner_part:], feed_ref[...]).astype(bf16)
    for index in range(inner_part // chunk):
        start = inner_part + index * chunk
        grads_send[inner_part + index * width : inner_part + (index + 1) * width, :] = dot_tn(
            normed_ref[...], preact_ref[:, start : start + chunk]
        ).astype(bf16)
    grads_send[2 * inner_part :, :] = dot_tn(context_ref[:, part:], attend_ref[...]).astype(bf16)


def attend_backward(
    groups, counts, query_ref, key_ref, value_ref, lse_ref, context_grad_ref, delta_ref,
    token_ref, resid_ref, own, other, table, series_own, sums_ref, inner_sum_ref,
    attend_own, send, series_near, series_far, near_out, far_out,
    dquery_ref, dkey_ref, dvalue_ref,
):
    rows, width = query_ref.shape
    head_dim = width // HEADS
    half, history = series_own.shape
    part = width // 2
    position, count = place_and_count(counts)
    lane = lax.broadcasted_iota(jnp.int32, (rows, 128), 1)
    dead = row_number(rows, position) >= count
    extra_query = jnp.where(lane == 127, jnp.ones((rows, 128), bf16), three_way(-lse_ref[...], lane))
    extra_key = jnp.where((lane == 127) & dead, -1e30, 0.0)
    extra_grad = delta_ref[...]

    def pair(index, carry):
        columns = pl.ds(pl.multiple_of(index * 128, 128), 128)
        queries = query_ref[:, columns]
        keys = key_ref[:, columns]
        values = value_ref[:, columns]
        grads = context_grad_ref[:, columns]
        dquery = dkey = dvalue = None
        for side in range(2):
            mine = (lane >= head_dim) if side else (lane < head_dim)
            hot = lane // 3 == index * 2 + side
            nothing = jnp.zeros_like(queries)
            query = jnp.where(mine, queries, nothing)
            grad = jnp.where(mine, grads, nothing)
            key = jnp.where(mine, keys, nothing)
            soft = jnp.exp2(
                dot_nt(
                    jnp.concatenate([keys, jnp.where(hot, 1.0, extra_key).astype(bf16)], axis=1),
                    jnp.concatenate([query, extra_query], axis=1),
                )
            )
            centered = dot_nt(
                jnp.concatenate([values, jnp.where(hot, 1.0, 0.0).astype(bf16)], axis=1),
                jnp.concatenate([grad, extra_grad], axis=1),
            )
            score_grad = (soft * centered).astype(bf16)
            one = dot_nn(soft.astype(bf16), grad)
            two = dot_nn(score_grad, query)
            three = dot_tn(key, score_grad)
            dvalue = one if dvalue is None else dvalue + one
            dkey = two if dkey is None else dkey + two
            dquery = three if dquery is None else dquery + three
        dvalue_ref[:, columns] = dvalue.astype(bf16)
        dkey_ref[:, columns] = (dkey * ln_two).astype(bf16)
        dquery_ref[:, columns] = (dquery.T * head_dim**-0.5).astype(bf16)
        return carry

    lax.fori_loop(0, width // 128, pair, 0)

    tokens = token_ref[...]
    total = resid_ref[...]
    near_out[...] = jnp.zeros_like(near_out)
    far_out[...] = jnp.zeros_like(far_out)
    for kind, grad_ref in enumerate((dquery_ref, dkey_ref, dvalue_ref)):
        low = grad_ref[...]
        attend_own[kind] = dot_tn(tokens, low[:, :part])
        far = dot_tn(tokens, low[:, part:]).astype(bf16)
        send[kind * part : (kind + 1) * part, :part] = far[:part]
        send[kind * part : (kind + 1) * part, part:] = far[part:]
        total = (
            total
            + dot_nt(low[:, :part], attend_block(own, half, kind))
            + dot_nt(low[:, part:], attend_block(other, half, kind))
        )
        if kind != 1:
            column = jnp.sum(low.astype(f32), axis=0, keepdims=True)
            start = kind // 2 * part
            near_out[7:8, start : start + part] = column[:, :part]
            far_out[7:8, start : start + part] = column[:, part:]
    low = total.astype(bf16)
    series_near[...] = dot_nt(low[:half], table[...])
    series_far[...] = dot_nt(low[half:], table[...])
    table_grad = dot_tn(series_own[...], low[:half]) + dot_tn(other[:half, :history], low[half:])
    row = lax.broadcasted_iota(jnp.int32, table_grad.shape, 0)
    seen = row >= history - lookback_of(groups[position], history)
    send[3 * part :, :] = jnp.where(seen, table_grad, 0.0).astype(bf16)
    shared = sums_ref[0:7, :]
    bias_grad = jnp.sum(low.astype(f32), axis=0, keepdims=True)
    near_out[0:7, :] = shared
    far_out[0:7, :] = shared
    near_out[0:1, :] = bias_grad
    far_out[0:1, :] = bias_grad
    count_near = inner_sum_ref.shape[1] // 2 // width
    for index in range(count_near):
        near_out[8 + index : 9 + index, :] = inner_sum_ref[0:1, index * width : (index + 1) * width]
        far_out[8 + index : 9 + index, :] = inner_sum_ref[
            0:1, (count_near + index) * width : (count_near + index + 1) * width
        ]


def left_product(start, matrix):
    start_high, start_low = split_two(start)
    high, low = split_two(matrix)
    both = dot_nt(jnp.concatenate([start_high, start_low], axis=0), high)
    return both[:8] + both[8:] + dot_nt(start_high, low)


def right_product(basis, matrix):
    basis_high, basis_low = split_two(basis)
    high, low = split_two(matrix)
    both = dot_nn(jnp.concatenate([basis_high, basis_low], axis=0), high)
    return both[:8] + both[8:] + dot_nn(basis_high, low)


def feed_matrices(
    active_ref, preact_ref, normed_ref, feed_ref, context_ref, attend_ref, received,
    e_outer, e_inner, e_mixer, s_outer, s_inner, s_mixer, output_near, output_far,
    outer, inner, mixer, left, output,
):
    width = feed_ref.shape[1]
    inner_part = outer.shape[0]
    part = mixer.shape[0]
    chunk = 512
    join_pair(output_near, output_far, output)
    outer[...] = (
        dot_tn(active_ref[:, :inner_part], feed_ref[...])
        + received[:inner_part, :].astype(f32)
        + e_outer[...]
    )
    for index in range(inner_part // chunk):
        columns = slice(index * chunk, (index + 1) * chunk)
        start = inner_part + index * width
        inner[:, columns] = (
            dot_tn(normed_ref[...], preact_ref[:, columns])
            + received[start : start + width, :].astype(f32)
            + e_inner[:, columns]
        )
    mixer[...] = (
        dot_tn(context_ref[:, :part], attend_ref[...])
        + received[2 * inner_part :, :].astype(f32)
        + e_mixer[...]
    )
    left[:, 0:1024] = left_product(s_outer[...], outer[...])
    left[:, 1024:1536] = left_product(s_inner[...], inner[...])
    left[:, 1536:1792] = left_product(s_mixer[...], mixer[...])


def other_matrices(
    groups, near_attend, own, received, e_attend, e_embed, s_attend, s_embed, left_part, near, far,
    series_near, series_far,
    attend, embed, left, series_grad,
):
    part = near_attend.shape[2]
    position = lax.axis_index("mp")
    join_pair(series_near, series_far, series_grad)
    total = None
    for kind in range(3):
        rows = slice(kind * part, (kind + 1) * part)
        block = jnp.concatenate([received[rows, :part], received[rows, part:]], axis=0)
        attend[kind] = near_attend[kind] + block.astype(f32) + e_attend[kind]
        term = left_product(s_attend[kind], attend[kind])
        total = term if total is None else total + term
    mine, theirs = groups[position], groups[1 - position]
    table_near = own[3 * part :, :].astype(f32)
    table_far = received[3 * part :, :].astype(f32)
    pieces = []
    for group in range(embed.shape[0]):
        grad = jnp.where(mine == group, table_near, 0.0) + jnp.where(theirs == group, table_far, 0.0)
        embed[group] = grad + e_embed[group]
        pieces.append(left_product(s_embed[...], embed[group]))
    used = embed.shape[0] * embed.shape[1]
    left[:, 0:1024] = jnp.concatenate(pieces + [jnp.zeros((8, 1024 - used), f32)], axis=1)
    left[:, 1024:2048] = left_part[:, 0:1024]
    left[:, 2048:2560] = total
    left[:, 2560:3328] = left_part[:, 1024:1792]
    common = near[1:7, :] + far[1:7, :]
    row = lax.broadcasted_iota(jnp.int32, (3, near.shape[1]), 0)
    bias = jnp.where(row == mine, near[0:1, :], 0.0) + jnp.where(row == theirs, far[0:1, :], 0.0)
    left[:, 3328:3840] = jnp.concatenate([bias, common[:5]], axis=0)
    rest = jnp.concatenate([common[5:6], near[7:10, :] + far[7:10, :]], axis=0)
    for row in range(4):
        left[2 * row : 2 * row + 1, 3840:4096] = rest[row : row + 1, :256]
        left[2 * row + 1 : 2 * row + 2, 3840:4096] = rest[row : row + 1, 256:]


def orthonormal_rows(vectors):
    rank = vectors.shape[0]
    row = lax.broadcasted_iota(jnp.int32, vectors.shape, 0)
    for index in range(rank):
        pivot = vectors[index : index + 1, :]
        inner = jnp.sum(vectors * pivot, axis=1, keepdims=True)
        size = inner[index : index + 1, :] + 1e-12
        reduced = vectors - pivot * (inner / size)
        vectors = jnp.where(
            row > index, reduced, jnp.where(row == index, vectors * lax.rsqrt(size), vectors)
        )
    return vectors


def reduce_factors(
    replicas, start_ref, embed, outer, attend, inner, mixer,
    left_ref, right_ref, mean_ref,
    summed, partial, gathered, parts_one, parts_two, send_sems, recv_sems,
):
    me = lax.axis_index("dp")
    barrier = pltpu.get_barrier_semaphore()
    chunk = start_ref.shape[1] // replicas
    share = 1.0 / replicas

    def peer(offset):
        return lax.rem(me + offset, replicas)

    def columns(index):
        return pl.ds(pl.multiple_of(index * chunk, 128), chunk)

    def each(what):
        def body(offset, carry):
            what(offset)
            return carry

        lax.fori_loop(1, replicas, body, 0)

    each(
        lambda offset: pl.semaphore_signal(
            barrier, inc=1, device_id={"dp": peer(offset)}, device_id_type=pl.DeviceIdType.MESH
        )
    )
    pl.semaphore_wait(barrier, replicas - 1)

    def all_sum(phase, source, parts, result):
        def scatter(offset):
            other = peer(offset)
            return pltpu.make_async_remote_copy(
                src_ref=source.at[:, columns(other)],
                dst_ref=parts.at[offset],
                send_sem=send_sems.at[2 * phase, offset],
                recv_sem=recv_sems.at[2 * phase, offset],
                device_id={"dp": other},
                device_id_type=pl.DeviceIdType.MESH,
            )

        def spread(offset, owner):
            return pltpu.make_async_remote_copy(
                src_ref=result.at[:, columns(owner)],
                dst_ref=result.at[:, columns(owner)],
                send_sem=send_sems.at[2 * phase + 1, offset],
                recv_sem=recv_sems.at[2 * phase + 1, offset],
                device_id={"dp": peer(offset)},
                device_id_type=pl.DeviceIdType.MESH,
            )

        each(lambda offset: scatter(offset).start())

        def collect(offset, total):
            scatter(offset).wait_recv()
            return total + parts[offset]

        total = lax.fori_loop(1, replicas, collect, source[:, columns(me)])
        result[:, columns(me)] = total * share
        each(lambda offset: spread(offset, me).start())
        each(lambda offset: spread(offset, lax.rem(me - offset + replicas, replicas)).wait_recv())
        each(lambda offset: scatter(offset).wait_send())
        each(lambda offset: spread(offset, me).wait_send())

    all_sum(0, start_ref, parts_one, summed)
    mean_ref[...] = summed[:, 3328:4096]
    bases = []
    for start, size in ((0, 1024), (1024, 1024), (2048, 512), (2560, 512), (3072, 256)):
        basis = orthonormal_rows(summed[:, start : start + size])
        left_ref[:, start : start + size] = basis
        bases.append(basis)
    height = embed.shape[1]
    total = None
    for group in range(embed.shape[0]):
        term = right_product(bases[0][:, group * height : (group + 1) * height], embed[group])
        total = term if total is None else total + term
    partial[:, 0:512] = total
    partial[:, 512:1024] = right_product(bases[1], outer[...])
    for kind in range(3):
        partial[:, 1024 + kind * 256 : 1280 + kind * 256] = right_product(bases[2], attend[kind])
    partial[:, 1792:2816] = right_product(bases[3], inner[...])
    partial[:, 2816:3328] = right_product(bases[4], mixer[...])
    partial[:, 3328:] = jnp.zeros((8, partial.shape[1] - 3328), f32)
    all_sum(1, partial, parts_two, gathered)
    right_ref[...] = gathered[:, :3328]


def renew_all(
    step_rate, mixer_rate, left, right, mean, *refs,
):
    matrices, weights, moments = refs[0:5], refs[5:10], refs[10:15]
    vectors, vector_moments = refs[15:20], refs[20:25]
    errors, new_weights, new_moments = refs[25:30], refs[30:35], refs[35:40]
    new_vectors, new_vector_moments = refs[40:45], refs[45:50]
    lefts, rights = refs[50:55], refs[55:60]
    step = pl.program_id(0)

    def approx(basis, factor):
        left_high, left_low = split_two(basis)
        right_high, right_low = split_two(factor)
        return dot_tn(
            jnp.concatenate([left_high, left_low, left_high, left_low], axis=0),
            jnp.concatenate([right_high, right_high, right_low, right_low], axis=0),
        )

    def write(index, where, update, rate):
        errors[index][where] = matrices[index][where] - update
        moment = momentum_decay * moments[index][where] + update
        new_moments[index][where] = moment
        new_weights[index][where] = weights[index][where] - rate * moment

    def cut(start, size):
        return pl.ds(pl.multiple_of(start + step * size, 128), size)

    every = (slice(None), slice(None))
    groups, height, block = matrices[0].shape
    factor = right[:, cut(0, block)]
    for group in range(groups):
        write(
            0, (group, slice(None), slice(None)),
            approx(left[:, group * height : (group + 1) * height], factor), step_rate,
        )
    write(1, every, approx(left[:, cut(1024, matrices[1].shape[0])], right[:, 512:1024]), step_rate)
    basis = left[:, cut(2048, matrices[2].shape[1])]
    for kind in range(3):
        write(
            2, (kind, slice(None), slice(None)),
            approx(basis, right[:, 1024 + kind * 256 : 1280 + kind * 256]), step_rate,
        )
    write(3, every, approx(left[:, cut(2560, matrices[3].shape[0])], right[:, 1792:2816]), step_rate)
    write(4, every, approx(left[:, 3072:3328], right[:, cut(2816, matrices[4].shape[1])]), mixer_rate)

    @pl.when(step == 0)
    def _():
        for group in range(groups):
            lefts[0][group] = left[:, group * height : (group + 1) * height]
        lefts[1][...] = left[:, 1024:2048]
        lefts[2][...] = left[:, 2048:2560]
        lefts[3][...] = left[:, 2560:3072]
        lefts[4][...] = left[:, 3072:3328]
        rights[0][...] = right[:, 0:512]
        rights[1][...] = right[:, 512:1024]
        for kind in range(3):
            rights[2][kind] = right[:, 1024 + kind * 256 : 1280 + kind * 256]
        rights[3][...] = right[:, 1792:2816]
        rights[4][...] = right[:, 2816:3328]

        def renew(index, rows, columns, gradient):
            moment = momentum_decay * vector_moments[index][rows, columns] + gradient
            new_vector_moments[index][rows, columns] = moment
            new_vectors[index][rows, columns] = vectors[index][rows, columns] - step_rate * moment

        renew(0, slice(0, 3), slice(None), mean[0:3, :512])
        renew(1, slice(0, 2), slice(None), mean[3:5, :512])
        renew(2, slice(0, 3), slice(None), mean[5:8, :512])
        renew(2, slice(3, 4), slice(0, 256), mean[0:1, 512:])
        renew(2, slice(3, 4), slice(256, 512), mean[1:2, 512:])
        renew(3, slice(0, 1), slice(None), mean[2:3, 512:])
        renew(3, slice(1, 2), slice(None), mean[3:4, 512:])
        for index in range(4):
            renew(
                4, slice(0, 1), slice(index * 256, (index + 1) * 256),
                mean[4 + index : 5 + index, 512:],
            )


def call(kernel, outs, args, *, in_specs=None, scratch=(), limit=32, name=None):
    return pl.pallas_call(
        kernel,
        out_shape=outs,
        in_specs=in_specs if in_specs is not None else [VM] * len(args),
        out_specs=jax.tree.map(lambda _: VM, outs),
        scratch_shapes=list(scratch),
        compiler_params=pltpu.CompilerParams(vmem_limit_bytes=limit * MIB),
        name=name,
    )(*args)


def sds(shape, dtype=f32):
    return jax.ShapeDtypeStruct(shape, dtype)


def local(
    series, groups, counts, cotangent,
    embed_weight, embed_moment, embed_error, embed_start,
    attend_weight, attend_moment, attend_error, attend_start,
    mixer_weight, mixer_moment, mixer_error, mixer_start,
    inner_weight, inner_moment, inner_error, inner_start,
    outer_weight, outer_moment, outer_error, outer_start,
    embed_bias, embed_bias_moment, query_bias, query_bias_moment,
    inner_bias, inner_bias_moment, norm_gains, gains_moment, shared_biases, biases_moment,
):
    replicas = lax.axis_size("dp")
    half, windows, history = series.shape
    rows = 2 * half
    group_count, _, width = embed_weight.shape
    part = attend_weight.shape[2]
    inner_part = inner_weight.shape[1]
    units = 2 * inner_part
    turned = lambda a: a.transpose(1, 0, 2)

    def swap(values):
        return lax.ppermute(values, "mp", [(0, 1), (1, 0)])

    low = sds((rows, width), bf16)
    full = sds((rows, width))
    near = sds((half, width))
    send_one, series_own, table, bias_row, small = call(
        prepare_attention,
        [sds((half + 3 * part, width), bf16), sds((half, history), bf16), sds((history, width), bf16),
         sds((1, width)), sds((8, inner_part))],
        (groups, series, turned(attend_weight), embed_weight, embed_bias, query_bias, inner_bias[None]),
        in_specs=[SM] + [VM] * 6, limit=LIMITS[0],
        name="prepare_attention",
    )
    other_one = swap(send_one)
    small_other = swap(small)
    send_two, cot_own = call(
        prepare_feed,
        [sds((part + 2 * inner_part + half, width), bf16), sds((half, width), bf16)],
        (cotangent, mixer_weight, inner_weight, outer_weight), limit=LIMITS[1],
        name="prepare_feed",
    )
    other_two = swap(send_two)
    hidden, tokens, queries, keys, values, context, lse = call(
        attend_forward,
        [full, low, low, low, low, low, sds((rows, 128))],
        (counts, series_own, table, bias_row, send_one, other_one, small, small_other),
        in_specs=[SM] + [VM] * 7, limit=LIMITS[2],
        name="attend_forward",
    )
    (
        output_near, output_send, active, preact_grad, normed_low, feed_grad, attend_out, resid_one,
        context_grad, delta, sums, inner_sums, grads_send,
    ) = call(
        functools.partial(feed_forward, TILES),
        [near, near, sds((rows, units), bf16), sds((rows, units), bf16), low, low, low, full, low,
         sds((rows, 128), bf16), sds((8, width)), sds((8, units)),
         sds((2 * inner_part + part, width), bf16)],
        (counts, context, hidden, send_two, other_two, small, small_other, norm_gains, shared_biases, cot_own),
        in_specs=[SM] + [VM] * 9, limit=LIMITS[3],
        scratch=[pltpu.VMEM((rows // TILES, units), bf16)],
        name="feed_forward",
    )
    output_other = swap(output_send)
    grads_other = swap(grads_send)
    attend_near, send_three, series_near, series_far, sums_near, sums_far = call(
        attend_backward,
        [sds((3, width, part)), sds((3 * part + history, width), bf16), sds((half, history)),
         sds((half, history)), sds((16, width)), sds((16, width))],
        (groups, counts, queries, keys, values, lse, context_grad, delta, tokens, resid_one, send_one,
         other_one, table, series_own, sums, inner_sums),
        in_specs=[SM] * 2 + [VM] * 14, limit=LIMITS[4],
        scratch=[pltpu.VMEM((rows, width), bf16)] * 3,
        name="attend_backward",
    )
    other_three = swap(send_three)
    series_other = swap(series_far)
    sums_other = swap(sums_far)
    outer_matrix, inner_matrix, mixer_matrix, left_part, output = call(
        feed_matrices,
        [sds(outer_weight.shape), sds(inner_weight.shape), sds(mixer_weight.shape), sds((8, 1792)),
         sds((half, windows, width))],
        (active, preact_grad, normed_low, feed_grad, context, attend_out, grads_other,
         outer_error[0], inner_error[0], mixer_error[0], outer_start[0].T, inner_start.T, mixer_start[0].T,
         output_near, output_other),
        limit=LIMITS[5],
        name="feed_matrices",
    )
    attend_matrix, embed_matrix, left_partial, series_grad = call(
        other_matrices,
        [sds((3, width, part)), sds(embed_weight.shape), sds((8, 4096)), sds((half, windows, history))],
        (groups, attend_near, send_three, other_three, turned(attend_error[0]), embed_error[0],
         attend_start.transpose(0, 2, 1), embed_start.T, left_part, sums_near, sums_other,
         series_near, series_other),
        in_specs=[SM] + [VM] * 12, limit=LIMITS[6],
        name="other_matrices",
    )
    matrices = (embed_matrix, outer_matrix, attend_matrix, inner_matrix, mixer_matrix)
    padded = max(128, -(-4096 // replicas // 128) * 128)
    total = padded * replicas
    if total > 4096:
        left_partial = jnp.pad(left_partial, ((0, 0), (0, total - 4096)))
    left, right, mean = pl.pallas_call(
        functools.partial(reduce_factors, replicas),
        out_shape=[sds((8, 3328)), sds((8, 3328)), sds((8, 768))],
        in_specs=[VM] * 6,
        out_specs=[VM] * 3,
        scratch_shapes=[
            pltpu.VMEM((8, total), f32), pltpu.VMEM((8, total), f32), pltpu.VMEM((8, total), f32),
            pltpu.VMEM((replicas, 8, padded), f32), pltpu.VMEM((replicas, 8, padded), f32),
            pltpu.SemaphoreType.DMA((4, replicas)), pltpu.SemaphoreType.DMA((4, replicas)),
        ],
        compiler_params=pltpu.CompilerParams(
            collective_id=1, has_side_effects=True, vmem_limit_bytes=LIMITS[7] * MIB
        ),
        name="reduce_factors",
    )(left_partial, *matrices)

    step_rate = base_rate * math.sqrt(replicas * 7 / (windows * rows))
    mixer_rate = step_rate * math.sqrt(width / max(width * 16 // rows, 1))
    steps = 4
    whole = lambda a: pl.BlockSpec(a.shape, lambda i: (0,) * len(a.shape))
    column = lambda a: pl.BlockSpec((a.shape[0], a.shape[1] // steps), lambda i: (0, i))
    row = lambda a: pl.BlockSpec((a.shape[0] // steps, a.shape[1]), lambda i: (i, 0))
    middle = lambda a: pl.BlockSpec((a.shape[0], a.shape[1] // steps, a.shape[2]), lambda i: (0, i, 0))
    last = lambda a: pl.BlockSpec((a.shape[0], a.shape[1], a.shape[2] // steps), lambda i: (0, 0, i))
    specs = [spec(a) for spec, a in zip((last, row, middle, row, column), matrices)]
    vectors = (embed_bias, norm_gains, shared_biases, query_bias, inner_bias[None])
    vector_moments = (
        embed_bias_moment, gains_moment, biases_moment, query_bias_moment, inner_bias_moment[None]
    )
    vector_specs = [whole(a) for a in vectors]
    factors = [
        sds((group_count, 8, history)), sds((8, 1024)), sds((8, 512)), sds((8, 512)), sds((8, 256)),
        sds((8, 512)), sds((8, 512)), sds((3, 8, part)), sds((8, 1024)), sds((8, 512)),
    ]
    found = pl.pallas_call(
        functools.partial(renew_all, step_rate, mixer_rate),
        grid=(steps,),
        out_shape=[sds(a.shape) for a in matrices] * 3 + [sds(a.shape) for a in vectors] * 2 + factors,
        in_specs=[whole(left), whole(right), whole(mean)] + specs * 3 + vector_specs * 2,
        out_specs=specs * 3 + vector_specs * 2 + [whole(a) for a in factors],
        compiler_params=pltpu.CompilerParams(vmem_limit_bytes=LIMITS[8] * MIB),
        name="renew_all",
    )(
        left, right, mean, *matrices,
        embed_weight, outer_weight, turned(attend_weight), inner_weight, mixer_weight,
        embed_moment, outer_moment, turned(attend_moment), inner_moment, mixer_moment,
        *vectors, *vector_moments,
    )
    errors, weights, moments = found[0:5], found[5:10], found[10:15]
    new_vectors, new_vector_moments = found[15:20], found[20:25]
    lefts, rights = found[25:30], found[30:35]
    return (
        output,
        series_grad,
        weights[0],
        moments[0],
        errors[0][None],
        lefts[0].transpose(0, 2, 1),
        rights[0].T,
        turned(weights[2]),
        turned(moments[2]),
        turned(errors[2])[None],
        lefts[2].T[None],
        rights[2].transpose(0, 2, 1),
        weights[4],
        moments[4],
        errors[4][None],
        lefts[4].T,
        rights[4].T[None],
        weights[3],
        moments[3],
        errors[3][None],
        lefts[3].T[None],
        rights[3].T,
        weights[1],
        moments[1],
        errors[1][None],
        lefts[1].T,
        rights[1].T[None],
        new_vector_moments[0],
        new_vectors[0],
        new_vector_moments[3],
        new_vectors[3],
        new_vector_moments[4][0],
        new_vectors[4][0],
        new_vector_moments[1],
        new_vectors[1],
        new_vector_moments[2],
        new_vectors[2],
    )


def solution(mesh):
    return jax.shard_map(
        local,
        mesh=mesh,
        in_specs=(
            P("mp", "dp", None),
            P("dp"),
            P("dp"),
            P("mp", "dp", None),
            P(),
            P(),
            P("dp", None, None, None),
            P(),
            P(None, None, "mp"),
            P(None, None, "mp"),
            P("dp", None, None, "mp"),
            P(None, "mp", None),
            P("mp", None),
            P("mp", None),
            P("dp", "mp", None),
            P("mp", None, None),
            P(None, "mp"),
            P(None, "mp"),
            P("dp", None, "mp"),
            P("mp", None),
            P("mp", None),
            P("mp", None),
            P("dp", "mp", None),
            P("mp", None, None),
            P(),
            P(),
            P(None, "mp"),
            P(None, "mp"),
            P("mp"),
            P("mp"),
            P(),
            P(),
            P(),
            P(),
        ),
        out_specs=(
            P("mp", "dp", None),
            P("mp", "dp", None),
            P(),
            P(),
            P("dp", None, None, None),
            P(),
            P(),
            P(None, None, "mp"),
            P(None, None, "mp"),
            P("dp", None, None, "mp"),
            P("mp", None, None),
            P(None, "mp", None),
            P("mp", None),
            P("mp", None),
            P("dp", "mp", None),
            P("mp", None),
            P("mp", None, None),
            P(None, "mp"),
            P(None, "mp"),
            P("dp", None, "mp"),
            P("mp", None, None),
            P("mp", None),
            P("mp", None),
            P("mp", None),
            P("dp", "mp", None),
            P("mp", None),
            P("mp", None, None),
            P(),
            P(),
            P(None, "mp"),
            P(None, "mp"),
            P("mp"),
            P("mp"),
            P(),
            P(),
            P(),
            P(),
        ),
        check_vma=False,
    )
```

```python
import functools
import math

import jax
import jax.numpy as jnp
from jax import lax
from jax.experimental import pallas as pl
from jax.experimental.pallas import tpu as pltpu
from jax.sharding import PartitionSpec as P

HEADS = 8
momentum_decay = 0.9
norm_epsilon = 1e-05
base_rate = 0.03
inverse_root_two = 0.7071067811865476
inverse_root_tau = 0.3989422804014327
log2_e = 1.4426950408889634
ln_two = 0.6931471805599453
f32 = jnp.float32
bf16 = jnp.bfloat16
VMEM = pltpu.VMEM
VM = pl.BlockSpec(memory_space=pltpu.VMEM)
HB = pl.BlockSpec(memory_space=pltpu.HBM)
MIB = 1024 * 1024


def dot_nn(a, b):
    return lax.dot_general(a, b, (((1,), (0,)), ((), ())), preferred_element_type=f32)


def dot_nt(a, b):
    return lax.dot_general(a, b, (((1,), (1,)), ((), ())), preferred_element_type=f32)


def dot_tn(a, b):
    return lax.dot_general(a, b, (((0,), (0,)), ((), ())), preferred_element_type=f32)


def split_two(x):
    high = x.astype(bf16)
    return high, (x - high.astype(f32)).astype(bf16)


def three_way(x, lane):
    high = x.astype(bf16).astype(f32)
    rest = x - high
    middle = rest.astype(bf16).astype(f32)
    last = rest - middle
    place = lax.rem(lane, 3)
    return jnp.where(place == 0, high, jnp.where(place == 1, middle, last)).astype(bf16)


LIMITS = (12, 14, 12, 8, 16, 8, 8, 28)
TILES = 4


def row_number(rows, position):
    half = rows // 2
    index = lax.broadcasted_iota(jnp.int32, (rows, 128), 0)
    return jnp.where(index < half, index + position * half, index - half + (1 - position) * half)


def lookback_of(group, history):
    return jnp.where(
        group == 0, history * 2 // 7, jnp.where(group == 1, history * 4 // 7, history)
    ).astype(jnp.int32)


def split_pair(pair_ref, mine, theirs, columns):
    position = lax.axis_index("mp")

    @pl.when(position == 0)
    def _():
        mine[:, columns] = pair_ref[:, 0, :]
        theirs[:, columns] = pair_ref[:, 1, :]

    @pl.when(position != 0)
    def _():
        mine[:, columns] = pair_ref[:, 1, :]
        theirs[:, columns] = pair_ref[:, 0, :]


def join_pair(mine, theirs, pair_ref):
    position = lax.axis_index("mp")

    @pl.when(position == 0)
    def _():
        pair_ref[:, 0, :] = mine[...]
        pair_ref[:, 1, :] = theirs[...]

    @pl.when(position != 0)
    def _():
        pair_ref[:, 1, :] = mine[...]
        pair_ref[:, 0, :] = theirs[...]


def three_parts(x):
    high = x.astype(bf16)
    rest = x - high.astype(f32)
    middle = rest.astype(bf16)
    return high, middle, (rest - middle.astype(f32)).astype(bf16)


def prepare(
    groups_hbm, counts_hbm, series_hbm, attend_hbm, query_bias_hbm, inner_bias_hbm,
    cot_hbm, mixer_hbm, inner_hbm, outer_hbm,
    send, received, series_own, small, facts, send_feed, cot_own,
    groups, counts, series, attend, query_bias, inner_bias, cotangent, mixer, inner, outer,
    done, send_sems, recv_sems,
):
    position = lax.axis_index("mp")
    partner = {"mp": 1 - position}
    barrier = pltpu.get_barrier_semaphore()
    pl.semaphore_signal(barrier, inc=1, device_id=partner, device_id_type=pl.DeviceIdType.MESH)
    copies = []
    for source, target in (
        (query_bias_hbm, query_bias), (inner_bias_hbm, inner_bias), (attend_hbm, attend),
        (series_hbm, series), (groups_hbm, groups), (counts_hbm, counts), (cot_hbm, cotangent),
        (mixer_hbm, mixer), (inner_hbm, inner), (outer_hbm, outer),
    ):
        copies.append(pltpu.make_async_copy(source, target, done.at[len(copies)]))
        copies[-1].start()
    half, _, history = series.shape
    width = send.shape[1]
    depth = attend.shape[1] // 2
    end = half + 3 * depth
    part = query_bias.shape[1]
    trades = [
        pltpu.make_async_remote_copy(
            src_ref=send.at[rows], dst_ref=received.at[rows], send_sem=send_sems.at[index],
            recv_sem=recv_sems.at[index], device_id=partner, device_id_type=pl.DeviceIdType.MESH,
        )
        for index, rows in enumerate((slice(half, end + 16), slice(0, half)))
    ]
    copies[0].wait()
    copies[1].wait()
    small[...] = jnp.zeros_like(small)
    small[0:2, :part] = query_bias[...]
    small[2:3, :] = inner_bias[...]
    values = jnp.concatenate(
        [
            jnp.concatenate([query_bias[0:1, :], query_bias[1:2, :]], axis=1),
            inner_bias[:, :width],
            inner_bias[:, width:],
            jnp.zeros((1, width), f32),
        ],
        axis=0,
    )
    send[end : end + 16, :] = jnp.concatenate(
        [*three_parts(values), jnp.zeros((4, width), bf16)], axis=0
    )
    copies[2].wait()
    for kind in range(3):
        rows = slice(half + kind * depth, half + (kind + 1) * depth)
        send[rows, :256] = attend[kind, :depth, :].astype(bf16)
        send[rows, 256:] = attend[kind, depth:, :].astype(bf16)
    pl.semaphore_wait(barrier, 1)
    trades[0].start()
    send[:half, 256:] = jnp.zeros((half, width - 256), bf16)
    copies[3].wait()
    split_pair(series, series_own, send.at[:half], slice(0, history))
    trades[1].start()
    copies[4].wait()
    copies[5].wait()
    group = jnp.where(position == 0, groups[0], groups[1])
    other_group = jnp.where(position == 0, groups[1], groups[0])
    count = jnp.where(position == 0, counts[0], counts[1])
    first = history - lookback_of(group, history)
    row = lax.broadcasted_iota(jnp.int32, facts.shape, 0)
    facts[...] = jnp.where(
        row == 0, count, jnp.where(row == 1, first, jnp.where(row == 2, group, other_group))
    )
    m, d, o = mixer.shape[0], inner.shape[0], outer.shape[0]
    copies[6].wait()
    split_pair(cotangent, cot_own, send_feed.at[m + 2 * d + o :], slice(None))
    copies[7].wait()
    send_feed[:m] = mixer[...].astype(bf16)
    copies[8].wait()
    send_feed[m : m + d] = inner[:, :512].astype(bf16)
    send_feed[m + d : m + 2 * d] = inner[:, 512:].astype(bf16)
    copies[9].wait()
    send_feed[m + 2 * d : m + 2 * d + o] = outer[...].astype(bf16)
    for trade in trades:
        trade.wait()


def unpack_small(other, small_other):
    part = other.shape[1] // 2
    parts = other[other.shape[0] - 16 :, :].astype(f32)
    values = parts[0:4] + parts[4:8] + parts[8:12]
    small_other[0:1, :part] = values[0:1, :part]
    small_other[1:2, :part] = values[0:1, part:]
    small_other[2:3, : 2 * part] = values[1:2, :]
    small_other[2:3, 2 * part :] = values[2:3, :]


def attend_block(pack, half, kind):
    start = half + kind * 256
    return jnp.concatenate([pack[start : start + 256, :256], pack[start : start + 256, 256:]], axis=0)


def attend_forward(
    facts, series_own, embed, embed_bias, own, other, small,
    hidden_ref, token_ref, query_ref, key_ref, value_ref, context_ref, lse_ref, small_other, table,
):
    unpack_small(other, small_other)
    chosen, bias_row = embed[0], embed_bias[0:1, :]
    for group in range(1, embed.shape[0]):
        here = facts[2:3, 0:1] == group
        chosen = jnp.where(here, embed[group], chosen)
        bias_row = jnp.where(here, embed_bias[group : group + 1, :], bias_row)
    row = lax.broadcasted_iota(jnp.int32, chosen.shape, 0)
    table[...] = jnp.where(row >= facts[1:2, 0:1], chosen, 0.0).astype(bf16)
    rows, width = hidden_ref.shape
    half, history = series_own.shape
    part = width // 2
    head_dim = width // HEADS
    position, count = lax.axis_index("mp"), facts[0:1, 0:1]
    for index, block in enumerate((series_own[...], other[:half, :history])):
        values = dot_nn(block, table[...]) + bias_row
        hidden_ref[pl.ds(index * half, half), :] = values
        token_ref[pl.ds(index * half, half), :] = values.astype(bf16)
    scale = head_dim**-0.5 * log2_e
    tokens = token_ref[...]
    for index, (pack, bias) in enumerate(((own, small), (other, small_other))):
        columns = pl.ds(index * part, part)
        query_ref[:, columns] = (
            (dot_nn(tokens, attend_block(pack, half, 0)) + bias[0:1, :part]) * scale
        ).astype(bf16)
        key_ref[:, columns] = dot_nn(tokens, attend_block(pack, half, 1)).astype(bf16)
        value_ref[:, columns] = (
            dot_nn(tokens, attend_block(pack, half, 2)) + bias[1:2, :part]
        ).astype(bf16)
    lane = lax.broadcasted_iota(jnp.int32, (rows, 128), 1)
    dead = row_number(rows, position) >= count
    extra_query = jnp.where(lane == 0, 1.0, 0.0).astype(bf16)
    extra_key = jnp.where((lane == 0) & dead, -1e30, 0.0).astype(bf16)
    ones = jnp.ones((rows, 128), bf16)
    lse_ref[...] = jnp.zeros_like(lse_ref)

    def pair(index, carry):
        columns = pl.ds(pl.multiple_of(index * 128, 128), 128)
        queries = query_ref[:, columns]
        keys = jnp.concatenate([key_ref[:, columns], extra_key], axis=1)
        values = jnp.concatenate([value_ref[:, columns], ones], axis=1)
        found = []
        for side in range(2):
            mine = (lane >= head_dim) if side else (lane < head_dim)
            query = jnp.concatenate(
                [jnp.where(mine, queries, jnp.zeros_like(queries)), extra_query], axis=1
            )
            scores = dot_nt(query, keys)
            peak = jnp.max(scores, axis=1, keepdims=True)
            soft = jnp.exp2(scores - peak).astype(bf16)
            mixed = dot_nn(soft, values)
            total = mixed[:, 128:]
            found.append(mixed[:, :128] / total)
            log_total = jnp.broadcast_to(peak, (rows, 128)) + jnp.log2(total)
            lse_ref[...] = jnp.where(lane // 3 == index * 2 + side, log_total, lse_ref[...])
        context_ref[:, columns] = jnp.where(lane < head_dim, found[0], found[1]).astype(bf16)
        return carry

    lax.fori_loop(0, width // 128, pair, 0)


def norm_rows(values, gain, shift):
    centered = values - jnp.mean(values, axis=-1, keepdims=True)
    inverse = lax.rsqrt(jnp.mean(centered * centered, axis=-1, keepdims=True) + norm_epsilon)
    unit = centered * inverse
    return unit * gain + shift, unit, inverse


def norm_rows_back(upstream, unit, inverse, gain):
    scaled = upstream * gain
    return inverse * (
        scaled
        - jnp.mean(scaled, axis=-1, keepdims=True)
        - unit * jnp.mean(scaled * unit, axis=-1, keepdims=True)
    )


def feed_forward(
    tiles, facts, context_ref, hidden_ref, own, other, small, small_other, gains, biases, cot_own,
    output_ref, output_send, active_ref, preact_ref, normed_ref, feed_ref, attend_ref, resid_ref,
    context_grad_ref, delta_ref, sums_ref, inner_sum_ref, grads_send, slope_ref,
):
    rows, width = hidden_ref.shape
    tile = rows // tiles
    half = rows // 2
    part = width // 2
    units = active_ref.shape[1]
    inner_part = units // 2
    chunk = 512
    position, count = lax.axis_index("mp"), facts[0:1, 0:1]
    sums_ref[...] = jnp.zeros_like(sums_ref)
    inner_sum_ref[...] = jnp.zeros_like(inner_sum_ref)
    at_inner = part
    at_outer = part + inner_part
    at_cot = at_outer + inner_part

    def inner_chunk(index):
        pack = (own, other)[index * chunk // inner_part]
        start = at_inner + (index * chunk % inner_part) // chunk * width
        return pack[start : start + width, :]

    def outer_chunk(index):
        pack = (own, other)[index * chunk // inner_part]
        start = at_outer + index * chunk % inner_part
        return pack[start : start + chunk, :]

    head_dim = width // HEADS
    head = lax.broadcasted_iota(jnp.int32, (width, 128), 0) // head_dim
    lane = lax.broadcasted_iota(jnp.int32, (width, 128), 1)
    chooser = jnp.where(lane // 3 == head, -1.0, 0.0).astype(bf16)

    def add(row, values):
        sums_ref[row : row + 1, :] += jnp.sum(values, axis=0, keepdims=True)

    def one_tile(step, carry):
        place = pl.ds(pl.multiple_of(step * tile, tile), tile)
        context = context_ref[place, :]
        attended = dot_nn(context[:, :part], own[:part, :]) + dot_nn(
            context[:, part:], other[:part, :]
        )
        normed, unit_one, inverse_one = norm_rows(
            hidden_ref[place, :] + attended + biases[2:3, :], gains[0:1, :], biases[0:1, :]
        )
        normed_low = normed.astype(bf16)
        normed_ref[place, :] = normed_low
        for index in range(units // chunk):
            columns = slice(index * chunk, (index + 1) * chunk)
            bias = (small, small_other)[index * chunk // inner_part]
            start = index * chunk % inner_part
            preact = dot_nn(normed_low, inner_chunk(index)) + bias[2:3, start : start + chunk]
            phi = 0.5 + 0.5 * lax.erf(preact * inverse_root_two)
            active_ref[place, columns] = (preact * phi).astype(bf16)
            slope_ref[:, columns] = (
                phi + preact * jnp.exp2(preact * preact * (-0.5 * log2_e)) * inverse_root_tau
            ).astype(bf16)
        feed_out = dot_nn(active_ref[place, :inner_part], own[at_outer:at_cot, :]) + dot_nn(
            active_ref[place, inner_part:], other[at_outer:at_cot, :]
        )
        output, unit_two, inverse_two = norm_rows(
            normed + feed_out + biases[3:4, :], gains[1:2, :], biases[1:2, :]
        )
        index = lax.broadcasted_iota(jnp.int32, (tile, width), 0)

        @pl.when(step < tiles // 2)
        def _():
            output_ref[place, :] = output
        far = step - tiles // 2
        far_place = pl.ds(pl.multiple_of(jnp.maximum(far, 0) * tile, tile), tile)
        near_place = pl.ds(pl.multiple_of(jnp.minimum(step, tiles // 2 - 1) * tile, tile), tile)

        @pl.when(step >= tiles // 2)
        def _():
            output_send[far_place, :] = output
        cot = jnp.where(
            step < tiles // 2,
            cot_own[near_place, :],
            other[pl.ds(pl.multiple_of(at_cot + jnp.maximum(far, 0) * tile, 32), tile), :],
        ).astype(f32)
        first = jnp.where(
            step < tiles // 2,
            position * half + step * tile,
            (1 - position) * half + far * tile,
        )
        upstream = jnp.where(index + first < count, cot, 0.0)
        resid_two = norm_rows_back(upstream, unit_two, inverse_two, gains[1:2, :])
        feed_grad = resid_two.astype(bf16)
        feed_ref[place, :] = feed_grad
        for index in range(units // chunk):
            columns = slice(index * chunk, (index + 1) * chunk)
            grad = dot_nt(feed_grad, outer_chunk(index))
            preact_ref[place, columns] = (grad * slope_ref[:, columns].astype(f32)).astype(bf16)
        normed_grad = resid_two
        for index in range(units // chunk):
            columns = slice(index * chunk, (index + 1) * chunk)
            normed_grad = normed_grad + dot_nt(preact_ref[place, columns], inner_chunk(index))
        resid_one = norm_rows_back(normed_grad, unit_one, inverse_one, gains[0:1, :])
        resid_ref[place, :] = resid_one
        attend_grad = resid_one.astype(bf16)
        attend_ref[place, :] = attend_grad
        context_grad = jnp.concatenate(
            [dot_nt(attend_grad, own[:part, :]), dot_nt(attend_grad, other[:part, :])], axis=1
        ).astype(bf16)
        context_grad_ref[place, :] = context_grad
        high, low = split_two(context_grad.astype(f32) * context.astype(f32))
        delta = dot_nn(high, chooser) + dot_nn(low, chooser)
        delta_ref[place, :] = three_way(delta, lax.broadcasted_iota(jnp.int32, (tile, 128), 1))
        add(1, normed_grad * unit_one)
        add(2, upstream * unit_two)
        add(3, normed_grad)
        add(4, upstream)
        add(5, resid_one)
        add(6, resid_two)
        inner_sum_ref[0:1, :] += jnp.sum(preact_ref[place, :].astype(f32), axis=0, keepdims=True)
        return carry

    lax.fori_loop(0, tiles, one_tile, 0)
    grads_send[:inner_part, :] = dot_tn(active_ref[:, inner_part:], feed_ref[...]).astype(bf16)
    for index in range(inner_part // chunk):
        start = inner_part + index * chunk
        grads_send[inner_part + index * width : inner_part + (index + 1) * width, :] = dot_tn(
            normed_ref[...], preact_ref[:, start : start + chunk]
        ).astype(bf16)
    grads_send[2 * inner_part :, :] = dot_tn(context_ref[:, part:], attend_ref[...]).astype(bf16)


def attend_backward(
    facts, query_ref, key_ref, value_ref, lse_ref, context_grad_ref, delta_ref,
    token_ref, resid_ref, own, other, table, series_own, sums_ref, inner_sum_ref,
    attend_own, send, series_near, series_far, near_out, far_out,
    dquery_ref, dkey_ref, dvalue_ref,
):
    rows, width = query_ref.shape
    head_dim = width // HEADS
    half, history = series_own.shape
    part = width // 2
    position, count = lax.axis_index("mp"), facts[0:1, 0:1]
    lane = lax.broadcasted_iota(jnp.int32, (rows, 128), 1)
    dead = row_number(rows, position) >= count
    extra_query = jnp.where(lane == 127, jnp.ones((rows, 128), bf16), three_way(-lse_ref[...], lane))
    extra_key = jnp.where((lane == 127) & dead, -1e30, 0.0)
    extra_grad = delta_ref[...]

    def pair(index, carry):
        columns = pl.ds(pl.multiple_of(index * 128, 128), 128)
        queries = query_ref[:, columns]
        keys = key_ref[:, columns]
        values = value_ref[:, columns]
        grads = context_grad_ref[:, columns]
        dquery = dkey = dvalue = None
        for side in range(2):
            mine = (lane >= head_dim) if side else (lane < head_dim)
            hot = lane // 3 == index * 2 + side
            nothing = jnp.zeros_like(queries)
            query = jnp.where(mine, queries, nothing)
            grad = jnp.where(mine, grads, nothing)
            key = jnp.where(mine, keys, nothing)
            soft = jnp.exp2(
                dot_nt(
                    jnp.concatenate([keys, jnp.where(hot, 1.0, extra_key).astype(bf16)], axis=1),
                    jnp.concatenate([query, extra_query], axis=1),
                )
            )
            centered = dot_nt(
                jnp.concatenate([values, jnp.where(hot, 1.0, 0.0).astype(bf16)], axis=1),
                jnp.concatenate([grad, extra_grad], axis=1),
            )
            score_grad = (soft * centered).astype(bf16)
            one = dot_nn(soft.astype(bf16), grad)
            two = dot_nn(score_grad, query)
            three = dot_tn(key, score_grad)
            dvalue = one if dvalue is None else dvalue + one
            dkey = two if dkey is None else dkey + two
            dquery = three if dquery is None else dquery + three
        dvalue_ref[:, columns] = dvalue.astype(bf16)
        dkey_ref[:, columns] = (dkey * ln_two).astype(bf16)
        dquery_ref[:, columns] = (dquery.T * head_dim**-0.5).astype(bf16)
        return carry

    lax.fori_loop(0, width // 128, pair, 0)

    tokens = token_ref[...]
    total = resid_ref[...]
    near_out[...] = jnp.zeros_like(near_out)
    far_out[...] = jnp.zeros_like(far_out)
    for kind, grad_ref in enumerate((dquery_ref, dkey_ref, dvalue_ref)):
        low = grad_ref[...]
        attend_own[kind] = dot_tn(tokens, low[:, :part])
        far = dot_tn(tokens, low[:, part:]).astype(bf16)
        send[kind * part : (kind + 1) * part, :part] = far[:part]
        send[kind * part : (kind + 1) * part, part:] = far[part:]
        total = (
            total
            + dot_nt(low[:, :part], attend_block(own, half, kind))
            + dot_nt(low[:, part:], attend_block(other, half, kind))
        )
        if kind != 1:
            column = jnp.sum(low.astype(f32), axis=0, keepdims=True)
            start = kind // 2 * part
            near_out[7:8, start : start + part] = column[:, :part]
            far_out[7:8, start : start + part] = column[:, part:]
    low = total.astype(bf16)
    series_near[...] = dot_nt(low[:half], table[...])
    series_far[...] = dot_nt(low[half:], table[...])
    table_grad = dot_tn(series_own[...], low[:half]) + dot_tn(other[:half, :history], low[half:])
    row = lax.broadcasted_iota(jnp.int32, table_grad.shape, 0)
    seen = row >= facts[1:2, 0:1]
    send[3 * part :, :] = jnp.where(seen, table_grad, 0.0).astype(bf16)
    shared = sums_ref[0:7, :]
    bias_grad = jnp.sum(low.astype(f32), axis=0, keepdims=True)
    near_out[0:7, :] = shared
    far_out[0:7, :] = shared
    near_out[0:1, :] = bias_grad
    far_out[0:1, :] = bias_grad
    count_near = inner_sum_ref.shape[1] // 2 // width
    for index in range(count_near):
        near_out[8 + index : 9 + index, :] = inner_sum_ref[0:1, index * width : (index + 1) * width]
        far_out[8 + index : 9 + index, :] = inner_sum_ref[
            0:1, (count_near + index) * width : (count_near + index + 1) * width
        ]


def left_product(start, matrix):
    start_high, start_low = split_two(start)
    high, low = split_two(matrix)
    both = dot_nt(jnp.concatenate([start_high, start_low], axis=0), high)
    return both[:8] + both[8:] + dot_nt(start_high, low)


def right_product(basis, matrix):
    basis_high, basis_low = split_two(basis)
    high, low = split_two(matrix)
    both = dot_nn(jnp.concatenate([basis_high, basis_low], axis=0), high)
    return both[:8] + both[8:] + dot_nn(basis_high, low)


def feed_matrices(
    active_ref, preact_ref, normed_ref, feed_ref, context_ref, attend_ref, received,
    e_outer, e_inner, e_mixer, s_outer, s_inner, s_mixer, output_near, output_far,
    outer, inner, mixer, left, output,
):
    width = feed_ref.shape[1]
    inner_part = outer.shape[0]
    part = mixer.shape[0]
    chunk = 512
    join_pair(output_near, output_far, output)
    outer[...] = (
        dot_tn(active_ref[:, :inner_part], feed_ref[...])
        + received[:inner_part, :].astype(f32)
        + e_outer[...]
    )
    for index in range(inner_part // chunk):
        columns = slice(index * chunk, (index + 1) * chunk)
        start = inner_part + index * width
        inner[:, columns] = (
            dot_tn(normed_ref[...], preact_ref[:, columns])
            + received[start : start + width, :].astype(f32)
            + e_inner[:, columns]
        )
    mixer[...] = (
        dot_tn(context_ref[:, :part], attend_ref[...])
        + received[2 * inner_part :, :].astype(f32)
        + e_mixer[...]
    )
    left[:, 0:1024] = left_product(s_outer[...], outer[...])
    left[:, 1024:1536] = left_product(s_inner[...], inner[...])
    left[:, 1536:1792] = left_product(s_mixer[...], mixer[...])


def orthonormal_rows(vectors):
    rank = vectors.shape[0]
    row = lax.broadcasted_iota(jnp.int32, vectors.shape, 0)
    for index in range(rank):
        pivot = vectors[index : index + 1, :]
        inner = jnp.sum(vectors * pivot, axis=1, keepdims=True)
        size = inner[index : index + 1, :] + 1e-12
        reduced = vectors - pivot * (inner / size)
        vectors = jnp.where(
            row > index, reduced, jnp.where(row == index, vectors * lax.rsqrt(size), vectors)
        )
    return vectors


def reduce_factors(
    replicas, facts, near_attend, own, received, e_attend, e_embed, s_attend, s_embed, left_part,
    near, far, outer, inner, mixer,
    left_ref, right_ref, mean_ref, attend, embed,
    start_ref, summed, partial, gathered, parts_one, parts_two, send_sems, recv_sems,
):
    me = lax.axis_index("dp")
    barrier = pltpu.get_barrier_semaphore()
    chunk = start_ref.shape[1] // replicas
    share = 1.0 / replicas

    def peer(offset):
        return lax.rem(me + offset, replicas)

    def columns(index):
        return pl.ds(pl.multiple_of(index * chunk, 128), chunk)

    def each(what):
        def body(offset, carry):
            what(offset)
            return carry

        lax.fori_loop(1, replicas, body, 0)

    each(
        lambda offset: pl.semaphore_signal(
            barrier, inc=1, device_id={"dp": peer(offset)}, device_id_type=pl.DeviceIdType.MESH
        )
    )
    part = near_attend.shape[2]
    total = None
    for kind in range(3):
        rows = slice(kind * part, (kind + 1) * part)
        block = jnp.concatenate([received[rows, :part], received[rows, part:]], axis=0)
        attend[kind] = near_attend[kind] + block.astype(f32) + e_attend[kind]
        term = left_product(s_attend[kind], attend[kind])
        total = term if total is None else total + term
    mine, theirs = facts[2:3, 0:1], facts[3:4, 0:1]
    table_near = own[3 * part :, :].astype(f32)
    table_far = received[3 * part :, :].astype(f32)
    pieces = []
    for group in range(embed.shape[0]):
        grad = jnp.where(mine == group, table_near, 0.0) + jnp.where(theirs == group, table_far, 0.0)
        embed[group] = grad + e_embed[group]
        pieces.append(left_product(s_embed[...], embed[group]))
    used = embed.shape[0] * embed.shape[1]
    start_ref[:, 0:1024] = jnp.concatenate(pieces + [jnp.zeros((8, 1024 - used), f32)], axis=1)
    start_ref[:, 1024:2048] = left_part[:, 0:1024]
    start_ref[:, 2048:2560] = total
    start_ref[:, 2560:3328] = left_part[:, 1024:1792]
    common = near[1:7, :] + far[1:7, :]
    row = lax.broadcasted_iota(jnp.int32, (3, near.shape[1]), 0)
    bias = jnp.where(row == mine, near[0:1, :], 0.0) + jnp.where(row == theirs, far[0:1, :], 0.0)
    start_ref[:, 3328:3840] = jnp.concatenate([bias, common[:5]], axis=0)
    rest = jnp.concatenate([common[5:6], near[7:10, :] + far[7:10, :]], axis=0)
    for row in range(4):
        start_ref[2 * row : 2 * row + 1, 3840:4096] = rest[row : row + 1, :256]
        start_ref[2 * row + 1 : 2 * row + 2, 3840:4096] = rest[row : row + 1, 256:]
    if start_ref.shape[1] > 4096:
        start_ref[:, 4096:] = jnp.zeros((8, start_ref.shape[1] - 4096), f32)
    pl.semaphore_wait(barrier, replicas - 1)

    def all_sum(phase, source, parts, result):
        def scatter(offset):
            other = peer(offset)
            return pltpu.make_async_remote_copy(
                src_ref=source.at[:, columns(other)],
                dst_ref=parts.at[offset],
                send_sem=send_sems.at[2 * phase, offset],
                recv_sem=recv_sems.at[2 * phase, offset],
                device_id={"dp": other},
                device_id_type=pl.DeviceIdType.MESH,
            )

        def spread(offset, owner):
            return pltpu.make_async_remote_copy(
                src_ref=result.at[:, columns(owner)],
                dst_ref=result.at[:, columns(owner)],
                send_sem=send_sems.at[2 * phase + 1, offset],
                recv_sem=recv_sems.at[2 * phase + 1, offset],
                device_id={"dp": peer(offset)},
                device_id_type=pl.DeviceIdType.MESH,
            )

        each(lambda offset: scatter(offset).start())

        def collect(offset, total):
            scatter(offset).wait_recv()
            return total + parts[offset]

        total = lax.fori_loop(1, replicas, collect, source[:, columns(me)])
        result[:, columns(me)] = total * share
        each(lambda offset: spread(offset, me).start())
        each(lambda offset: spread(offset, lax.rem(me - offset + replicas, replicas)).wait_recv())
        each(lambda offset: scatter(offset).wait_send())
        each(lambda offset: spread(offset, me).wait_send())

    all_sum(0, start_ref, parts_one, summed)
    mean_ref[...] = summed[:, 3328:4096]
    bases = []
    for start, size in ((0, 1024), (1024, 1024), (2048, 512), (2560, 512), (3072, 256)):
        basis = orthonormal_rows(summed[:, start : start + size])
        left_ref[:, start : start + size] = basis
        bases.append(basis)
    height = embed.shape[1]
    total = None
    for group in range(embed.shape[0]):
        term = right_product(bases[0][:, group * height : (group + 1) * height], embed[group])
        total = term if total is None else total + term
    partial[:, 0:512] = total
    partial[:, 512:1024] = right_product(bases[1], outer[...])
    for kind in range(3):
        partial[:, 1024 + kind * 256 : 1280 + kind * 256] = right_product(bases[2], attend[kind])
    partial[:, 1792:2816] = right_product(bases[3], inner[...])
    partial[:, 2816:3328] = right_product(bases[4], mixer[...])
    partial[:, 3328:] = jnp.zeros((8, partial.shape[1] - 3328), f32)
    all_sum(1, partial, parts_two, gathered)
    right_ref[...] = gathered[:, :3328]


def renew_all(
    step_rate, mixer_rate, left, right, mean, series_near, series_far, *refs,
):
    matrices, weights, moments = refs[0:5], refs[5:10], refs[10:15]
    vectors, vector_moments = refs[15:20], refs[20:25]
    errors, new_weights, new_moments = refs[25:30], refs[30:35], refs[35:40]
    new_vectors, new_vector_moments = refs[40:45], refs[45:50]
    lefts, rights, series_grad = refs[50:55], refs[55:60], refs[60]
    step = pl.program_id(0)
    join_pair(series_near, series_far, series_grad)

    def approx(basis, factor):
        left_high, left_low = split_two(basis)
        right_high, right_low = split_two(factor)
        return dot_tn(
            jnp.concatenate([left_high, left_low, left_high, left_low], axis=0),
            jnp.concatenate([right_high, right_high, right_low, right_low], axis=0),
        )

    def write(index, where, update, rate):
        errors[index][where] = matrices[index][where] - update
        moment = momentum_decay * moments[index][where] + update
        new_moments[index][where] = moment
        new_weights[index][where] = weights[index][where] - rate * moment

    def cut(start, size):
        return pl.ds(pl.multiple_of(start + step * size, 128), size)

    every = (slice(None), slice(None))
    groups, height, block = matrices[0].shape
    factor = right[:, cut(0, block)]
    for group in range(groups):
        write(
            0, (group, slice(None), slice(None)),
            approx(left[:, group * height : (group + 1) * height], factor), step_rate,
        )
    write(1, every, approx(left[:, cut(1024, matrices[1].shape[0])], right[:, 512:1024]), step_rate)
    basis = left[:, cut(2048, matrices[2].shape[1])]
    for kind in range(3):
        write(
            2, (kind, slice(None), slice(None)),
            approx(basis, right[:, 1024 + kind * 256 : 1280 + kind * 256]), step_rate,
        )
    write(3, every, approx(left[:, cut(2560, matrices[3].shape[0])], right[:, 1792:2816]), step_rate)
    write(4, every, approx(left[:, 3072:3328], right[:, cut(2816, matrices[4].shape[1])]), mixer_rate)

    @pl.when(step == 0)
    def _():
        for group in range(groups):
            lefts[0][group] = left[:, group * height : (group + 1) * height]
        lefts[1][...] = left[:, 1024:2048]
        lefts[2][...] = left[:, 2048:2560]
        lefts[3][...] = left[:, 2560:3072]
        lefts[4][...] = left[:, 3072:3328]
        rights[0][...] = right[:, 0:512]
        rights[1][...] = right[:, 512:1024]
        for kind in range(3):
            rights[2][kind] = right[:, 1024 + kind * 256 : 1280 + kind * 256]
        rights[3][...] = right[:, 1792:2816]
        rights[4][...] = right[:, 2816:3328]

        def renew(index, rows, columns, gradient):
            moment = momentum_decay * vector_moments[index][rows, columns] + gradient
            new_vector_moments[index][rows, columns] = moment
            new_vectors[index][rows, columns] = vectors[index][rows, columns] - step_rate * moment

        renew(0, slice(0, 3), slice(None), mean[0:3, :512])
        renew(1, slice(0, 2), slice(None), mean[3:5, :512])
        renew(2, slice(0, 3), slice(None), mean[5:8, :512])
        renew(2, slice(3, 4), slice(0, 256), mean[0:1, 512:])
        renew(2, slice(3, 4), slice(256, 512), mean[1:2, 512:])
        renew(3, slice(0, 1), slice(None), mean[2:3, 512:])
        renew(3, slice(1, 2), slice(None), mean[3:4, 512:])
        for index in range(4):
            renew(
                4, slice(0, 1), slice(index * 256, (index + 1) * 256),
                mean[4 + index : 5 + index, 512:],
            )


def call(kernel, outs, args, *, cost, in_specs=None, scratch=(), limit=32, name=None):
    return pl.pallas_call(
        kernel,
        out_shape=outs,
        in_specs=in_specs if in_specs is not None else [VM] * len(args),
        out_specs=jax.tree.map(lambda _: VM, outs),
        scratch_shapes=list(scratch),
        compiler_params=pltpu.CompilerParams(vmem_limit_bytes=limit * MIB),
        cost_estimate=estimate(cost),
        name=name,
    )(*args)


def estimate(microseconds):
    return pl.CostEstimate(
        flops=int(microseconds * 1e9), bytes_accessed=int(microseconds * 2e6), transcendentals=0
    )


def sds(shape, dtype=f32):
    return jax.ShapeDtypeStruct(shape, dtype)


def local(
    series, groups, counts, cotangent,
    embed_weight, embed_moment, embed_error, embed_start,
    attend_weight, attend_moment, attend_error, attend_start,
    mixer_weight, mixer_moment, mixer_error, mixer_start,
    inner_weight, inner_moment, inner_error, inner_start,
    outer_weight, outer_moment, outer_error, outer_start,
    embed_bias, embed_bias_moment, query_bias, query_bias_moment,
    inner_bias, inner_bias_moment, norm_gains, gains_moment, shared_biases, biases_moment,
):
    replicas = lax.axis_size("dp")
    half, windows, history = series.shape
    rows = 2 * half
    group_count, _, width = embed_weight.shape
    part = attend_weight.shape[2]
    inner_part = inner_weight.shape[1]
    units = 2 * inner_part
    turned = lambda a: a.transpose(1, 0, 2)

    def swap(values):
        return lax.ppermute(values, "mp", [(0, 1), (1, 0)])

    low = sds((rows, width), bf16)
    full = sds((rows, width))
    near = sds((half, width))
    packed = sds((half + 3 * part + 16, width), bf16)
    send_one, other_one, series_own, small, facts, send_two, cot_own = pl.pallas_call(
        prepare,
        out_shape=[
            packed, packed, sds((half, history), bf16), sds((8, inner_part)), sds((8, 128), jnp.int32),
            sds((part + 2 * inner_part + half, width), bf16), sds((half, width), bf16),
        ],
        in_specs=[HB] * 10,
        out_specs=[VM] * 7,
        scratch_shapes=[
            pltpu.SMEM(groups.shape, jnp.int32), pltpu.SMEM(counts.shape, jnp.int32),
            pltpu.VMEM(series.shape, bf16), pltpu.VMEM((3, width, part), f32),
            pltpu.VMEM(query_bias.shape, f32), pltpu.VMEM((1, inner_part), f32),
            pltpu.VMEM(cotangent.shape, bf16), pltpu.VMEM(mixer_weight.shape, f32),
            pltpu.VMEM(inner_weight.shape, f32), pltpu.VMEM(outer_weight.shape, f32),
            pltpu.SemaphoreType.DMA((10,)), pltpu.SemaphoreType.DMA((2,)), pltpu.SemaphoreType.DMA((2,)),
        ],
        compiler_params=pltpu.CompilerParams(
            collective_id=2, has_side_effects=True, vmem_limit_bytes=LIMITS[0] * MIB
        ),
        cost_estimate=estimate(7),
        name="prepare",
    )(
        *(
            pltpu.with_memory_space_constraint(a, pltpu.HBM)
            for a in (
                groups, counts, series, turned(attend_weight), query_bias, inner_bias[None],
                cotangent, mixer_weight, inner_weight, outer_weight,
            )
        )
    )
    other_two = swap(send_two)
    hidden, tokens, queries, keys, values, context, lse, small_other, table = call(
        attend_forward,
        [full, low, low, low, low, low, sds((rows, 128)), sds((8, inner_part)), sds((history, width), bf16)],
        (facts, series_own, embed_weight, embed_bias, send_one, other_one, small),
        limit=LIMITS[2], cost=15,
        name="attend_forward",
    )
    (
        output_near, output_send, active, preact_grad, normed_low, feed_grad, attend_out, resid_one,
        context_grad, delta, sums, inner_sums, grads_send,
    ) = call(
        functools.partial(feed_forward, TILES),
        [near, near, sds((rows, units), bf16), sds((rows, units), bf16), low, low, low, full, low,
         sds((rows, 128), bf16), sds((8, width)), sds((8, units)),
         sds((2 * inner_part + part, width), bf16)],
        (facts, context, hidden, send_two, other_two, small, small_other, norm_gains, shared_biases, cot_own),
        limit=LIMITS[3], cost=22,
        scratch=[pltpu.VMEM((rows // TILES, units), bf16)],
        name="feed_forward",
    )
    output_other = swap(output_send)
    grads_other = swap(grads_send)
    attend_near, send_three, series_near, series_far, sums_near, sums_far = call(
        attend_backward,
        [sds((3, width, part)), sds((3 * part + history, width), bf16), sds((half, history)),
         sds((half, history)), sds((16, width)), sds((16, width))],
        (facts, queries, keys, values, lse, context_grad, delta, tokens, resid_one, send_one,
         other_one, table, series_own, sums, inner_sums),
        limit=LIMITS[4], cost=22,
        scratch=[pltpu.VMEM((rows, width), bf16)] * 3,
        name="attend_backward",
    )
    other_three = swap(send_three)
    series_other = swap(series_far)
    sums_other = swap(sums_far)
    outer_matrix, inner_matrix, mixer_matrix, left_part, output = call(
        feed_matrices,
        [sds(outer_weight.shape), sds(inner_weight.shape), sds(mixer_weight.shape), sds((8, 1792)),
         sds((half, windows, width))],
        (active, preact_grad, normed_low, feed_grad, context, attend_out, grads_other,
         outer_error[0], inner_error[0], mixer_error[0], outer_start[0].T, inner_start.T, mixer_start[0].T,
         output_near, output_other),
        limit=LIMITS[5], cost=6,
        name="feed_matrices",
    )
    padded = max(128, -(-4096 // replicas // 128) * 128)
    total = padded * replicas
    left, right, mean, attend_matrix, embed_matrix = pl.pallas_call(
        functools.partial(reduce_factors, replicas),
        out_shape=[sds((8, 3328)), sds((8, 3328)), sds((8, 768)), sds((3, width, part)), sds(embed_weight.shape)],
        in_specs=[VM] * 14,
        out_specs=[VM] * 5,
        scratch_shapes=[
            pltpu.VMEM((8, total), f32), pltpu.VMEM((8, total), f32), pltpu.VMEM((8, total), f32),
            pltpu.VMEM((8, total), f32),
            pltpu.VMEM((replicas, 8, padded), f32), pltpu.VMEM((replicas, 8, padded), f32),
            pltpu.SemaphoreType.DMA((4, replicas)), pltpu.SemaphoreType.DMA((4, replicas)),
        ],
        compiler_params=pltpu.CompilerParams(
            collective_id=1, has_side_effects=True, vmem_limit_bytes=LIMITS[6] * MIB
        ),
        cost_estimate=estimate(30),
        name="reduce_factors",
    )(
        facts, attend_near, send_three, other_three, turned(attend_error[0]), embed_error[0],
        attend_start.transpose(0, 2, 1), embed_start.T, left_part, sums_near, sums_other,
        outer_matrix, inner_matrix, mixer_matrix,
    )
    matrices = (embed_matrix, outer_matrix, attend_matrix, inner_matrix, mixer_matrix)

    step_rate = base_rate * math.sqrt(replicas * 7 / (windows * rows))
    mixer_rate = step_rate * math.sqrt(width / max(width * 16 // rows, 1))
    steps = 4
    whole = lambda a: pl.BlockSpec(a.shape, lambda i: (0,) * len(a.shape))
    column = lambda a: pl.BlockSpec((a.shape[0], a.shape[1] // steps), lambda i: (0, i))
    row = lambda a: pl.BlockSpec((a.shape[0] // steps, a.shape[1]), lambda i: (i, 0))
    middle = lambda a: pl.BlockSpec((a.shape[0], a.shape[1] // steps, a.shape[2]), lambda i: (0, i, 0))
    last = lambda a: pl.BlockSpec((a.shape[0], a.shape[1], a.shape[2] // steps), lambda i: (0, 0, i))
    specs = [spec(a) for spec, a in zip((last, row, middle, row, column), matrices)]
    vectors = (embed_bias, norm_gains, shared_biases, query_bias, inner_bias[None])
    vector_moments = (
        embed_bias_moment, gains_moment, biases_moment, query_bias_moment, inner_bias_moment[None]
    )
    vector_specs = [whole(a) for a in vectors]
    split = pl.BlockSpec((half // steps, history), lambda i: (i, 0))
    split_out = pl.BlockSpec((half // steps, windows, history), lambda i: (i, 0, 0))
    factors = [
        sds((group_count, 8, history)), sds((8, 1024)), sds((8, 512)), sds((8, 512)), sds((8, 256)),
        sds((8, 512)), sds((8, 512)), sds((3, 8, part)), sds((8, 1024)), sds((8, 512)),
    ]
    found = pl.pallas_call(
        functools.partial(renew_all, step_rate, mixer_rate),
        grid=(steps,),
        out_shape=[sds(a.shape) for a in matrices] * 3 + [sds(a.shape) for a in vectors] * 2
        + factors + [sds(series.shape)],
        in_specs=[whole(left), whole(right), whole(mean), split, split] + specs * 3 + vector_specs * 2,
        out_specs=specs * 3 + vector_specs * 2 + [whole(a) for a in factors] + [split_out],
        compiler_params=pltpu.CompilerParams(vmem_limit_bytes=LIMITS[7] * MIB),
        cost_estimate=estimate(12),
        name="renew_all",
    )(
        left, right, mean, series_near, series_other, *matrices,
        embed_weight, outer_weight, turned(attend_weight), inner_weight, mixer_weight,
        embed_moment, outer_moment, turned(attend_moment), inner_moment, mixer_moment,
        *vectors, *vector_moments,
    )
    errors, weights, moments = found[0:5], found[5:10], found[10:15]
    new_vectors, new_vector_moments = found[15:20], found[20:25]
    lefts, rights = found[25:30], found[30:35]
    return (
        output,
        found[35],
        weights[0],
        moments[0],
        errors[0][None],
        lefts[0].transpose(0, 2, 1),
        rights[0].T,
        turned(weights[2]),
        turned(moments[2]),
        turned(errors[2])[None],
        lefts[2].T[None],
        rights[2].transpose(0, 2, 1),
        weights[4],
        moments[4],
        errors[4][None],
        lefts[4].T,
        rights[4].T[None],
        weights[3],
        moments[3],
        errors[3][None],
        lefts[3].T[None],
        rights[3].T,
        weights[1],
        moments[1],
        errors[1][None],
        lefts[1].T,
        rights[1].T[None],
        new_vector_moments[0],
        new_vectors[0],
        new_vector_moments[3],
        new_vectors[3],
        new_vector_moments[4][0],
        new_vectors[4][0],
        new_vector_moments[1],
        new_vectors[1],
        new_vector_moments[2],
        new_vectors[2],
    )


def solution(mesh):
    return jax.shard_map(
        local,
        mesh=mesh,
        in_specs=(
            P("mp", "dp", None),
            P("dp"),
            P("dp"),
            P("mp", "dp", None),
            P(),
            P(),
            P("dp", None, None, None),
            P(),
            P(None, None, "mp"),
            P(None, None, "mp"),
            P("dp", None, None, "mp"),
            P(None, "mp", None),
            P("mp", None),
            P("mp", None),
            P("dp", "mp", None),
            P("mp", None, None),
            P(None, "mp"),
            P(None, "mp"),
            P("dp", None, "mp"),
            P("mp", None),
            P("mp", None),
            P("mp", None),
            P("dp", "mp", None),
            P("mp", None, None),
            P(),
            P(),
            P(None, "mp"),
            P(None, "mp"),
            P("mp"),
            P("mp"),
            P(),
            P(),
            P(),
            P(),
        ),
        out_specs=(
            P("mp", "dp", None),
            P("mp", "dp", None),
            P(),
            P(),
            P("dp", None, None, None),
            P(),
            P(),
            P(None, None, "mp"),
            P(None, None, "mp"),
            P("dp", None, None, "mp"),
            P("mp", None, None),
            P(None, "mp", None),
            P("mp", None),
            P("mp", None),
            P("dp", "mp", None),
            P("mp", None),
            P("mp", None, None),
            P(None, "mp"),
            P(None, "mp"),
            P("dp", None, "mp"),
            P("mp", None, None),
            P("mp", None),
            P("mp", None),
            P("mp", None),
            P("dp", "mp", None),
            P("mp", None),
            P("mp", None, None),
            P(),
            P(),
            P(None, "mp"),
            P(None, "mp"),
            P("mp"),
            P("mp"),
            P(),
            P(),
            P(),
            P(),
        ),
        check_vma=False,
    )
```

```python
import functools
import math

import jax
import jax.numpy as jnp
from jax import lax
from jax.experimental import pallas as pl
from jax.experimental.pallas import tpu as pltpu
from jax.sharding import PartitionSpec as P

HEADS = 8
momentum_decay = 0.9
norm_epsilon = 1e-05
base_rate = 0.03
inverse_root_two = 0.7071067811865476
inverse_root_tau = 0.3989422804014327
log2_e = 1.4426950408889634
ln_two = 0.6931471805599453
f32 = jnp.float32
bf16 = jnp.bfloat16
VMEM = pltpu.VMEM
VM = pl.BlockSpec(memory_space=pltpu.VMEM)
HB = pl.BlockSpec(memory_space=pltpu.HBM)
MIB = 1024 * 1024


def dot_nn(a, b):
    return lax.dot_general(a, b, (((1,), (0,)), ((), ())), preferred_element_type=f32)


def dot_nt(a, b):
    return lax.dot_general(a, b, (((1,), (1,)), ((), ())), preferred_element_type=f32)


def dot_tn(a, b):
    return lax.dot_general(a, b, (((0,), (0,)), ((), ())), preferred_element_type=f32)


def split_two(x):
    high = x.astype(bf16)
    return high, (x - high.astype(f32)).astype(bf16)


def three_way(x, lane):
    high = x.astype(bf16).astype(f32)
    rest = x - high
    middle = rest.astype(bf16).astype(f32)
    last = rest - middle
    place = lax.rem(lax.rem(lane, 64), 3)
    return jnp.where(place == 0, high, jnp.where(place == 1, middle, last)).astype(bf16)


LIMITS = (12, 14, 12, 14, 16, 8, 8, 28)
TILES = 2


def row_number(rows, position):
    half = rows // 2
    index = lax.broadcasted_iota(jnp.int32, (rows, 128), 0)
    return jnp.where(index < half, index + position * half, index - half + (1 - position) * half)


def lookback_of(group, history):
    return jnp.where(
        group == 0, history * 2 // 7, jnp.where(group == 1, history * 4 // 7, history)
    ).astype(jnp.int32)


def split_pair(pair_ref, mine, theirs, columns):
    position = lax.axis_index("mp")

    @pl.when(position == 0)
    def _():
        mine[:, columns] = pair_ref[:, 0, :]
        theirs[:, columns] = pair_ref[:, 1, :]

    @pl.when(position != 0)
    def _():
        mine[:, columns] = pair_ref[:, 1, :]
        theirs[:, columns] = pair_ref[:, 0, :]


def join_pair(mine, theirs, pair_ref):
    position = lax.axis_index("mp")

    @pl.when(position == 0)
    def _():
        pair_ref[:, 0, :] = mine[...]
        pair_ref[:, 1, :] = theirs[...]

    @pl.when(position != 0)
    def _():
        pair_ref[:, 1, :] = mine[...]
        pair_ref[:, 0, :] = theirs[...]


def three_parts(x):
    high = x.astype(bf16)
    rest = x - high.astype(f32)
    middle = rest.astype(bf16)
    return high, middle, (rest - middle.astype(f32)).astype(bf16)


def prepare(
    groups_hbm, counts_hbm, series_hbm, attend_hbm, query_bias_hbm, inner_bias_hbm,
    cot_hbm, mixer_hbm, inner_hbm, outer_hbm,
    send, received, series_own, small, facts, send_feed, cot_own,
    groups, counts, series, attend, query_bias, inner_bias, cotangent, mixer, inner, outer,
    done, send_sems, recv_sems,
):
    position = lax.axis_index("mp")
    partner = {"mp": 1 - position}
    barrier = pltpu.get_barrier_semaphore()
    pl.semaphore_signal(barrier, inc=1, device_id=partner, device_id_type=pl.DeviceIdType.MESH)
    copies = []
    for source, target in (
        (query_bias_hbm, query_bias), (inner_bias_hbm, inner_bias), (attend_hbm, attend),
        (series_hbm, series), (groups_hbm, groups), (counts_hbm, counts), (cot_hbm, cotangent),
        (mixer_hbm, mixer), (inner_hbm, inner), (outer_hbm, outer),
    ):
        copies.append(pltpu.make_async_copy(source, target, done.at[len(copies)]))
        copies[-1].start()
    half, _, history = series.shape
    width = send.shape[1]
    depth = attend.shape[1] // 2
    end = half + 3 * depth
    part = query_bias.shape[1]
    trades = [
        pltpu.make_async_remote_copy(
            src_ref=send.at[rows], dst_ref=received.at[rows], send_sem=send_sems.at[index],
            recv_sem=recv_sems.at[index], device_id=partner, device_id_type=pl.DeviceIdType.MESH,
        )
        for index, rows in enumerate((slice(half, end + 16), slice(0, half)))
    ]
    copies[0].wait()
    copies[1].wait()
    small[...] = jnp.zeros_like(small)
    small[0:2, :part] = query_bias[...]
    small[2:3, :] = inner_bias[...]
    values = jnp.concatenate(
        [
            jnp.concatenate([query_bias[0:1, :], query_bias[1:2, :]], axis=1),
            inner_bias[:, :width],
            inner_bias[:, width:],
            jnp.zeros((1, width), f32),
        ],
        axis=0,
    )
    send[end : end + 16, :] = jnp.concatenate(
        [*three_parts(values), jnp.zeros((4, width), bf16)], axis=0
    )
    copies[2].wait()
    for kind in range(3):
        rows = slice(half + kind * depth, half + (kind + 1) * depth)
        send[rows, :256] = attend[kind, :depth, :].astype(bf16)
        send[rows, 256:] = attend[kind, depth:, :].astype(bf16)
    pl.semaphore_wait(barrier, 1)
    trades[0].start()
    send[:half, 256:] = jnp.zeros((half, width - 256), bf16)
    copies[3].wait()
    split_pair(series, series_own, send.at[:half], slice(0, history))
    trades[1].start()
    copies[4].wait()
    copies[5].wait()
    group = jnp.where(position == 0, groups[0], groups[1])
    other_group = jnp.where(position == 0, groups[1], groups[0])
    count = jnp.where(position == 0, counts[0], counts[1])
    first = history - lookback_of(group, history)
    row = lax.broadcasted_iota(jnp.int32, facts.shape, 0)
    facts[...] = jnp.where(
        row == 0, count, jnp.where(row == 1, first, jnp.where(row == 2, group, other_group))
    )
    m, d, o = mixer.shape[0], inner.shape[0], outer.shape[0]
    copies[6].wait()
    split_pair(cotangent, cot_own, send_feed.at[m + 2 * d + o :], slice(None))
    copies[7].wait()
    send_feed[:m] = mixer[...].astype(bf16)
    copies[8].wait()
    send_feed[m : m + d] = inner[:, :512].astype(bf16)
    send_feed[m + d : m + 2 * d] = inner[:, 512:].astype(bf16)
    copies[9].wait()
    send_feed[m + 2 * d : m + 2 * d + o] = outer[...].astype(bf16)
    for trade in trades:
        trade.wait()


def unpack_small(other, small_other):
    part = other.shape[1] // 2
    parts = other[other.shape[0] - 16 :, :].astype(f32)
    values = parts[0:4] + parts[4:8] + parts[8:12]
    small_other[0:1, :part] = values[0:1, :part]
    small_other[1:2, :part] = values[0:1, part:]
    small_other[2:3, : 2 * part] = values[1:2, :]
    small_other[2:3, 2 * part :] = values[2:3, :]


def attend_block(pack, half, kind):
    start = half + kind * 256
    return jnp.concatenate([pack[start : start + 256, :256], pack[start : start + 256, 256:]], axis=0)


def attend_forward(
    facts, series_own, embed, embed_bias, own, other, small,
    hidden_ref, token_ref, query_ref, key_ref, value_ref, context_ref, lse_ref, small_other, table,
):
    unpack_small(other, small_other)
    chosen, bias_row = embed[0], embed_bias[0:1, :]
    for group in range(1, embed.shape[0]):
        here = facts[2:3, 0:1] == group
        chosen = jnp.where(here, embed[group], chosen)
        bias_row = jnp.where(here, embed_bias[group : group + 1, :], bias_row)
    row = lax.broadcasted_iota(jnp.int32, chosen.shape, 0)
    table[...] = jnp.where(row >= facts[1:2, 0:1], chosen, 0.0).astype(bf16)
    rows, width = hidden_ref.shape
    half, history = series_own.shape
    part = width // 2
    head_dim = width // HEADS
    position, count = lax.axis_index("mp"), facts[0:1, 0:1]
    for index, block in enumerate((series_own[...], other[:half, :history])):
        values = dot_nn(block, table[...]) + bias_row
        hidden_ref[pl.ds(index * half, half), :] = values
        token_ref[pl.ds(index * half, half), :] = values.astype(bf16)
    scale = head_dim**-0.5 * log2_e
    tokens = token_ref[...]
    for index, (pack, bias) in enumerate(((own, small), (other, small_other))):
        columns = pl.ds(index * part, part)
        query_ref[:, columns] = (
            (dot_nn(tokens, attend_block(pack, half, 0)) + bias[0:1, :part]) * scale
        ).astype(bf16)
        key_ref[:, columns] = dot_nn(tokens, attend_block(pack, half, 1)).astype(bf16)
        value_ref[:, columns] = (
            dot_nn(tokens, attend_block(pack, half, 2)) + bias[1:2, :part]
        ).astype(bf16)
    lane = lax.broadcasted_iota(jnp.int32, (rows, 128), 1)
    dead = row_number(rows, position) >= count
    last = lax.rem(lane, 64) == 63
    extra_query = jnp.where(last, 1.0, 0.0).astype(bf16)
    extra_key = jnp.where(last & dead, -1e30, 0.0).astype(bf16)
    ones = jnp.ones((rows, 128), bf16)

    def heads(shifted):
        def pair(index, carry):
            columns = pl.ds(pl.multiple_of(index * 128, 128), 128)
            queries = query_ref[:, columns]
            keys = key_ref[:, columns]
            values = value_ref[:, columns]
            found = []
            for side in range(2):
                mine = (lane >= head_dim) if side else (lane < head_dim)
                scores = dot_nt(
                    jnp.where(mine, keys, extra_key), jnp.where(mine, queries, extra_query)
                )
                if shifted:
                    peak = jnp.max(scores, axis=0, keepdims=True)
                    scores = scores - peak
                soft = jnp.exp2(scores).astype(bf16)
                mixed = dot_tn(jnp.where(mine, values, ones), soft)
                top, bottom = mixed[:head_dim], mixed[head_dim:]
                wanted, total = (bottom, top) if side else (top, bottom)
                found.append(wanted / total)
                log_total = jnp.log2(total[0:1])
                if shifted:
                    log_total = log_total + peak
                lse_ref[pl.ds(index * 2 + side, 1), :] = log_total
            context_ref[:, columns] = jnp.concatenate(found, axis=0).T.astype(bf16)
            return carry

        lax.fori_loop(0, width // 128, pair, 0)

    chooser = head_chooser(width, head_dim, 1.0)

    def longest(ref):
        values = ref[...].astype(f32)
        return jnp.max(dot_nn((values * values).astype(bf16), chooser), axis=0, keepdims=True)

    bound = jnp.max(longest(query_ref) * longest(key_ref))

    @pl.when(bound < 3600.0)
    def _():
        heads(False)

    @pl.when(jnp.logical_not(bound < 3600.0))
    def _():
        heads(True)


def head_chooser(width, head_dim, value):
    head = lax.broadcasted_iota(jnp.int32, (width, 128), 0) // head_dim
    lane = lax.broadcasted_iota(jnp.int32, (width, 128), 1)
    wanted = (lax.rem(lane, 64) // 3 == head) & ((lane >= 64) == (lax.rem(head, 2) == 0))
    return jnp.where(wanted, value, 0.0).astype(bf16)


def norm_rows(values, gain, shift):
    centered = values - jnp.mean(values, axis=-1, keepdims=True)
    inverse = lax.rsqrt(jnp.mean(centered * centered, axis=-1, keepdims=True) + norm_epsilon)
    unit = centered * inverse
    return unit * gain + shift, unit, inverse


def norm_rows_back(upstream, unit, inverse, gain):
    scaled = upstream * gain
    return inverse * (
        scaled
        - jnp.mean(scaled, axis=-1, keepdims=True)
        - unit * jnp.mean(scaled * unit, axis=-1, keepdims=True)
    )


def feed_forward(
    tiles, facts, context_ref, hidden_ref, own, other, small, small_other, gains, biases, cot_own,
    output_ref, output_send, active_near, preact_near, normed_ref, feed_ref, attend_ref, resid_ref,
    context_grad_ref, delta_ref, sums_ref, inner_sum_ref, grads_send, slope_ref, active_far, preact_far,
):
    rows, width = hidden_ref.shape
    tile = rows // tiles
    half = rows // 2
    part = width // 2
    inner_part = active_near.shape[1]
    units = 2 * inner_part
    chunk = 512
    position, count = lax.axis_index("mp"), facts[0:1, 0:1]
    sums_ref[...] = jnp.zeros_like(sums_ref)
    inner_sum_ref[...] = jnp.zeros_like(inner_sum_ref)
    at_inner = part
    at_outer = part + inner_part
    at_cot = at_outer + inner_part

    def inner_chunk(index):
        pack = (own, other)[index * chunk // inner_part]
        start = at_inner + (index * chunk % inner_part) // chunk * width
        return pack[start : start + width, :]

    def outer_chunk(index):
        pack = (own, other)[index * chunk // inner_part]
        start = at_outer + index * chunk % inner_part
        return pack[start : start + chunk, :]

    head_dim = width // HEADS
    chooser = head_chooser(width, head_dim, -1.0)

    def add(row, values):
        sums_ref[row : row + 1, :] += jnp.sum(values, axis=0, keepdims=True)

    def one_tile(step, carry):
        place = pl.ds(pl.multiple_of(step * tile, tile), tile)
        context = context_ref[place, :]
        attended = dot_nn(context[:, :part], own[:part, :]) + dot_nn(
            context[:, part:], other[:part, :]
        )
        normed, unit_one, inverse_one = norm_rows(
            hidden_ref[place, :] + attended + biases[2:3, :], gains[0:1, :], biases[0:1, :]
        )
        normed_low = normed.astype(bf16)
        normed_ref[place, :] = normed_low
        for index in range(units // chunk):
            columns = slice(index * chunk, (index + 1) * chunk)
            bias = (small, small_other)[index * chunk // inner_part]
            start = index * chunk % inner_part
            preact = dot_nn(normed_low, inner_chunk(index)) + bias[2:3, start : start + chunk]
            phi = 0.5 + 0.5 * lax.erf(preact * inverse_root_two)
            (active_near, active_far)[index * chunk // inner_part][place, start : start + chunk] = (preact * phi).astype(bf16)
            slope_ref[:, columns] = (
                phi + preact * jnp.exp2(preact * preact * (-0.5 * log2_e)) * inverse_root_tau
            ).astype(bf16)
        feed_out = dot_nn(active_near[place, :], own[at_outer:at_cot, :]) + dot_nn(
            active_far[place, :], other[at_outer:at_cot, :]
        )
        output, unit_two, inverse_two = norm_rows(
            normed + feed_out + biases[3:4, :], gains[1:2, :], biases[1:2, :]
        )
        index = lax.broadcasted_iota(jnp.int32, (tile, width), 0)

        @pl.when(step < tiles // 2)
        def _():
            output_ref[place, :] = output
        far = step - tiles // 2
        far_place = pl.ds(pl.multiple_of(jnp.maximum(far, 0) * tile, tile), tile)
        near_place = pl.ds(pl.multiple_of(jnp.minimum(step, tiles // 2 - 1) * tile, tile), tile)

        @pl.when(step >= tiles // 2)
        def _():
            output_send[far_place, :] = output
        cot = jnp.where(
            step < tiles // 2,
            cot_own[near_place, :],
            other[pl.ds(pl.multiple_of(at_cot + jnp.maximum(far, 0) * tile, 32), tile), :],
        ).astype(f32)
        first = jnp.where(
            step < tiles // 2,
            position * half + step * tile,
            (1 - position) * half + far * tile,
        )
        upstream = jnp.where(index + first < count, cot, 0.0)
        resid_two = norm_rows_back(upstream, unit_two, inverse_two, gains[1:2, :])
        feed_grad = resid_two.astype(bf16)
        feed_ref[place, :] = feed_grad
        for index in range(units // chunk):
            columns = slice(index * chunk, (index + 1) * chunk)
            grad = dot_nt(feed_grad, outer_chunk(index))
            start = index * chunk % inner_part
            (preact_near, preact_far)[index * chunk // inner_part][place, start : start + chunk] = (
                grad * slope_ref[:, columns].astype(f32)
            ).astype(bf16)
        normed_grad = resid_two
        for index in range(units // chunk):
            start = index * chunk % inner_part
            block = (preact_near, preact_far)[index * chunk // inner_part]
            normed_grad = normed_grad + dot_nt(
                block[place, start : start + chunk], inner_chunk(index)
            )
        resid_one = norm_rows_back(normed_grad, unit_one, inverse_one, gains[0:1, :])
        resid_ref[place, :] = resid_one
        attend_grad = resid_one.astype(bf16)
        attend_ref[place, :] = attend_grad
        context_grad = jnp.concatenate(
            [dot_nt(attend_grad, own[:part, :]), dot_nt(attend_grad, other[:part, :])], axis=1
        ).astype(bf16)
        context_grad_ref[place, :] = context_grad
        high, low = split_two(context_grad.astype(f32) * context.astype(f32))
        delta = dot_nn(high, chooser) + dot_nn(low, chooser)
        delta_ref[place, :] = three_way(delta, lax.broadcasted_iota(jnp.int32, (tile, 128), 1))
        add(1, normed_grad * unit_one)
        add(2, upstream * unit_two)
        add(3, normed_grad)
        add(4, upstream)
        add(5, resid_one)
        add(6, resid_two)
        for index, block in enumerate((preact_near, preact_far)):
            columns = slice(index * inner_part, (index + 1) * inner_part)
            inner_sum_ref[0:1, columns] += jnp.sum(
                block[place, :].astype(f32), axis=0, keepdims=True
            )
        return carry

    lax.fori_loop(0, tiles, one_tile, 0)
    grads_send[:inner_part, :] = dot_tn(active_far[...], feed_ref[...]).astype(bf16)
    for index in range(inner_part // chunk):
        start = index * chunk
        grads_send[inner_part + index * width : inner_part + (index + 1) * width, :] = dot_tn(
            normed_ref[...], preact_far[:, start : start + chunk]
        ).astype(bf16)
    grads_send[2 * inner_part :, :] = dot_tn(context_ref[:, part:], attend_ref[...]).astype(bf16)


def attend_backward(
    facts, query_ref, key_ref, value_ref, lse_ref, context_grad_ref, delta_ref,
    token_ref, resid_ref, own, other, table, series_own, sums_ref, inner_sum_ref,
    attend_own, send, series_near, series_far, near_out, far_out,
    dquery_ref, dkey_ref, dvalue_ref,
):
    rows, width = query_ref.shape
    head_dim = width // HEADS
    half, history = series_own.shape
    part = width // 2
    position, count = lax.axis_index("mp"), facts[0:1, 0:1]
    lane = lax.broadcasted_iota(jnp.int32, (rows, 128), 1)
    dead = row_number(rows, position) >= count
    last = lax.rem(lane, 64) == 63
    part_row = lax.broadcasted_iota(jnp.int32, (3 * HEADS, 128), 0)
    part_lane = lax.broadcasted_iota(jnp.int32, (3 * HEADS, 128), 1)
    part_head = lax.rem(part_row, HEADS)
    spread = jnp.where(
        part_lane
        == jnp.where(lax.rem(part_head, 2) == 0, 64, 0) + 3 * part_head + part_row // HEADS,
        -1.0,
        0.0,
    ).astype(bf16)
    extra_query = jnp.where(
        last, 1.0, dot_tn(jnp.concatenate(three_parts(lse_ref[...]), axis=0), spread)
    ).astype(bf16)
    extra_key = jnp.where(last & dead, -1e30, 0.0)
    extra_grad = delta_ref[...]
    nothing = jnp.zeros((rows, 128), bf16)

    def pair(index, carry):
        columns = pl.ds(pl.multiple_of(index * 128, 128), 128)
        queries = query_ref[:, columns]
        keys = key_ref[:, columns]
        values = value_ref[:, columns]
        grads = context_grad_ref[:, columns]
        softs, score_grads, own_grads, own_queries, own_keys = [], [], [], [], []
        for side in range(2):
            mine = (lane >= head_dim) if side else (lane < head_dim)
            hot = lax.rem(lane, 64) // 3 == index * 2 + side
            soft = jnp.exp2(
                dot_nt(
                    jnp.where(mine, keys, jnp.where(hot, 1.0, extra_key).astype(bf16)),
                    jnp.where(mine, queries, extra_query),
                )
            )
            centered = dot_nt(
                jnp.where(mine, values, jnp.where(hot, 1.0, 0.0).astype(bf16)),
                jnp.where(mine, grads, extra_grad),
            )
            softs.append(soft.astype(bf16))
            score_grads.append((soft * centered).astype(bf16))
            own_grads.append(jnp.where(mine, grads, nothing))
            own_queries.append(jnp.where(mine, queries, nothing))
            own_keys.append(jnp.where(mine, keys, nothing))
        dvalue = dot_nn(jnp.concatenate(softs, axis=1), jnp.concatenate(own_grads, axis=0))
        dkey = dot_nn(jnp.concatenate(score_grads, axis=1), jnp.concatenate(own_queries, axis=0))
        dquery = dot_tn(jnp.concatenate(own_keys, axis=0), jnp.concatenate(score_grads, axis=0))
        dvalue_ref[:, columns] = dvalue.astype(bf16)
        dkey_ref[:, columns] = (dkey * ln_two).astype(bf16)
        dquery_ref[:, columns] = (dquery.T * head_dim**-0.5).astype(bf16)
        return carry

    lax.fori_loop(0, width // 128, pair, 0)

    tokens = token_ref[...]
    total = resid_ref[...]
    near_out[...] = jnp.zeros_like(near_out)
    far_out[...] = jnp.zeros_like(far_out)
    for kind, grad_ref in enumerate((dquery_ref, dkey_ref, dvalue_ref)):
        low = grad_ref[...]
        attend_own[kind] = dot_tn(tokens, low[:, :part])
        far = dot_tn(tokens, low[:, part:]).astype(bf16)
        send[kind * part : (kind + 1) * part, :part] = far[:part]
        send[kind * part : (kind + 1) * part, part:] = far[part:]
        total = (
            total
            + dot_nt(low[:, :part], attend_block(own, half, kind))
            + dot_nt(low[:, part:], attend_block(other, half, kind))
        )
        if kind != 1:
            column = jnp.sum(low.astype(f32), axis=0, keepdims=True)
            start = kind // 2 * part
            near_out[7:8, start : start + part] = column[:, :part]
            far_out[7:8, start : start + part] = column[:, part:]
    low = total.astype(bf16)
    series_near[...] = dot_nt(low[:half], table[...])
    series_far[...] = dot_nt(low[half:], table[...])
    table_grad = dot_tn(series_own[...], low[:half]) + dot_tn(other[:half, :history], low[half:])
    row = lax.broadcasted_iota(jnp.int32, table_grad.shape, 0)
    seen = row >= facts[1:2, 0:1]
    send[3 * part :, :] = jnp.where(seen, table_grad, 0.0).astype(bf16)
    shared = sums_ref[0:7, :]
    bias_grad = jnp.sum(low.astype(f32), axis=0, keepdims=True)
    near_out[0:7, :] = shared
    far_out[0:7, :] = shared
    near_out[0:1, :] = bias_grad
    far_out[0:1, :] = bias_grad
    count_near = inner_sum_ref.shape[1] // 2 // width
    for index in range(count_near):
        near_out[8 + index : 9 + index, :] = inner_sum_ref[0:1, index * width : (index + 1) * width]
        far_out[8 + index : 9 + index, :] = inner_sum_ref[
            0:1, (count_near + index) * width : (count_near + index + 1) * width
        ]


def left_product(start, matrix):
    both = dot_nt(jnp.concatenate(split_two(start), axis=0), matrix.astype(bf16))
    return both[:8] + both[8:]


def right_product(basis, matrix):
    both = dot_nn(jnp.concatenate(split_two(basis), axis=0), matrix.astype(bf16))
    return both[:8] + both[8:]


def feed_matrices(
    active_ref, preact_ref, normed_ref, feed_ref, context_ref, attend_ref, received,
    e_outer, e_inner, e_mixer, s_outer, s_inner, s_mixer, output_near, output_far,
    outer, inner, mixer, left, output,
):
    width = feed_ref.shape[1]
    inner_part = outer.shape[0]
    part = mixer.shape[0]
    chunk = 512
    join_pair(output_near, output_far, output)
    outer[...] = (
        dot_tn(active_ref[...], feed_ref[...])
        + received[:inner_part, :].astype(f32)
        + e_outer[...]
    )
    for index in range(inner_part // chunk):
        columns = slice(index * chunk, (index + 1) * chunk)
        start = inner_part + index * width
        inner[:, columns] = (
            dot_tn(normed_ref[...], preact_ref[:, columns])
            + received[start : start + width, :].astype(f32)
            + e_inner[:, columns]
        )
    mixer[...] = (
        dot_tn(context_ref[:, :part], attend_ref[...])
        + received[2 * inner_part :, :].astype(f32)
        + e_mixer[...]
    )
    left[:, 0:1024] = left_product(s_outer[...], outer[...])
    left[:, 1024:1536] = left_product(s_inner[...], inner[...])
    left[:, 1536:1792] = left_product(s_mixer[...], mixer[...])


def orthonormal_rows(vectors):
    rank = vectors.shape[0]
    row = lax.broadcasted_iota(jnp.int32, vectors.shape, 0)
    for index in range(rank):
        pivot = vectors[index : index + 1, :]
        inner = jnp.sum(vectors * pivot, axis=1, keepdims=True)
        size = inner[index : index + 1, :] + 1e-12
        reduced = vectors - pivot * (inner / size)
        vectors = jnp.where(
            row > index, reduced, jnp.where(row == index, vectors * lax.rsqrt(size), vectors)
        )
    return vectors


def reduce_factors(
    replicas, facts, near_attend, own, received, e_attend, e_embed, s_attend, s_embed, left_part,
    near, far, outer, inner, mixer,
    left_ref, right_ref, mean_ref, attend, embed,
    start_ref, summed, partial, gathered, parts_one, parts_two, send_sems, recv_sems,
):
    me = lax.axis_index("dp")
    barrier = pltpu.get_barrier_semaphore()
    chunk = start_ref.shape[1] // replicas
    share = 1.0 / replicas

    paired = replicas & (replicas - 1) == 0

    def peer(offset):
        return jnp.bitwise_xor(me, offset) if paired else lax.rem(me + offset, replicas)

    def source_of(offset):
        return jnp.bitwise_xor(me, offset) if paired else lax.rem(me - offset + replicas, replicas)

    def columns(index):
        return pl.ds(pl.multiple_of(index * chunk, 128), chunk)

    def each(what):
        if replicas <= 16:
            for offset in range(replicas - 1, 0, -1):
                what(offset)
            return

        def body(index, carry):
            what(replicas - index)
            return carry

        lax.fori_loop(1, replicas, body, 0)

    each(
        lambda offset: pl.semaphore_signal(
            barrier, inc=1, device_id={"dp": peer(offset)}, device_id_type=pl.DeviceIdType.MESH
        )
    )
    part = near_attend.shape[2]
    total = None
    for kind in range(3):
        rows = slice(kind * part, (kind + 1) * part)
        block = jnp.concatenate([received[rows, :part], received[rows, part:]], axis=0)
        attend[kind] = near_attend[kind] + block.astype(f32) + e_attend[kind]
        term = left_product(s_attend[kind], attend[kind])
        total = term if total is None else total + term
    mine, theirs = facts[2:3, 0:1], facts[3:4, 0:1]
    table_near = own[3 * part :, :].astype(f32)
    table_far = received[3 * part :, :].astype(f32)
    pieces = []
    for group in range(embed.shape[0]):
        grad = jnp.where(mine == group, table_near, 0.0) + jnp.where(theirs == group, table_far, 0.0)
        embed[group] = grad + e_embed[group]
        pieces.append(left_product(s_embed[...], embed[group]))
    used = embed.shape[0] * embed.shape[1]
    start_ref[:, 0:1024] = jnp.concatenate(pieces + [jnp.zeros((8, 1024 - used), f32)], axis=1)
    start_ref[:, 1024:2048] = left_part[:, 0:1024]
    start_ref[:, 2048:2560] = total
    start_ref[:, 2560:3328] = left_part[:, 1024:1792]
    common = near[1:7, :] + far[1:7, :]
    row = lax.broadcasted_iota(jnp.int32, (3, near.shape[1]), 0)
    bias = jnp.where(row == mine, near[0:1, :], 0.0) + jnp.where(row == theirs, far[0:1, :], 0.0)
    start_ref[:, 3328:3840] = jnp.concatenate([bias, common[:5]], axis=0)
    rest = jnp.concatenate([common[5:6], near[7:10, :] + far[7:10, :]], axis=0)
    for row in range(4):
        start_ref[2 * row : 2 * row + 1, 3840:4096] = rest[row : row + 1, :256]
        start_ref[2 * row + 1 : 2 * row + 2, 3840:4096] = rest[row : row + 1, 256:]
    if start_ref.shape[1] > 4096:
        start_ref[:, 4096:] = jnp.zeros((8, start_ref.shape[1] - 4096), f32)
    pl.semaphore_wait(barrier, replicas - 1)

    def all_sum(phase, source, parts, result):
        def scatter(offset):
            other = peer(offset)
            return pltpu.make_async_remote_copy(
                src_ref=source.at[:, columns(other)],
                dst_ref=parts.at[offset],
                send_sem=send_sems.at[2 * phase, offset],
                recv_sem=recv_sems.at[2 * phase, offset],
                device_id={"dp": other},
                device_id_type=pl.DeviceIdType.MESH,
            )

        def spread(offset, owner):
            return pltpu.make_async_remote_copy(
                src_ref=result.at[:, columns(owner)],
                dst_ref=result.at[:, columns(owner)],
                send_sem=send_sems.at[2 * phase + 1, offset],
                recv_sem=recv_sems.at[2 * phase + 1, offset],
                device_id={"dp": peer(offset)},
                device_id_type=pl.DeviceIdType.MESH,
            )

        each(lambda offset: scatter(offset).start())

        def collect(offset, total):
            scatter(offset).wait_recv()
            return total + parts[offset]

        total = source[:, columns(me)]
        if replicas <= 16:
            for offset in range(1, replicas):
                total = collect(offset, total)
        else:
            total = lax.fori_loop(1, replicas, collect, total)
        result[:, columns(me)] = total * share
        each(lambda offset: spread(offset, me).start())
        each(lambda offset: spread(offset, source_of(offset)).wait_recv())
        each(lambda offset: scatter(offset).wait_send())
        each(lambda offset: spread(offset, me).wait_send())

    all_sum(0, start_ref, parts_one, summed)
    mean_ref[...] = summed[:, 3328:4096]
    bases = []
    for start, size in ((0, 1024), (1024, 1024), (2048, 512), (2560, 512), (3072, 256)):
        basis = orthonormal_rows(summed[:, start : start + size])
        left_ref[:, start : start + size] = basis
        bases.append(basis)
    height = embed.shape[1]
    total = None
    for group in range(embed.shape[0]):
        term = right_product(bases[0][:, group * height : (group + 1) * height], embed[group])
        total = term if total is None else total + term
    partial[:, 0:512] = total
    partial[:, 512:1024] = right_product(bases[1], outer[...])
    for kind in range(3):
        partial[:, 1024 + kind * 256 : 1280 + kind * 256] = right_product(bases[2], attend[kind])
    partial[:, 1792:2816] = right_product(bases[3], inner[...])
    partial[:, 2816:3328] = right_product(bases[4], mixer[...])
    partial[:, 3328:] = jnp.zeros((8, partial.shape[1] - 3328), f32)
    all_sum(1, partial, parts_two, gathered)
    right_ref[...] = gathered[:, :3328]


def renew_all(
    step_rate, mixer_rate, left, right, mean, series_near, series_far, *refs,
):
    matrices, weights, moments = refs[0:5], refs[5:10], refs[10:15]
    vectors, vector_moments = refs[15:20], refs[20:25]
    errors, new_weights, new_moments = refs[25:30], refs[30:35], refs[35:40]
    new_vectors, new_vector_moments = refs[40:45], refs[45:50]
    lefts, rights, series_grad = refs[50:55], refs[55:60], refs[60]
    step = pl.program_id(0)
    join_pair(series_near, series_far, series_grad)

    def approx(basis, factor):
        left_high, left_low = split_two(basis)
        right_high, right_low = split_two(factor)
        return dot_tn(
            jnp.concatenate([left_high, left_low, left_high, left_low], axis=0),
            jnp.concatenate([right_high, right_high, right_low, right_low], axis=0),
        )

    def write(index, where, update, rate):
        errors[index][where] = matrices[index][where] - update
        moment = momentum_decay * moments[index][where] + update
        new_moments[index][where] = moment
        new_weights[index][where] = weights[index][where] - rate * moment

    def cut(start, size):
        return pl.ds(pl.multiple_of(start + step * size, 128), size)

    every = (slice(None), slice(None))
    groups, height, block = matrices[0].shape
    factor = right[:, cut(0, block)]
    for group in range(groups):
        write(
            0, (group, slice(None), slice(None)),
            approx(left[:, group * height : (group + 1) * height], factor), step_rate,
        )
    write(1, every, approx(left[:, cut(1024, matrices[1].shape[0])], right[:, 512:1024]), step_rate)
    basis = left[:, cut(2048, matrices[2].shape[1])]
    for kind in range(3):
        write(
            2, (kind, slice(None), slice(None)),
            approx(basis, right[:, 1024 + kind * 256 : 1280 + kind * 256]), step_rate,
        )
    write(3, every, approx(left[:, cut(2560, matrices[3].shape[0])], right[:, 1792:2816]), step_rate)
    write(4, every, approx(left[:, 3072:3328], right[:, cut(2816, matrices[4].shape[1])]), mixer_rate)

    @pl.when(step == 0)
    def _():
        for group in range(groups):
            lefts[0][group] = left[:, group * height : (group + 1) * height]
        lefts[1][...] = left[:, 1024:2048]
        lefts[2][...] = left[:, 2048:2560]
        lefts[3][...] = left[:, 2560:3072]
        lefts[4][...] = left[:, 3072:3328]
        rights[0][...] = right[:, 0:512]
        rights[1][...] = right[:, 512:1024]
        for kind in range(3):
            rights[2][kind] = right[:, 1024 + kind * 256 : 1280 + kind * 256]
        rights[3][...] = right[:, 1792:2816]
        rights[4][...] = right[:, 2816:3328]

        def renew(index, rows, columns, gradient):
            moment = momentum_decay * vector_moments[index][rows, columns] + gradient
            new_vector_moments[index][rows, columns] = moment
            new_vectors[index][rows, columns] = vectors[index][rows, columns] - step_rate * moment

        renew(0, slice(0, 3), slice(None), mean[0:3, :512])
        renew(1, slice(0, 2), slice(None), mean[3:5, :512])
        renew(2, slice(0, 3), slice(None), mean[5:8, :512])
        renew(2, slice(3, 4), slice(0, 256), mean[0:1, 512:])
        renew(2, slice(3, 4), slice(256, 512), mean[1:2, 512:])
        renew(3, slice(0, 1), slice(None), mean[2:3, 512:])
        renew(3, slice(1, 2), slice(None), mean[3:4, 512:])
        for index in range(4):
            renew(
                4, slice(0, 1), slice(index * 256, (index + 1) * 256),
                mean[4 + index : 5 + index, 512:],
            )


def call(kernel, outs, args, *, cost, in_specs=None, scratch=(), limit=32, name=None):
    return pl.pallas_call(
        kernel,
        out_shape=outs,
        in_specs=in_specs if in_specs is not None else [VM] * len(args),
        out_specs=jax.tree.map(lambda _: VM, outs),
        scratch_shapes=list(scratch),
        compiler_params=pltpu.CompilerParams(vmem_limit_bytes=limit * MIB),
        cost_estimate=estimate(cost),
        name=name,
    )(*args)


def estimate(microseconds):
    return pl.CostEstimate(
        flops=int(microseconds * 1e9), bytes_accessed=int(microseconds * 2e6), transcendentals=0
    )


def sds(shape, dtype=f32):
    return jax.ShapeDtypeStruct(shape, dtype)


def local(
    series, groups, counts, cotangent,
    embed_weight, embed_moment, embed_error, embed_start,
    attend_weight, attend_moment, attend_error, attend_start,
    mixer_weight, mixer_moment, mixer_error, mixer_start,
    inner_weight, inner_moment, inner_error, inner_start,
    outer_weight, outer_moment, outer_error, outer_start,
    embed_bias, embed_bias_moment, query_bias, query_bias_moment,
    inner_bias, inner_bias_moment, norm_gains, gains_moment, shared_biases, biases_moment,
):
    replicas = lax.axis_size("dp")
    half, windows, history = series.shape
    rows = 2 * half
    group_count, _, width = embed_weight.shape
    part = attend_weight.shape[2]
    inner_part = inner_weight.shape[1]
    units = 2 * inner_part
    turned = lambda a: a.transpose(1, 0, 2)

    def swap(values):
        return lax.ppermute(values, "mp", [(0, 1), (1, 0)])

    low = sds((rows, width), bf16)
    full = sds((rows, width))
    near = sds((half, width))
    packed = sds((half + 3 * part + 16, width), bf16)
    send_one, other_one, series_own, small, facts, send_two, cot_own = pl.pallas_call(
        prepare,
        out_shape=[
            packed, packed, sds((half, history), bf16), sds((8, inner_part)), sds((8, 128), jnp.int32),
            sds((part + 2 * inner_part + half, width), bf16), sds((half, width), bf16),
        ],
        in_specs=[HB] * 10,
        out_specs=[VM] * 7,
        scratch_shapes=[
            pltpu.SMEM(groups.shape, jnp.int32), pltpu.SMEM(counts.shape, jnp.int32),
            pltpu.VMEM(series.shape, bf16), pltpu.VMEM((3, width, part), f32),
            pltpu.VMEM(query_bias.shape, f32), pltpu.VMEM((1, inner_part), f32),
            pltpu.VMEM(cotangent.shape, bf16), pltpu.VMEM(mixer_weight.shape, f32),
            pltpu.VMEM(inner_weight.shape, f32), pltpu.VMEM(outer_weight.shape, f32),
            pltpu.SemaphoreType.DMA((10,)), pltpu.SemaphoreType.DMA((2,)), pltpu.SemaphoreType.DMA((2,)),
        ],
        compiler_params=pltpu.CompilerParams(
            collective_id=2, has_side_effects=True, vmem_limit_bytes=LIMITS[0] * MIB
        ),
        cost_estimate=estimate(7),
        name="prepare",
    )(
        *(
            pltpu.with_memory_space_constraint(a, pltpu.HBM)
            for a in (
                groups, counts, series, turned(attend_weight), query_bias, inner_bias[None],
                cotangent, mixer_weight, inner_weight, outer_weight,
            )
        )
    )
    other_two = swap(send_two)
    hidden, tokens, queries, keys, values, context, lse, small_other, table = call(
        attend_forward,
        [full, low, low, low, low, low, sds((HEADS, rows)), sds((8, inner_part)), sds((history, width), bf16)],
        (facts, series_own, embed_weight, embed_bias, send_one, other_one, small),
        limit=LIMITS[2], cost=15,
        name="attend_forward",
    )
    (
        output_near, output_send, active, preact_grad, normed_low, feed_grad, attend_out, resid_one,
        context_grad, delta, sums, inner_sums, grads_send,
    ) = call(
        functools.partial(feed_forward, TILES),
        [near, near, sds((rows, inner_part), bf16), sds((rows, inner_part), bf16), low, low, low, full, low,
         sds((rows, 128), bf16), sds((8, width)), sds((8, units)),
         sds((2 * inner_part + part, width), bf16)],
        (facts, context, hidden, send_two, other_two, small, small_other, norm_gains, shared_biases, cot_own),
        limit=LIMITS[3], cost=22,
        scratch=[
            pltpu.VMEM((rows // TILES, units), bf16), pltpu.VMEM((rows, inner_part), bf16),
            pltpu.VMEM((rows, inner_part), bf16),
        ],
        name="feed_forward",
    )
    output_other = swap(output_send)
    grads_other = swap(grads_send)
    attend_near, send_three, series_near, series_far, sums_near, sums_far = call(
        attend_backward,
        [sds((3, width, part)), sds((3 * part + history, width), bf16), sds((half, history)),
         sds((half, history)), sds((16, width)), sds((16, width))],
        (facts, queries, keys, values, lse, context_grad, delta, tokens, resid_one, send_one,
         other_one, table, series_own, sums, inner_sums),
        limit=LIMITS[4], cost=22,
        scratch=[pltpu.VMEM((rows, width), bf16)] * 3,
        name="attend_backward",
    )
    other_three = swap(send_three)
    series_other = swap(series_far)
    sums_other = swap(sums_far)
    outer_matrix, inner_matrix, mixer_matrix, left_part, output = call(
        feed_matrices,
        [sds(outer_weight.shape), sds(inner_weight.shape), sds(mixer_weight.shape), sds((8, 1792)),
         sds((half, windows, width))],
        (active, preact_grad, normed_low, feed_grad, context, attend_out, grads_other,
         outer_error[0], inner_error[0], mixer_error[0], outer_start[0].T, inner_start.T, mixer_start[0].T,
         output_near, output_other),
        limit=LIMITS[5], cost=6,
        name="feed_matrices",
    )
    padded = max(128, -(-4096 // replicas // 128) * 128)
    total = padded * replicas
    left, right, mean, attend_matrix, embed_matrix = pl.pallas_call(
        functools.partial(reduce_factors, replicas),
        out_shape=[sds((8, 3328)), sds((8, 3328)), sds((8, 768)), sds((3, width, part)), sds(embed_weight.shape)],
        in_specs=[VM] * 14,
        out_specs=[VM] * 5,
        scratch_shapes=[
            pltpu.VMEM((8, total), f32), pltpu.VMEM((8, total), f32), pltpu.VMEM((8, total), f32),
            pltpu.VMEM((8, total), f32),
            pltpu.VMEM((replicas, 8, padded), f32), pltpu.VMEM((replicas, 8, padded), f32),
            pltpu.SemaphoreType.DMA((4, replicas)), pltpu.SemaphoreType.DMA((4, replicas)),
        ],
        compiler_params=pltpu.CompilerParams(
            collective_id=1, has_side_effects=True, vmem_limit_bytes=LIMITS[6] * MIB
        ),
        cost_estimate=estimate(30),
        name="reduce_factors",
    )(
        facts, attend_near, send_three, other_three, turned(attend_error[0]), embed_error[0],
        attend_start.transpose(0, 2, 1), embed_start.T, left_part, sums_near, sums_other,
        outer_matrix, inner_matrix, mixer_matrix,
    )
    matrices = (embed_matrix, outer_matrix, attend_matrix, inner_matrix, mixer_matrix)

    step_rate = base_rate * math.sqrt(replicas * 7 / (windows * rows))
    mixer_rate = step_rate * math.sqrt(width / max(width * 16 // rows, 1))
    steps = 4
    whole = lambda a: pl.BlockSpec(a.shape, lambda i: (0,) * len(a.shape))
    column = lambda a: pl.BlockSpec((a.shape[0], a.shape[1] // steps), lambda i: (0, i))
    row = lambda a: pl.BlockSpec((a.shape[0] // steps, a.shape[1]), lambda i: (i, 0))
    middle = lambda a: pl.BlockSpec((a.shape[0], a.shape[1] // steps, a.shape[2]), lambda i: (0, i, 0))
    last = lambda a: pl.BlockSpec((a.shape[0], a.shape[1], a.shape[2] // steps), lambda i: (0, 0, i))
    specs = [spec(a) for spec, a in zip((last, row, middle, row, column), matrices)]
    vectors = (embed_bias, norm_gains, shared_biases, query_bias, inner_bias[None])
    vector_moments = (
        embed_bias_moment, gains_moment, biases_moment, query_bias_moment, inner_bias_moment[None]
    )
    vector_specs = [whole(a) for a in vectors]
    split = pl.BlockSpec((half // steps, history), lambda i: (i, 0))
    split_out = pl.BlockSpec((half // steps, windows, history), lambda i: (i, 0, 0))
    factors = [
        sds((group_count, 8, history)), sds((8, 1024)), sds((8, 512)), sds((8, 512)), sds((8, 256)),
        sds((8, 512)), sds((8, 512)), sds((3, 8, part)), sds((8, 1024)), sds((8, 512)),
    ]
    found = pl.pallas_call(
        functools.partial(renew_all, step_rate, mixer_rate),
        grid=(steps,),
        out_shape=[sds(a.shape) for a in matrices] * 3 + [sds(a.shape) for a in vectors] * 2
        + factors + [sds(series.shape)],
        in_specs=[whole(left), whole(right), whole(mean), split, split] + specs * 3 + vector_specs * 2,
        out_specs=specs * 3 + vector_specs * 2 + [whole(a) for a in factors] + [split_out],
        compiler_params=pltpu.CompilerParams(vmem_limit_bytes=LIMITS[7] * MIB),
        cost_estimate=estimate(12),
        name="renew_all",
    )(
        left, right, mean, series_near, series_other, *matrices,
        embed_weight, outer_weight, turned(attend_weight), inner_weight, mixer_weight,
        embed_moment, outer_moment, turned(attend_moment), inner_moment, mixer_moment,
        *vectors, *vector_moments,
    )
    errors, weights, moments = found[0:5], found[5:10], found[10:15]
    new_vectors, new_vector_moments = found[15:20], found[20:25]
    lefts, rights = found[25:30], found[30:35]
    return (
        output,
        found[35],
        weights[0],
        moments[0],
        errors[0][None],
        lefts[0].transpose(0, 2, 1),
        rights[0].T,
        turned(weights[2]),
        turned(moments[2]),
        turned(errors[2])[None],
        lefts[2].T[None],
        rights[2].transpose(0, 2, 1),
        weights[4],
        moments[4],
        errors[4][None],
        lefts[4].T,
        rights[4].T[None],
        weights[3],
        moments[3],
        errors[3][None],
        lefts[3].T[None],
        rights[3].T,
        weights[1],
        moments[1],
        errors[1][None],
        lefts[1].T,
        rights[1].T[None],
        new_vector_moments[0],
        new_vectors[0],
        new_vector_moments[3],
        new_vectors[3],
        new_vector_moments[4][0],
        new_vectors[4][0],
        new_vector_moments[1],
        new_vectors[1],
        new_vector_moments[2],
        new_vectors[2],
    )


def solution(mesh):
    return jax.shard_map(
        local,
        mesh=mesh,
        in_specs=(
            P("mp", "dp", None),
            P("dp"),
            P("dp"),
            P("mp", "dp", None),
            P(),
            P(),
            P("dp", None, None, None),
            P(),
            P(None, None, "mp"),
            P(None, None, "mp"),
            P("dp", None, None, "mp"),
            P(None, "mp", None),
            P("mp", None),
            P("mp", None),
            P("dp", "mp", None),
            P("mp", None, None),
            P(None, "mp"),
            P(None, "mp"),
            P("dp", None, "mp"),
            P("mp", None),
            P("mp", None),
            P("mp", None),
            P("dp", "mp", None),
            P("mp", None, None),
            P(),
            P(),
            P(None, "mp"),
            P(None, "mp"),
            P("mp"),
            P("mp"),
            P(),
            P(),
            P(),
            P(),
        ),
        out_specs=(
            P("mp", "dp", None),
            P("mp", "dp", None),
            P(),
            P(),
            P("dp", None, None, None),
            P(),
            P(),
            P(None, None, "mp"),
            P(None, None, "mp"),
            P("dp", None, None, "mp"),
            P("mp", None, None),
            P(None, "mp", None),
            P("mp", None),
            P("mp", None),
            P("dp", "mp", None),
            P("mp", None),
            P("mp", None, None),
            P(None, "mp"),
            P(None, "mp"),
            P("dp", None, "mp"),
            P("mp", None, None),
            P("mp", None),
            P("mp", None),
            P("mp", None),
            P("dp", "mp", None),
            P("mp", None),
            P("mp", None, None),
            P(),
            P(),
            P(None, "mp"),
            P(None, "mp"),
            P("mp"),
            P("mp"),
            P(),
            P(),
            P(),
            P(),
        ),
        check_vma=False,
    )
```

```python
import functools
import math

import jax
import jax.numpy as jnp
from jax import lax
from jax.experimental import pallas as pl
from jax.experimental.pallas import tpu as pltpu
from jax.sharding import PartitionSpec as P

HEADS = 8
momentum_decay = 0.9
norm_epsilon = 1e-05
base_rate = 0.03
inverse_root_two = 0.7071067811865476
inverse_root_tau = 0.3989422804014327
log2_e = 1.4426950408889634
ln_two = 0.6931471805599453
f32 = jnp.float32
bf16 = jnp.bfloat16
VMEM = pltpu.VMEM
VM = pl.BlockSpec(memory_space=pltpu.VMEM)
HB = pl.BlockSpec(memory_space=pltpu.HBM)
MIB = 1024 * 1024


def dot_nn(a, b):
    return lax.dot_general(a, b, (((1,), (0,)), ((), ())), preferred_element_type=f32)


def dot_nt(a, b):
    return lax.dot_general(a, b, (((1,), (1,)), ((), ())), preferred_element_type=f32)


def dot_tn(a, b):
    return lax.dot_general(a, b, (((0,), (0,)), ((), ())), preferred_element_type=f32)


def split_two(x):
    high = x.astype(bf16)
    return high, (x - high.astype(f32)).astype(bf16)


def three_way(x, lane):
    high = x.astype(bf16).astype(f32)
    rest = x - high
    middle = rest.astype(bf16).astype(f32)
    last = rest - middle
    place = lax.rem(lax.rem(lane, 64), 3)
    return jnp.where(place == 0, high, jnp.where(place == 1, middle, last)).astype(bf16)


LIMITS = (12, 14, 12, 14, 16, 8, 8, 28)
TILES = 2


def row_number(rows, position):
    half = rows // 2
    index = lax.broadcasted_iota(jnp.int32, (rows, 128), 0)
    return jnp.where(index < half, index + position * half, index - half + (1 - position) * half)


def lookback_of(group, history):
    return jnp.where(
        group == 0, history * 2 // 7, jnp.where(group == 1, history * 4 // 7, history)
    ).astype(jnp.int32)


def split_pair(pair_ref, mine, theirs, columns):
    position = lax.axis_index("mp")

    @pl.when(position == 0)
    def _():
        mine[:, columns] = pair_ref[:, 0, :]
        theirs[:, columns] = pair_ref[:, 1, :]

    @pl.when(position != 0)
    def _():
        mine[:, columns] = pair_ref[:, 1, :]
        theirs[:, columns] = pair_ref[:, 0, :]


def join_pair(mine, theirs, pair_ref):
    position = lax.axis_index("mp")

    @pl.when(position == 0)
    def _():
        pair_ref[:, 0, :] = mine[...]
        pair_ref[:, 1, :] = theirs[...]

    @pl.when(position != 0)
    def _():
        pair_ref[:, 1, :] = mine[...]
        pair_ref[:, 0, :] = theirs[...]


def three_parts(x):
    high = x.astype(bf16)
    rest = x - high.astype(f32)
    middle = rest.astype(bf16)
    return high, middle, (rest - middle.astype(f32)).astype(bf16)


def prepare(
    groups_hbm, counts_hbm, series_hbm, attend_hbm, query_bias_hbm, inner_bias_hbm,
    cot_hbm, mixer_hbm, inner_hbm, outer_hbm,
    send, received, series_own, small, facts, send_feed, cot_own,
    groups, counts, series, attend, query_bias, inner_bias, cotangent, mixer, inner, outer,
    done, send_sems, recv_sems,
):
    position = lax.axis_index("mp")
    partner = {"mp": 1 - position}
    barrier = pltpu.get_barrier_semaphore()
    pl.semaphore_signal(barrier, inc=1, device_id=partner, device_id_type=pl.DeviceIdType.MESH)
    copies = []
    for source, target in (
        (query_bias_hbm, query_bias), (inner_bias_hbm, inner_bias), (attend_hbm, attend),
        (series_hbm, series), (groups_hbm, groups), (counts_hbm, counts), (cot_hbm, cotangent),
        (mixer_hbm, mixer), (inner_hbm, inner), (outer_hbm, outer),
    ):
        copies.append(pltpu.make_async_copy(source, target, done.at[len(copies)]))
        copies[-1].start()
    half, _, history = series.shape
    width = send.shape[1]
    depth = attend.shape[1] // 2
    end = half + 3 * depth
    part = query_bias.shape[1]
    trades = [
        pltpu.make_async_remote_copy(
            src_ref=send.at[rows], dst_ref=received.at[rows], send_sem=send_sems.at[index],
            recv_sem=recv_sems.at[index], device_id=partner, device_id_type=pl.DeviceIdType.MESH,
        )
        for index, rows in enumerate((slice(half, end + 16), slice(0, half)))
    ]
    copies[0].wait()
    copies[1].wait()
    small[...] = jnp.zeros_like(small)
    small[0:2, :part] = query_bias[...]
    small[2:3, :] = inner_bias[...]
    values = jnp.concatenate(
        [
            jnp.concatenate([query_bias[0:1, :], query_bias[1:2, :]], axis=1),
            inner_bias[:, :width],
            inner_bias[:, width:],
            jnp.zeros((1, width), f32),
        ],
        axis=0,
    )
    send[end : end + 16, :] = jnp.concatenate(
        [*three_parts(values), jnp.zeros((4, width), bf16)], axis=0
    )
    copies[2].wait()
    for kind in range(3):
        rows = slice(half + kind * depth, half + (kind + 1) * depth)
        send[rows, :256] = attend[kind, :depth, :].astype(bf16)
        send[rows, 256:] = attend[kind, depth:, :].astype(bf16)
    pl.semaphore_wait(barrier, 1)
    trades[0].start()
    send[:half, 256:] = jnp.zeros((half, width - 256), bf16)
    copies[3].wait()
    split_pair(series, series_own, send.at[:half], slice(0, history))
    trades[1].start()
    copies[4].wait()
    copies[5].wait()
    group = jnp.where(position == 0, groups[0], groups[1])
    other_group = jnp.where(position == 0, groups[1], groups[0])
    count = jnp.where(position == 0, counts[0], counts[1])
    first = history - lookback_of(group, history)
    row = lax.broadcasted_iota(jnp.int32, facts.shape, 0)
    facts[...] = jnp.where(
        row == 0, count, jnp.where(row == 1, first, jnp.where(row == 2, group, other_group))
    )
    m, d, o = mixer.shape[0], inner.shape[0], outer.shape[0]
    copies[6].wait()
    split_pair(cotangent, cot_own, send_feed.at[m + 2 * d + o :], slice(None))
    copies[7].wait()
    send_feed[:m] = mixer[...].astype(bf16)
    copies[8].wait()
    send_feed[m : m + d] = inner[:, :512].astype(bf16)
    send_feed[m + d : m + 2 * d] = inner[:, 512:].astype(bf16)
    copies[9].wait()
    send_feed[m + 2 * d : m + 2 * d + o] = outer[...].astype(bf16)
    for trade in trades:
        trade.wait()


def unpack_small(other, small_other):
    part = other.shape[1] // 2
    parts = other[other.shape[0] - 16 :, :].astype(f32)
    values = parts[0:4] + parts[4:8] + parts[8:12]
    small_other[0:1, :part] = values[0:1, :part]
    small_other[1:2, :part] = values[0:1, part:]
    small_other[2:3, : 2 * part] = values[1:2, :]
    small_other[2:3, 2 * part :] = values[2:3, :]


def attend_block(pack, half, kind):
    start = half + kind * 256
    return jnp.concatenate([pack[start : start + 256, :256], pack[start : start + 256, 256:]], axis=0)


def attend_forward(
    facts, series_own, embed, embed_bias, own, other, small,
    hidden_ref, token_ref, query_ref, key_ref, value_ref, context_ref, lse_ref, small_other, table, peak_ref,
):
    unpack_small(other, small_other)
    chosen, bias_row = embed[0], embed_bias[0:1, :]
    for group in range(1, embed.shape[0]):
        here = facts[2:3, 0:1] == group
        chosen = jnp.where(here, embed[group], chosen)
        bias_row = jnp.where(here, embed_bias[group : group + 1, :], bias_row)
    row = lax.broadcasted_iota(jnp.int32, chosen.shape, 0)
    table[...] = jnp.where(row >= facts[1:2, 0:1], chosen, 0.0).astype(bf16)
    rows, width = hidden_ref.shape
    half, history = series_own.shape
    part = width // 2
    head_dim = width // HEADS
    position, count = lax.axis_index("mp"), facts[0:1, 0:1]
    for index, block in enumerate((series_own[...], other[:half, :history])):
        values = dot_nn(block, table[...]) + bias_row
        hidden_ref[pl.ds(index * half, half), :] = values
        token_ref[pl.ds(index * half, half), :] = values.astype(bf16)
    scale = head_dim**-0.5 * log2_e
    tokens = token_ref[...]
    for index, (pack, bias) in enumerate(((own, small), (other, small_other))):
        columns = pl.ds(index * part, part)
        query_ref[:, columns] = (
            (dot_nn(tokens, attend_block(pack, half, 0)) + bias[0:1, :part]) * scale
        ).astype(bf16)
        key_ref[:, columns] = dot_nn(tokens, attend_block(pack, half, 1)).astype(bf16)
        value_ref[:, columns] = (
            dot_nn(tokens, attend_block(pack, half, 2)) + bias[1:2, :part]
        ).astype(bf16)
    lane = lax.broadcasted_iota(jnp.int32, (rows, 128), 1)
    dead = row_number(rows, position) >= count
    last = lax.rem(lane, 64) == 63
    extra_query = jnp.where(last, 1.0, 0.0).astype(bf16)
    extra_key = jnp.where(last & dead, -1e30, 0.0).astype(bf16)
    ones = jnp.ones((rows, 128), bf16)

    chooser = head_chooser(width, head_dim, 1.0)

    def longest(ref):
        values = ref[...].astype(f32)
        return jnp.max(dot_nn((values * values).astype(bf16), chooser), axis=0, keepdims=True)

    bound = jnp.max(longest(query_ref) * longest(key_ref))
    peak_ref[...] = jnp.zeros_like(peak_ref)

    @pl.when(jnp.logical_not(bound < 3600.0))
    def _():
        block = 128
        block_lane = lane[:block]

        def one_head(head, carry):
            columns = pl.ds(pl.multiple_of(head // 2 * 128, 128), 128)
            side = lax.rem(head, 2)
            query = jnp.where((lane // head_dim) == side, query_ref[:, columns], extra_query)

            def one_block(index, peak):
                place = pl.ds(pl.multiple_of(index * block, block), block)
                keys = key_ref[place, columns]
                far = lax.broadcasted_iota(jnp.int32, (block, 128), 0) + index * block
                near = jnp.where(
                    far < half, far + position * half, far - half + (1 - position) * half
                )
                mask = jnp.where(
                    (lax.rem(block_lane, 64) == 63) & (near >= count), -1e30, 0.0
                ).astype(bf16)
                scores = dot_nt(jnp.where((block_lane // head_dim) == side, keys, mask), query)
                return jnp.maximum(peak, jnp.max(scores, axis=0, keepdims=True))

            peak_ref[pl.ds(head, 1), :] = lax.fori_loop(
                0, rows // block, one_block, jnp.full((1, rows), -1e30, f32)
            )
            return carry

        lax.fori_loop(0, HEADS, one_head, 0)

    spread = part_spreader(-1.0)
    extra_query = jnp.where(
        last, 1.0, dot_tn(jnp.concatenate(three_parts(peak_ref[...]), axis=0), spread)
    ).astype(bf16)
    extra_key = jnp.where(last & dead, -1e30, 0.0)

    def pair(index, carry):
        columns = pl.ds(pl.multiple_of(index * 128, 128), 128)
        queries = query_ref[:, columns]
        keys = key_ref[:, columns]
        values = value_ref[:, columns]
        found = []
        for side in range(2):
            mine = (lane >= head_dim) if side else (lane < head_dim)
            hot = lax.rem(lane, 64) // 3 == index * 2 + side
            scores = dot_nt(
                jnp.where(mine, keys, jnp.where(hot, 1.0, extra_key).astype(bf16)),
                jnp.where(mine, queries, extra_query),
            )
            soft = jnp.exp2(scores).astype(bf16)
            mixed = dot_tn(jnp.where(mine, values, ones), soft)
            top, bottom = mixed[:head_dim], mixed[head_dim:]
            wanted, total = (bottom, top) if side else (top, bottom)
            found.append(wanted / total)
            place = pl.ds(index * 2 + side, 1)
            lse_ref[place, :] = jnp.log2(total[0:1]) + peak_ref[place, :]
        context_ref[:, columns] = jnp.concatenate(found, axis=0).T.astype(bf16)
        return carry

    lax.fori_loop(0, width // 128, pair, 0)


def part_spreader(value):
    row = lax.broadcasted_iota(jnp.int32, (3 * HEADS, 128), 0)
    lane = lax.broadcasted_iota(jnp.int32, (3 * HEADS, 128), 1)
    head = lax.rem(row, HEADS)
    wanted = lane == jnp.where(lax.rem(head, 2) == 0, 64, 0) + 3 * head + row // HEADS
    return jnp.where(wanted, value, 0.0).astype(bf16)


def head_chooser(width, head_dim, value):
    head = lax.broadcasted_iota(jnp.int32, (width, 128), 0) // head_dim
    lane = lax.broadcasted_iota(jnp.int32, (width, 128), 1)
    wanted = (lax.rem(lane, 64) // 3 == head) & ((lane >= 64) == (lax.rem(head, 2) == 0))
    return jnp.where(wanted, value, 0.0).astype(bf16)


def norm_rows(values, gain, shift):
    centered = values - jnp.mean(values, axis=-1, keepdims=True)
    inverse = lax.rsqrt(jnp.mean(centered * centered, axis=-1, keepdims=True) + norm_epsilon)
    unit = centered * inverse
    return unit * gain + shift, unit, inverse


def norm_rows_back(upstream, unit, inverse, gain):
    scaled = upstream * gain
    return inverse * (
        scaled
        - jnp.mean(scaled, axis=-1, keepdims=True)
        - unit * jnp.mean(scaled * unit, axis=-1, keepdims=True)
    )


def feed_forward(
    tiles, facts, context_ref, hidden_ref, own, other, small, small_other, gains, biases, cot_own,
    output_ref, output_send, active_near, preact_near, normed_ref, feed_ref, attend_ref, resid_ref,
    context_grad_ref, delta_ref, sums_ref, inner_sum_ref, grads_send, slope_ref, active_far, preact_far,
):
    rows, width = hidden_ref.shape
    tile = rows // tiles
    half = rows // 2
    part = width // 2
    inner_part = active_near.shape[1]
    units = 2 * inner_part
    chunk = 512
    position, count = lax.axis_index("mp"), facts[0:1, 0:1]
    sums_ref[...] = jnp.zeros_like(sums_ref)
    inner_sum_ref[...] = jnp.zeros_like(inner_sum_ref)
    at_inner = part
    at_outer = part + inner_part
    at_cot = at_outer + inner_part

    def inner_chunk(index):
        pack = (own, other)[index * chunk // inner_part]
        start = at_inner + (index * chunk % inner_part) // chunk * width
        return pack[start : start + width, :]

    def outer_chunk(index):
        pack = (own, other)[index * chunk // inner_part]
        start = at_outer + index * chunk % inner_part
        return pack[start : start + chunk, :]

    head_dim = width // HEADS
    chooser = head_chooser(width, head_dim, -1.0)

    def add(row, values):
        sums_ref[row : row + 1, :] += jnp.sum(values, axis=0, keepdims=True)

    def one_tile(step, carry):
        place = pl.ds(pl.multiple_of(step * tile, tile), tile)
        context = context_ref[place, :]
        attended = dot_nn(context[:, :part], own[:part, :]) + dot_nn(
            context[:, part:], other[:part, :]
        )
        normed, unit_one, inverse_one = norm_rows(
            hidden_ref[place, :] + attended + biases[2:3, :], gains[0:1, :], biases[0:1, :]
        )
        normed_low = normed.astype(bf16)
        normed_ref[place, :] = normed_low
        for index in range(units // chunk):
            columns = slice(index * chunk, (index + 1) * chunk)
            bias = (small, small_other)[index * chunk // inner_part]
            start = index * chunk % inner_part
            preact = dot_nn(normed_low, inner_chunk(index)) + bias[2:3, start : start + chunk]
            phi = 0.5 + 0.5 * lax.erf(preact * inverse_root_two)
            (active_near, active_far)[index * chunk // inner_part][place, start : start + chunk] = (preact * phi).astype(bf16)
            slope_ref[:, columns] = (
                phi + preact * jnp.exp2(preact * preact * (-0.5 * log2_e)) * inverse_root_tau
            ).astype(bf16)
        feed_out = dot_nn(active_near[place, :], own[at_outer:at_cot, :]) + dot_nn(
            active_far[place, :], other[at_outer:at_cot, :]
        )
        output, unit_two, inverse_two = norm_rows(
            normed + feed_out + biases[3:4, :], gains[1:2, :], biases[1:2, :]
        )
        index = lax.broadcasted_iota(jnp.int32, (tile, width), 0)

        @pl.when(step < tiles // 2)
        def _():
            output_ref[place, :] = output
        far = step - tiles // 2
        far_place = pl.ds(pl.multiple_of(jnp.maximum(far, 0) * tile, tile), tile)
        near_place = pl.ds(pl.multiple_of(jnp.minimum(step, tiles // 2 - 1) * tile, tile), tile)

        @pl.when(step >= tiles // 2)
        def _():
            output_send[far_place, :] = output
        cot = jnp.where(
            step < tiles // 2,
            cot_own[near_place, :],
            other[pl.ds(pl.multiple_of(at_cot + jnp.maximum(far, 0) * tile, 32), tile), :],
        ).astype(f32)
        first = jnp.where(
            step < tiles // 2,
            position * half + step * tile,
            (1 - position) * half + far * tile,
        )
        upstream = jnp.where(index + first < count, cot, 0.0)
        resid_two = norm_rows_back(upstream, unit_two, inverse_two, gains[1:2, :])
        feed_grad = resid_two.astype(bf16)
        feed_ref[place, :] = feed_grad
        for index in range(units // chunk):
            columns = slice(index * chunk, (index + 1) * chunk)
            grad = dot_nt(feed_grad, outer_chunk(index))
            start = index * chunk % inner_part
            (preact_near, preact_far)[index * chunk // inner_part][place, start : start + chunk] = (
                grad * slope_ref[:, columns].astype(f32)
            ).astype(bf16)
        normed_grad = resid_two
        for index in range(units // chunk):
            start = index * chunk % inner_part
            block = (preact_near, preact_far)[index * chunk // inner_part]
            normed_grad = normed_grad + dot_nt(
                block[place, start : start + chunk], inner_chunk(index)
            )
        resid_one = norm_rows_back(normed_grad, unit_one, inverse_one, gains[0:1, :])
        resid_ref[place, :] = resid_one
        attend_grad = resid_one.astype(bf16)
        attend_ref[place, :] = attend_grad
        context_grad = jnp.concatenate(
            [dot_nt(attend_grad, own[:part, :]), dot_nt(attend_grad, other[:part, :])], axis=1
        ).astype(bf16)
        context_grad_ref[place, :] = context_grad
        high, low = split_two(context_grad.astype(f32) * context.astype(f32))
        delta = dot_nn(high, chooser) + dot_nn(low, chooser)
        delta_ref[place, :] = three_way(delta, lax.broadcasted_iota(jnp.int32, (tile, 128), 1))
        add(1, normed_grad * unit_one)
        add(2, upstream * unit_two)
        add(3, normed_grad)
        add(4, upstream)
        add(5, resid_one)
        add(6, resid_two)
        for index, block in enumerate((preact_near, preact_far)):
            columns = slice(index * inner_part, (index + 1) * inner_part)
            inner_sum_ref[0:1, columns] += jnp.sum(
                block[place, :].astype(f32), axis=0, keepdims=True
            )
        return carry

    lax.fori_loop(0, tiles, one_tile, 0)
    grads_send[:inner_part, :] = dot_tn(active_far[...], feed_ref[...]).astype(bf16)
    for index in range(inner_part // chunk):
        start = index * chunk
        grads_send[inner_part + index * width : inner_part + (index + 1) * width, :] = dot_tn(
            normed_ref[...], preact_far[:, start : start + chunk]
        ).astype(bf16)
    grads_send[2 * inner_part :, :] = dot_tn(context_ref[:, part:], attend_ref[...]).astype(bf16)


def attend_backward(
    facts, query_ref, key_ref, value_ref, lse_ref, context_grad_ref, delta_ref,
    token_ref, resid_ref, own, other, table, series_own, sums_ref, inner_sum_ref,
    attend_own, send, series_near, series_far, near_out, far_out,
    dquery_ref, dkey_ref, dvalue_ref,
):
    rows, width = query_ref.shape
    head_dim = width // HEADS
    half, history = series_own.shape
    part = width // 2
    position, count = lax.axis_index("mp"), facts[0:1, 0:1]
    lane = lax.broadcasted_iota(jnp.int32, (rows, 128), 1)
    dead = row_number(rows, position) >= count
    last = lax.rem(lane, 64) == 63
    spread = part_spreader(-1.0)
    extra_query = jnp.where(
        last, 1.0, dot_tn(jnp.concatenate(three_parts(lse_ref[...]), axis=0), spread)
    ).astype(bf16)
    extra_key = jnp.where(last & dead, -1e30, 0.0)
    extra_grad = delta_ref[...]
    nothing = jnp.zeros((rows, 128), bf16)

    def pair(index, carry):
        columns = pl.ds(pl.multiple_of(index * 128, 128), 128)
        queries = query_ref[:, columns]
        keys = key_ref[:, columns]
        values = value_ref[:, columns]
        grads = context_grad_ref[:, columns]
        softs, score_grads, own_grads, own_queries, own_keys = [], [], [], [], []
        for side in range(2):
            mine = (lane >= head_dim) if side else (lane < head_dim)
            hot = lax.rem(lane, 64) // 3 == index * 2 + side
            soft = jnp.exp2(
                dot_nt(
                    jnp.where(mine, keys, jnp.where(hot, 1.0, extra_key).astype(bf16)),
                    jnp.where(mine, queries, extra_query),
                )
            )
            centered = dot_nt(
                jnp.where(mine, values, jnp.where(hot, 1.0, 0.0).astype(bf16)),
                jnp.where(mine, grads, extra_grad),
            )
            softs.append(soft.astype(bf16))
            score_grads.append((soft * centered).astype(bf16))
            own_grads.append(jnp.where(mine, grads, nothing))
            own_queries.append(jnp.where(mine, queries, nothing))
            own_keys.append(jnp.where(mine, keys, nothing))
        dvalue = dot_nn(jnp.concatenate(softs, axis=1), jnp.concatenate(own_grads, axis=0))
        dkey = dot_nn(jnp.concatenate(score_grads, axis=1), jnp.concatenate(own_queries, axis=0))
        dquery = dot_tn(jnp.concatenate(own_keys, axis=0), jnp.concatenate(score_grads, axis=0))
        dvalue_ref[:, columns] = dvalue.astype(bf16)
        dkey_ref[:, columns] = (dkey * ln_two).astype(bf16)
        dquery_ref[:, columns] = (dquery.T * head_dim**-0.5).astype(bf16)
        return carry

    lax.fori_loop(0, width // 128, pair, 0)

    tokens = token_ref[...]
    total = resid_ref[...]
    near_out[...] = jnp.zeros_like(near_out)
    far_out[...] = jnp.zeros_like(far_out)
    for kind, grad_ref in enumerate((dquery_ref, dkey_ref, dvalue_ref)):
        low = grad_ref[...]
        attend_own[kind] = dot_tn(tokens, low[:, :part])
        far = dot_tn(tokens, low[:, part:]).astype(bf16)
        send[kind * part : (kind + 1) * part, :part] = far[:part]
        send[kind * part : (kind + 1) * part, part:] = far[part:]
        total = (
            total
            + dot_nt(low[:, :part], attend_block(own, half, kind))
            + dot_nt(low[:, part:], attend_block(other, half, kind))
        )
        if kind != 1:
            column = jnp.sum(low.astype(f32), axis=0, keepdims=True)
            start = kind // 2 * part
            near_out[7:8, start : start + part] = column[:, :part]
            far_out[7:8, start : start + part] = column[:, part:]
    low = total.astype(bf16)
    series_near[...] = dot_nt(low[:half], table[...])
    series_far[...] = dot_nt(low[half:], table[...])
    table_grad = dot_tn(series_own[...], low[:half]) + dot_tn(other[:half, :history], low[half:])
    row = lax.broadcasted_iota(jnp.int32, table_grad.shape, 0)
    seen = row >= facts[1:2, 0:1]
    send[3 * part :, :] = jnp.where(seen, table_grad, 0.0).astype(bf16)
    shared = sums_ref[0:7, :]
    bias_grad = jnp.sum(low.astype(f32), axis=0, keepdims=True)
    near_out[0:7, :] = shared
    far_out[0:7, :] = shared
    near_out[0:1, :] = bias_grad
    far_out[0:1, :] = bias_grad
    count_near = inner_sum_ref.shape[1] // 2 // width
    for index in range(count_near):
        near_out[8 + index : 9 + index, :] = inner_sum_ref[0:1, index * width : (index + 1) * width]
        far_out[8 + index : 9 + index, :] = inner_sum_ref[
            0:1, (count_near + index) * width : (count_near + index + 1) * width
        ]


def left_product(start, matrix):
    both = dot_nt(jnp.concatenate(split_two(start), axis=0), matrix.astype(bf16))
    return both[:8] + both[8:]


def right_product(basis, matrix):
    both = dot_nn(jnp.concatenate(split_two(basis), axis=0), matrix.astype(bf16))
    return both[:8] + both[8:]


def feed_matrices(
    active_ref, preact_ref, normed_ref, feed_ref, context_ref, attend_ref, received,
    e_outer, e_inner, e_mixer, s_outer, s_inner, s_mixer, output_near, output_far,
    outer, inner, mixer, left, output,
):
    width = feed_ref.shape[1]
    inner_part = outer.shape[0]
    part = mixer.shape[0]
    chunk = 512
    join_pair(output_near, output_far, output)
    outer[...] = (
        dot_tn(active_ref[...], feed_ref[...])
        + received[:inner_part, :].astype(f32)
        + e_outer[...]
    )
    for index in range(inner_part // chunk):
        columns = slice(index * chunk, (index + 1) * chunk)
        start = inner_part + index * width
        inner[:, columns] = (
            dot_tn(normed_ref[...], preact_ref[:, columns])
            + received[start : start + width, :].astype(f32)
            + e_inner[:, columns]
        )
    mixer[...] = (
        dot_tn(context_ref[:, :part], attend_ref[...])
        + received[2 * inner_part :, :].astype(f32)
        + e_mixer[...]
    )
    left[:, 0:1024] = left_product(s_outer[...], outer[...])
    left[:, 1024:1536] = left_product(s_inner[...], inner[...])
    left[:, 1536:1792] = left_product(s_mixer[...], mixer[...])


def orthonormal_rows(blocks):
    rows = [lax.broadcasted_iota(jnp.int32, block.shape, 0) for block in blocks]
    for index in range(blocks[0].shape[0]):
        pivots = [block[index : index + 1, :] for block in blocks]
        inners = [jnp.sum(block * pivot, axis=1, keepdims=True) for block, pivot in zip(blocks, pivots)]
        sizes = [inner[index : index + 1, :] + 1e-12 for inner in inners]
        blocks = [
            jnp.where(
                row > index,
                block - pivot * (inner / size),
                jnp.where(row == index, block * lax.rsqrt(size), block),
            )
            for block, row, pivot, inner, size in zip(blocks, rows, pivots, inners, sizes)
        ]
    return blocks


def reduce_factors(
    replicas, facts, near_attend, own, received, e_attend, e_embed, s_attend, s_embed, left_part,
    near, far, outer, inner, mixer,
    left_ref, right_ref, mean_ref, attend, embed,
    start_ref, summed, partial, gathered, parts_one, parts_two, send_sems, recv_sems,
):
    me = lax.axis_index("dp")
    barrier = pltpu.get_barrier_semaphore()
    chunk = start_ref.shape[1] // replicas
    share = 1.0 / replicas

    paired = replicas & (replicas - 1) == 0

    def peer(offset):
        return jnp.bitwise_xor(me, offset) if paired else lax.rem(me + offset, replicas)

    def source_of(offset):
        return jnp.bitwise_xor(me, offset) if paired else lax.rem(me - offset + replicas, replicas)

    def columns(index):
        return pl.ds(pl.multiple_of(index * chunk, 128), chunk)

    far_first = sorted(
        range(1, min(replicas, 17)), key=lambda k: -((k & 1) + (k >> 1 & 1) + (k >> 2))
    )

    def each(what):
        if replicas <= 16:
            for offset in far_first:
                what(offset)
            return

        def body(index, carry):
            what(replicas - index)
            return carry

        lax.fori_loop(1, replicas, body, 0)

    each(
        lambda offset: pl.semaphore_signal(
            barrier, inc=1, device_id={"dp": peer(offset)}, device_id_type=pl.DeviceIdType.MESH
        )
    )
    part = near_attend.shape[2]
    total = None
    for kind in range(3):
        rows = slice(kind * part, (kind + 1) * part)
        block = jnp.concatenate([received[rows, :part], received[rows, part:]], axis=0)
        attend[kind] = near_attend[kind] + block.astype(f32) + e_attend[kind]
        term = left_product(s_attend[kind], attend[kind])
        total = term if total is None else total + term
    mine, theirs = facts[2:3, 0:1], facts[3:4, 0:1]
    table_near = own[3 * part :, :].astype(f32)
    table_far = received[3 * part :, :].astype(f32)
    pieces = []
    for group in range(embed.shape[0]):
        grad = jnp.where(mine == group, table_near, 0.0) + jnp.where(theirs == group, table_far, 0.0)
        embed[group] = grad + e_embed[group]
        pieces.append(left_product(s_embed[...], embed[group]))
    used = embed.shape[0] * embed.shape[1]
    start_ref[:, 0:1024] = jnp.concatenate(pieces + [jnp.zeros((8, 1024 - used), f32)], axis=1)
    start_ref[:, 1024:2048] = left_part[:, 0:1024]
    start_ref[:, 2048:2560] = total
    start_ref[:, 2560:3328] = left_part[:, 1024:1792]
    common = near[1:7, :] + far[1:7, :]
    row = lax.broadcasted_iota(jnp.int32, (3, near.shape[1]), 0)
    bias = jnp.where(row == mine, near[0:1, :], 0.0) + jnp.where(row == theirs, far[0:1, :], 0.0)
    start_ref[:, 3328:3840] = jnp.concatenate([bias, common[:5]], axis=0)
    rest = jnp.concatenate([common[5:6], near[7:10, :] + far[7:10, :]], axis=0)
    for row in range(4):
        start_ref[2 * row : 2 * row + 1, 3840:4096] = rest[row : row + 1, :256]
        start_ref[2 * row + 1 : 2 * row + 2, 3840:4096] = rest[row : row + 1, 256:]
    if start_ref.shape[1] > 4096:
        start_ref[:, 4096:] = jnp.zeros((8, start_ref.shape[1] - 4096), f32)
    pl.semaphore_wait(barrier, replicas - 1)

    def all_sum(phase, source, parts, result):
        def scatter(offset):
            other = peer(offset)
            return pltpu.make_async_remote_copy(
                src_ref=source.at[:, columns(other)],
                dst_ref=parts.at[offset],
                send_sem=send_sems.at[2 * phase, offset],
                recv_sem=recv_sems.at[2 * phase, offset],
                device_id={"dp": other},
                device_id_type=pl.DeviceIdType.MESH,
            )

        def spread(offset, owner):
            return pltpu.make_async_remote_copy(
                src_ref=result.at[:, columns(owner)],
                dst_ref=result.at[:, columns(owner)],
                send_sem=send_sems.at[2 * phase + 1, offset],
                recv_sem=recv_sems.at[2 * phase + 1, offset],
                device_id={"dp": peer(offset)},
                device_id_type=pl.DeviceIdType.MESH,
            )

        each(lambda offset: scatter(offset).start())

        def collect(offset, total):
            scatter(offset).wait_recv()
            return total + parts[offset]

        total = source[:, columns(me)]
        if replicas <= 16:
            for offset in range(1, replicas):
                total = collect(offset, total)
        else:
            total = lax.fori_loop(1, replicas, collect, total)
        result[:, columns(me)] = total * share
        each(lambda offset: spread(offset, me).start())
        each(lambda offset: spread(offset, source_of(offset)).wait_recv())
        each(lambda offset: scatter(offset).wait_send())
        each(lambda offset: spread(offset, me).wait_send())

    all_sum(0, start_ref, parts_one, summed)
    mean_ref[...] = summed[:, 3328:4096]
    places = ((0, 1024), (1024, 1024), (2048, 512), (2560, 512), (3072, 256))
    bases = orthonormal_rows([summed[:, start : start + size] for start, size in places])
    for (start, size), basis in zip(places, bases):
        left_ref[:, start : start + size] = basis
    height = embed.shape[1]
    total = None
    for group in range(embed.shape[0]):
        term = right_product(bases[0][:, group * height : (group + 1) * height], embed[group])
        total = term if total is None else total + term
    partial[:, 0:512] = total
    partial[:, 512:1024] = right_product(bases[1], outer[...])
    for kind in range(3):
        partial[:, 1024 + kind * 256 : 1280 + kind * 256] = right_product(bases[2], attend[kind])
    partial[:, 1792:2816] = right_product(bases[3], inner[...])
    partial[:, 2816:3328] = right_product(bases[4], mixer[...])
    partial[:, 3328:] = jnp.zeros((8, partial.shape[1] - 3328), f32)
    all_sum(1, partial, parts_two, gathered)
    right_ref[...] = gathered[:, :3328]


def renew_all(
    step_rate, mixer_rate, left, right, mean, series_near, series_far, *refs,
):
    matrices, weights, moments = refs[0:5], refs[5:10], refs[10:15]
    vectors, vector_moments = refs[15:20], refs[20:25]
    errors, new_weights, new_moments = refs[25:30], refs[30:35], refs[35:40]
    new_vectors, new_vector_moments = refs[40:45], refs[45:50]
    lefts, rights, series_grad = refs[50:55], refs[55:60], refs[60]
    step = pl.program_id(0)
    join_pair(series_near, series_far, series_grad)

    def approx(basis, factor):
        left_high, left_low = split_two(basis)
        right_high, right_low = split_two(factor)
        return dot_tn(
            jnp.concatenate([left_high, left_low, left_high, left_low], axis=0),
            jnp.concatenate([right_high, right_high, right_low, right_low], axis=0),
        )

    def write(index, where, update, rate):
        errors[index][where] = matrices[index][where] - update
        moment = momentum_decay * moments[index][where] + update
        new_moments[index][where] = moment
        new_weights[index][where] = weights[index][where] - rate * moment

    def cut(start, size):
        return pl.ds(pl.multiple_of(start + step * size, 128), size)

    every = (slice(None), slice(None))
    groups, height, block = matrices[0].shape
    factor = right[:, cut(0, block)]
    for group in range(groups):
        write(
            0, (group, slice(None), slice(None)),
            approx(left[:, group * height : (group + 1) * height], factor), step_rate,
        )
    write(1, every, approx(left[:, cut(1024, matrices[1].shape[0])], right[:, 512:1024]), step_rate)
    basis = left[:, cut(2048, matrices[2].shape[1])]
    for kind in range(3):
        write(
            2, (kind, slice(None), slice(None)),
            approx(basis, right[:, 1024 + kind * 256 : 1280 + kind * 256]), step_rate,
        )
    write(3, every, approx(left[:, cut(2560, matrices[3].shape[0])], right[:, 1792:2816]), step_rate)
    write(4, every, approx(left[:, 3072:3328], right[:, cut(2816, matrices[4].shape[1])]), mixer_rate)

    @pl.when(step == 0)
    def _():
        for group in range(groups):
            lefts[0][group] = left[:, group * height : (group + 1) * height]
        lefts[1][...] = left[:, 1024:2048]
        lefts[2][...] = left[:, 2048:2560]
        lefts[3][...] = left[:, 2560:3072]
        lefts[4][...] = left[:, 3072:3328]
        rights[0][...] = right[:, 0:512]
        rights[1][...] = right[:, 512:1024]
        for kind in range(3):
            rights[2][kind] = right[:, 1024 + kind * 256 : 1280 + kind * 256]
        rights[3][...] = right[:, 1792:2816]
        rights[4][...] = right[:, 2816:3328]

        def renew(index, rows, columns, gradient):
            moment = momentum_decay * vector_moments[index][rows, columns] + gradient
            new_vector_moments[index][rows, columns] = moment
            new_vectors[index][rows, columns] = vectors[index][rows, columns] - step_rate * moment

        renew(0, slice(0, 3), slice(None), mean[0:3, :512])
        renew(1, slice(0, 2), slice(None), mean[3:5, :512])
        renew(2, slice(0, 3), slice(None), mean[5:8, :512])
        renew(2, slice(3, 4), slice(0, 256), mean[0:1, 512:])
        renew(2, slice(3, 4), slice(256, 512), mean[1:2, 512:])
        renew(3, slice(0, 1), slice(None), mean[2:3, 512:])
        renew(3, slice(1, 2), slice(None), mean[3:4, 512:])
        for index in range(4):
            renew(
                4, slice(0, 1), slice(index * 256, (index + 1) * 256),
                mean[4 + index : 5 + index, 512:],
            )


def call(kernel, outs, args, *, cost, in_specs=None, scratch=(), limit=32, name=None):
    return pl.pallas_call(
        kernel,
        out_shape=outs,
        in_specs=in_specs if in_specs is not None else [VM] * len(args),
        out_specs=jax.tree.map(lambda _: VM, outs),
        scratch_shapes=list(scratch),
        compiler_params=pltpu.CompilerParams(vmem_limit_bytes=limit * MIB),
        cost_estimate=estimate(cost),
        name=name,
    )(*args)


def estimate(microseconds):
    return pl.CostEstimate(
        flops=int(microseconds * 1e9), bytes_accessed=int(microseconds * 2e6), transcendentals=0
    )


def sds(shape, dtype=f32):
    return jax.ShapeDtypeStruct(shape, dtype)


def local(
    series, groups, counts, cotangent,
    embed_weight, embed_moment, embed_error, embed_start,
    attend_weight, attend_moment, attend_error, attend_start,
    mixer_weight, mixer_moment, mixer_error, mixer_start,
    inner_weight, inner_moment, inner_error, inner_start,
    outer_weight, outer_moment, outer_error, outer_start,
    embed_bias, embed_bias_moment, query_bias, query_bias_moment,
    inner_bias, inner_bias_moment, norm_gains, gains_moment, shared_biases, biases_moment,
):
    replicas = lax.axis_size("dp")
    half, windows, history = series.shape
    rows = 2 * half
    group_count, _, width = embed_weight.shape
    part = attend_weight.shape[2]
    inner_part = inner_weight.shape[1]
    units = 2 * inner_part
    turned = lambda a: a.transpose(1, 0, 2)

    def swap(values):
        return lax.ppermute(values, "mp", [(0, 1), (1, 0)])

    low = sds((rows, width), bf16)
    full = sds((rows, width))
    near = sds((half, width))
    packed = sds((half + 3 * part + 16, width), bf16)
    send_one, other_one, series_own, small, facts, send_two, cot_own = pl.pallas_call(
        prepare,
        out_shape=[
            packed, packed, sds((half, history), bf16), sds((8, inner_part)), sds((8, 128), jnp.int32),
            sds((part + 2 * inner_part + half, width), bf16), sds((half, width), bf16),
        ],
        in_specs=[HB] * 10,
        out_specs=[VM] * 7,
        scratch_shapes=[
            pltpu.SMEM(groups.shape, jnp.int32), pltpu.SMEM(counts.shape, jnp.int32),
            pltpu.VMEM(series.shape, bf16), pltpu.VMEM((3, width, part), f32),
            pltpu.VMEM(query_bias.shape, f32), pltpu.VMEM((1, inner_part), f32),
            pltpu.VMEM(cotangent.shape, bf16), pltpu.VMEM(mixer_weight.shape, f32),
            pltpu.VMEM(inner_weight.shape, f32), pltpu.VMEM(outer_weight.shape, f32),
            pltpu.SemaphoreType.DMA((10,)), pltpu.SemaphoreType.DMA((2,)), pltpu.SemaphoreType.DMA((2,)),
        ],
        compiler_params=pltpu.CompilerParams(
            collective_id=2, has_side_effects=True, vmem_limit_bytes=LIMITS[0] * MIB
        ),
        cost_estimate=estimate(7),
        name="prepare",
    )(
        *(
            pltpu.with_memory_space_constraint(a, pltpu.HBM)
            for a in (
                groups, counts, series, turned(attend_weight), query_bias, inner_bias[None],
                cotangent, mixer_weight, inner_weight, outer_weight,
            )
        )
    )
    other_two = swap(send_two)
    hidden, tokens, queries, keys, values, context, lse, small_other, table = call(
        attend_forward,
        [full, low, low, low, low, low, sds((HEADS, rows)), sds((8, inner_part)), sds((history, width), bf16)],
        (facts, series_own, embed_weight, embed_bias, send_one, other_one, small),
        limit=LIMITS[2], cost=15, scratch=[pltpu.VMEM((HEADS, rows), f32)],
        name="attend_forward",
    )
    (
        output_near, output_send, active, preact_grad, normed_low, feed_grad, attend_out, resid_one,
        context_grad, delta, sums, inner_sums, grads_send,
    ) = call(
        functools.partial(feed_forward, TILES),
        [near, near, sds((rows, inner_part), bf16), sds((rows, inner_part), bf16), low, low, low, full, low,
         sds((rows, 128), bf16), sds((8, width)), sds((8, units)),
         sds((2 * inner_part + part, width), bf16)],
        (facts, context, hidden, send_two, other_two, small, small_other, norm_gains, shared_biases, cot_own),
        limit=LIMITS[3], cost=22,
        scratch=[
            pltpu.VMEM((rows // TILES, units), bf16), pltpu.VMEM((rows, inner_part), bf16),
            pltpu.VMEM((rows, inner_part), bf16),
        ],
        name="feed_forward",
    )
    output_other = swap(output_send)
    grads_other = swap(grads_send)
    attend_near, send_three, series_near, series_far, sums_near, sums_far = call(
        attend_backward,
        [sds((3, width, part)), sds((3 * part + history, width), bf16), sds((half, history)),
         sds((half, history)), sds((16, width)), sds((16, width))],
        (facts, queries, keys, values, lse, context_grad, delta, tokens, resid_one, send_one,
         other_one, table, series_own, sums, inner_sums),
        limit=LIMITS[4], cost=22,
        scratch=[pltpu.VMEM((rows, width), bf16)] * 3,
        name="attend_backward",
    )
    other_three = swap(send_three)
    series_other = swap(series_far)
    sums_other = swap(sums_far)
    outer_matrix, inner_matrix, mixer_matrix, left_part, output = call(
        feed_matrices,
        [sds(outer_weight.shape), sds(inner_weight.shape), sds(mixer_weight.shape), sds((8, 1792)),
         sds((half, windows, width))],
        (active, preact_grad, normed_low, feed_grad, context, attend_out, grads_other,
         outer_error[0], inner_error[0], mixer_error[0], outer_start[0].T, inner_start.T, mixer_start[0].T,
         output_near, output_other),
        limit=LIMITS[5], cost=6,
        name="feed_matrices",
    )
    padded = max(128, -(-4096 // replicas // 128) * 128)
    total = padded * replicas
    left, right, mean, attend_matrix, embed_matrix = pl.pallas_call(
        functools.partial(reduce_factors, replicas),
        out_shape=[sds((8, 3328)), sds((8, 3328)), sds((8, 768)), sds((3, width, part)), sds(embed_weight.shape)],
        in_specs=[VM] * 14,
        out_specs=[VM] * 5,
        scratch_shapes=[
            pltpu.VMEM((8, total), f32), pltpu.VMEM((8, total), f32), pltpu.VMEM((8, total), f32),
            pltpu.VMEM((8, total), f32),
            pltpu.VMEM((replicas, 8, padded), f32), pltpu.VMEM((replicas, 8, padded), f32),
            pltpu.SemaphoreType.DMA((4, replicas)), pltpu.SemaphoreType.DMA((4, replicas)),
        ],
        compiler_params=pltpu.CompilerParams(
            collective_id=1, has_side_effects=True, vmem_limit_bytes=LIMITS[6] * MIB
        ),
        cost_estimate=estimate(30),
        name="reduce_factors",
    )(
        facts, attend_near, send_three, other_three, turned(attend_error[0]), embed_error[0],
        attend_start.transpose(0, 2, 1), embed_start.T, left_part, sums_near, sums_other,
        outer_matrix, inner_matrix, mixer_matrix,
    )
    matrices = (embed_matrix, outer_matrix, attend_matrix, inner_matrix, mixer_matrix)

    step_rate = base_rate * math.sqrt(replicas * 7 / (windows * rows))
    mixer_rate = step_rate * math.sqrt(width / max(width * 16 // rows, 1))
    steps = 4
    whole = lambda a: pl.BlockSpec(a.shape, lambda i: (0,) * len(a.shape))
    column = lambda a: pl.BlockSpec((a.shape[0], a.shape[1] // steps), lambda i: (0, i))
    row = lambda a: pl.BlockSpec((a.shape[0] // steps, a.shape[1]), lambda i: (i, 0))
    middle = lambda a: pl.BlockSpec((a.shape[0], a.shape[1] // steps, a.shape[2]), lambda i: (0, i, 0))
    last = lambda a: pl.BlockSpec((a.shape[0], a.shape[1], a.shape[2] // steps), lambda i: (0, 0, i))
    specs = [spec(a) for spec, a in zip((last, row, middle, row, column), matrices)]
    vectors = (embed_bias, norm_gains, shared_biases, query_bias, inner_bias[None])
    vector_moments = (
        embed_bias_moment, gains_moment, biases_moment, query_bias_moment, inner_bias_moment[None]
    )
    vector_specs = [whole(a) for a in vectors]
    split = pl.BlockSpec((half // steps, history), lambda i: (i, 0))
    split_out = pl.BlockSpec((half // steps, windows, history), lambda i: (i, 0, 0))
    factors = [
        sds((group_count, 8, history)), sds((8, 1024)), sds((8, 512)), sds((8, 512)), sds((8, 256)),
        sds((8, 512)), sds((8, 512)), sds((3, 8, part)), sds((8, 1024)), sds((8, 512)),
    ]
    found = pl.pallas_call(
        functools.partial(renew_all, step_rate, mixer_rate),
        grid=(steps,),
        out_shape=[sds(a.shape) for a in matrices] * 3 + [sds(a.shape) for a in vectors] * 2
        + factors + [sds(series.shape)],
        in_specs=[whole(left), whole(right), whole(mean), split, split] + specs * 3 + vector_specs * 2,
        out_specs=specs * 3 + vector_specs * 2 + [whole(a) for a in factors] + [split_out],
        compiler_params=pltpu.CompilerParams(vmem_limit_bytes=LIMITS[7] * MIB),
        cost_estimate=estimate(12),
        name="renew_all",
    )(
        left, right, mean, series_near, series_other, *matrices,
        embed_weight, outer_weight, turned(attend_weight), inner_weight, mixer_weight,
        embed_moment, outer_moment, turned(attend_moment), inner_moment, mixer_moment,
        *vectors, *vector_moments,
    )
    errors, weights, moments = found[0:5], found[5:10], found[10:15]
    new_vectors, new_vector_moments = found[15:20], found[20:25]
    lefts, rights = found[25:30], found[30:35]
    return (
        output,
        found[35],
        weights[0],
        moments[0],
        errors[0][None],
        lefts[0].transpose(0, 2, 1),
        rights[0].T,
        turned(weights[2]),
        turned(moments[2]),
        turned(errors[2])[None],
        lefts[2].T[None],
        rights[2].transpose(0, 2, 1),
        weights[4],
        moments[4],
        errors[4][None],
        lefts[4].T,
        rights[4].T[None],
        weights[3],
        moments[3],
        errors[3][None],
        lefts[3].T[None],
        rights[3].T,
        weights[1],
        moments[1],
        errors[1][None],
        lefts[1].T,
        rights[1].T[None],
        new_vector_moments[0],
        new_vectors[0],
        new_vector_moments[3],
        new_vectors[3],
        new_vector_moments[4][0],
        new_vectors[4][0],
        new_vector_moments[1],
        new_vectors[1],
        new_vector_moments[2],
        new_vectors[2],
    )


def solution(mesh):
    return jax.shard_map(
        local,
        mesh=mesh,
        in_specs=(
            P("mp", "dp", None),
            P("dp"),
            P("dp"),
            P("mp", "dp", None),
            P(),
            P(),
            P("dp", None, None, None),
            P(),
            P(None, None, "mp"),
            P(None, None, "mp"),
            P("dp", None, None, "mp"),
            P(None, "mp", None),
            P("mp", None),
            P("mp", None),
            P("dp", "mp", None),
            P("mp", None, None),
            P(None, "mp"),
            P(None, "mp"),
            P("dp", None, "mp"),
            P("mp", None),
            P("mp", None),
            P("mp", None),
            P("dp", "mp", None),
            P("mp", None, None),
            P(),
            P(),
            P(None, "mp"),
            P(None, "mp"),
            P("mp"),
            P("mp"),
            P(),
            P(),
            P(),
            P(),
        ),
        out_specs=(
            P("mp", "dp", None),
            P("mp", "dp", None),
            P(),
            P(),
            P("dp", None, None, None),
            P(),
            P(),
            P(None, None, "mp"),
            P(None, None, "mp"),
            P("dp", None, None, "mp"),
            P("mp", None, None),
            P(None, "mp", None),
            P("mp", None),
            P("mp", None),
            P("dp", "mp", None),
            P("mp", None),
            P("mp", None, None),
            P(None, "mp"),
            P(None, "mp"),
            P("dp", None, "mp"),
            P("mp", None, None),
            P("mp", None),
            P("mp", None),
            P("mp", None),
            P("dp", "mp", None),
            P("mp", None),
            P("mp", None, None),
            P(),
            P(),
            P(None, "mp"),
            P(None, "mp"),
            P("mp"),
            P("mp"),
            P(),
            P(),
            P(),
            P(),
        ),
        check_vma=False,
    )
```

```python
import functools
import math

import jax
import jax.numpy as jnp
from jax import lax
from jax.experimental import pallas as pl
from jax.experimental.pallas import tpu as pltpu
from jax.sharding import PartitionSpec as P

HEADS = 8
momentum_decay = 0.9
norm_epsilon = 1e-05
base_rate = 0.03
inverse_root_two = 0.7071067811865476
inverse_root_tau = 0.3989422804014327
log2_e = 1.4426950408889634
ln_two = 0.6931471805599453
f32 = jnp.float32
bf16 = jnp.bfloat16
VMEM = pltpu.VMEM
VM = pl.BlockSpec(memory_space=pltpu.VMEM)
HB = pl.BlockSpec(memory_space=pltpu.HBM)
MIB = 1024 * 1024


def dot_nn(a, b):
    return lax.dot_general(a, b, (((1,), (0,)), ((), ())), preferred_element_type=f32)


def dot_nt(a, b):
    return lax.dot_general(a, b, (((1,), (1,)), ((), ())), preferred_element_type=f32)


def dot_tn(a, b):
    return lax.dot_general(a, b, (((0,), (0,)), ((), ())), preferred_element_type=f32)


def split_two(x):
    high = x.astype(bf16)
    return high, (x - high.astype(f32)).astype(bf16)


def three_way(x, lane):
    high = x.astype(bf16).astype(f32)
    rest = x - high
    middle = rest.astype(bf16).astype(f32)
    last = rest - middle
    place = lax.rem(lax.rem(lane, 64), 3)
    return jnp.where(place == 0, high, jnp.where(place == 1, middle, last)).astype(bf16)


LIMITS = (12, 14, 12, 14, 16, 8, 8, 28)
TILES = 2


def row_number(rows, position):
    half = rows // 2
    index = lax.broadcasted_iota(jnp.int32, (rows, 128), 0)
    return jnp.where(index < half, index + position * half, index - half + (1 - position) * half)


def lookback_of(group, history):
    return jnp.where(
        group == 0, history * 2 // 7, jnp.where(group == 1, history * 4 // 7, history)
    ).astype(jnp.int32)


def take_window(pair_ref, window, home, columns):
    for index in range(2):

        @pl.when(window == index)
        def _(index=index):
            home[:, columns] = pair_ref[:, index, :]


def join_copies(mine, theirs, home, done):
    position = lax.axis_index("mp")
    return [
        pltpu.make_async_copy(source, home.at[:, window, :], done.at[index])
        for index, (source, window) in enumerate(((mine, position), (theirs, 1 - position)))
    ]


def three_parts(x):
    high = x.astype(bf16)
    rest = x - high.astype(f32)
    middle = rest.astype(bf16)
    return high, middle, (rest - middle.astype(f32)).astype(bf16)


def prepare(
    groups_hbm, counts_hbm, series_hbm, attend_hbm, query_bias_hbm, inner_bias_hbm,
    cot_hbm, mixer_hbm, inner_hbm, outer_hbm,
    send, received, series_own, small, facts, send_feed, cot_own,
    groups, counts, series, attend, query_bias, inner_bias, cotangent, mixer, inner, outer,
    done, send_sems, recv_sems,
):
    position = lax.axis_index("mp")
    partner = {"mp": 1 - position}
    barrier = pltpu.get_barrier_semaphore()
    pl.semaphore_signal(barrier, inc=1, device_id=partner, device_id_type=pl.DeviceIdType.MESH)
    copies = []
    for source, target in (
        (query_bias_hbm, query_bias), (inner_bias_hbm, inner_bias), (attend_hbm, attend),
        (series_hbm, series), (groups_hbm, groups), (counts_hbm, counts), (cot_hbm, cotangent),
        (mixer_hbm, mixer), (inner_hbm, inner), (outer_hbm, outer),
    ):
        copies.append(pltpu.make_async_copy(source, target, done.at[len(copies)]))
        copies[-1].start()
    half, _, history = series.shape
    width = send.shape[1]
    depth = attend.shape[1] // 2
    end = half + 3 * depth
    part = query_bias.shape[1]
    trades = [
        pltpu.make_async_remote_copy(
            src_ref=send.at[rows], dst_ref=received.at[rows], send_sem=send_sems.at[index],
            recv_sem=recv_sems.at[index], device_id=partner, device_id_type=pl.DeviceIdType.MESH,
        )
        for index, rows in enumerate((slice(half, end + 16), slice(0, half)))
    ]
    copies[0].wait()
    copies[1].wait()
    small[...] = jnp.zeros_like(small)
    small[0:2, :part] = query_bias[...]
    small[2:3, :] = inner_bias[...]
    values = jnp.concatenate(
        [
            jnp.concatenate([query_bias[0:1, :], query_bias[1:2, :]], axis=1),
            inner_bias[:, :width],
            inner_bias[:, width:],
            jnp.zeros((1, width), f32),
        ],
        axis=0,
    )
    send[end : end + 16, :] = jnp.concatenate(
        [*three_parts(values), jnp.zeros((4, width), bf16)], axis=0
    )
    copies[2].wait()
    for kind in range(3):
        rows = slice(half + kind * depth, half + (kind + 1) * depth)
        send[rows, :256] = attend[kind, :depth, :].astype(bf16)
        send[rows, 256:] = attend[kind, depth:, :].astype(bf16)
    pl.semaphore_wait(barrier, 1)
    trades[0].start()
    send[:half, 256:] = jnp.zeros((half, width - 256), bf16)
    copies[3].wait()
    take_window(series, 1 - position, send.at[:half], slice(0, history))
    trades[1].start()
    take_window(series, position, series_own, slice(None))
    copies[4].wait()
    copies[5].wait()
    group = jnp.where(position == 0, groups[0], groups[1])
    other_group = jnp.where(position == 0, groups[1], groups[0])
    count = jnp.where(position == 0, counts[0], counts[1])
    first = history - lookback_of(group, history)
    row = lax.broadcasted_iota(jnp.int32, facts.shape, 0)
    facts[...] = jnp.where(
        row == 0, count, jnp.where(row == 1, first, jnp.where(row == 2, group, other_group))
    )
    m, d, o = mixer.shape[0], inner.shape[0], outer.shape[0]
    copies[6].wait()
    take_window(cotangent, 1 - position, send_feed.at[m + 2 * d + o :], slice(None))
    take_window(cotangent, position, cot_own, slice(None))
    copies[7].wait()
    send_feed[:m] = mixer[...].astype(bf16)
    copies[8].wait()
    send_feed[m : m + d] = inner[:, :512].astype(bf16)
    send_feed[m + d : m + 2 * d] = inner[:, 512:].astype(bf16)
    copies[9].wait()
    send_feed[m + 2 * d : m + 2 * d + o] = outer[...].astype(bf16)
    for trade in trades:
        trade.wait()


def unpack_small(other, small_other):
    part = other.shape[1] // 2
    parts = other[other.shape[0] - 16 :, :].astype(f32)
    values = parts[0:4] + parts[4:8] + parts[8:12]
    small_other[0:1, :part] = values[0:1, :part]
    small_other[1:2, :part] = values[0:1, part:]
    small_other[2:3, : 2 * part] = values[1:2, :]
    small_other[2:3, 2 * part :] = values[2:3, :]


def attend_block(pack, half, kind):
    start = half + kind * 256
    return jnp.concatenate([pack[start : start + 256, :256], pack[start : start + 256, 256:]], axis=0)


def attend_forward(
    facts, series_own, embed, embed_bias, own, other, small,
    hidden_ref, token_ref, query_ref, key_ref, value_ref, context_ref, lse_ref, small_other, table, peak_ref,
):
    unpack_small(other, small_other)
    chosen, bias_row = embed[0], embed_bias[0:1, :]
    for group in range(1, embed.shape[0]):
        here = facts[2:3, 0:1] == group
        chosen = jnp.where(here, embed[group], chosen)
        bias_row = jnp.where(here, embed_bias[group : group + 1, :], bias_row)
    row = lax.broadcasted_iota(jnp.int32, chosen.shape, 0)
    table[...] = jnp.where(row >= facts[1:2, 0:1], chosen, 0.0).astype(bf16)
    rows, width = hidden_ref.shape
    half, history = series_own.shape
    part = width // 2
    head_dim = width // HEADS
    position, count = lax.axis_index("mp"), facts[0:1, 0:1]
    for index, block in enumerate((series_own[...], other[:half, :history])):
        values = dot_nn(block, table[...]) + bias_row
        hidden_ref[pl.ds(index * half, half), :] = values
        token_ref[pl.ds(index * half, half), :] = values.astype(bf16)
    scale = head_dim**-0.5 * log2_e
    tokens = token_ref[...]
    for index, (pack, bias) in enumerate(((own, small), (other, small_other))):
        columns = pl.ds(index * part, part)
        query_ref[:, columns] = (
            (dot_nn(tokens, attend_block(pack, half, 0)) + bias[0:1, :part]) * scale
        ).astype(bf16)
        key_ref[:, columns] = dot_nn(tokens, attend_block(pack, half, 1)).astype(bf16)
        value_ref[:, columns] = (
            dot_nn(tokens, attend_block(pack, half, 2)) + bias[1:2, :part]
        ).astype(bf16)
    lane = lax.broadcasted_iota(jnp.int32, (rows, 128), 1)
    dead = row_number(rows, position) >= count
    last = lax.rem(lane, 64) == 63
    extra_query = jnp.where(last, 1.0, 0.0).astype(bf16)
    extra_key = jnp.where(last & dead, -1e30, 0.0).astype(bf16)
    ones = jnp.ones((rows, 128), bf16)

    chooser = head_chooser(width, head_dim, 1.0)

    def longest(ref):
        values = ref[...].astype(f32)
        return jnp.max(dot_nn((values * values).astype(bf16), chooser), axis=0, keepdims=True)

    bound = jnp.max(longest(query_ref) * longest(key_ref))
    peak_ref[...] = jnp.zeros_like(peak_ref)

    @pl.when(jnp.logical_not(bound < 3600.0))
    def _():
        block = 128
        block_lane = lane[:block]

        def one_head(head, carry):
            columns = pl.ds(pl.multiple_of(head // 2 * 128, 128), 128)
            side = lax.rem(head, 2)
            query = jnp.where((lane // head_dim) == side, query_ref[:, columns], extra_query)

            def one_block(index, peak):
                place = pl.ds(pl.multiple_of(index * block, block), block)
                keys = key_ref[place, columns]
                far = lax.broadcasted_iota(jnp.int32, (block, 128), 0) + index * block
                near = jnp.where(
                    far < half, far + position * half, far - half + (1 - position) * half
                )
                mask = jnp.where(
                    (lax.rem(block_lane, 64) == 63) & (near >= count), -1e30, 0.0
                ).astype(bf16)
                scores = dot_nt(jnp.where((block_lane // head_dim) == side, keys, mask), query)
                return jnp.maximum(peak, jnp.max(scores, axis=0, keepdims=True))

            peak_ref[pl.ds(head, 1), :] = lax.fori_loop(
                0, rows // block, one_block, jnp.full((1, rows), -1e30, f32)
            )
            return carry

        lax.fori_loop(0, HEADS, one_head, 0)

    spread = part_spreader(-1.0)
    extra_query = jnp.where(
        last, 1.0, dot_tn(jnp.concatenate(three_parts(peak_ref[...]), axis=0), spread)
    ).astype(bf16)
    extra_key = jnp.where(last & dead, -1e30, 0.0)

    def pair(index, carry):
        columns = pl.ds(pl.multiple_of(index * 128, 128), 128)
        queries = query_ref[:, columns]
        keys = key_ref[:, columns]
        values = value_ref[:, columns]
        found = []
        for side in range(2):
            mine = (lane >= head_dim) if side else (lane < head_dim)
            hot = lax.rem(lane, 64) // 3 == index * 2 + side
            scores = dot_nt(
                jnp.where(mine, keys, jnp.where(hot, 1.0, extra_key).astype(bf16)),
                jnp.where(mine, queries, extra_query),
            )
            soft = jnp.exp2(scores).astype(bf16)
            mixed = dot_tn(jnp.where(mine, values, ones), soft)
            top, bottom = mixed[:head_dim], mixed[head_dim:]
            wanted, total = (bottom, top) if side else (top, bottom)
            found.append(wanted / total)
            place = pl.ds(index * 2 + side, 1)
            lse_ref[place, :] = jnp.log2(total[0:1]) + peak_ref[place, :]
        context_ref[:, columns] = jnp.concatenate(found, axis=0).T.astype(bf16)
        return carry

    lax.fori_loop(0, width // 128, pair, 0)


def part_spreader(value):
    row = lax.broadcasted_iota(jnp.int32, (3 * HEADS, 128), 0)
    lane = lax.broadcasted_iota(jnp.int32, (3 * HEADS, 128), 1)
    head = lax.rem(row, HEADS)
    wanted = lane == jnp.where(lax.rem(head, 2) == 0, 64, 0) + 3 * head + row // HEADS
    return jnp.where(wanted, value, 0.0).astype(bf16)


def head_chooser(width, head_dim, value):
    head = lax.broadcasted_iota(jnp.int32, (width, 128), 0) // head_dim
    lane = lax.broadcasted_iota(jnp.int32, (width, 128), 1)
    wanted = (lax.rem(lane, 64) // 3 == head) & ((lane >= 64) == (lax.rem(head, 2) == 0))
    return jnp.where(wanted, value, 0.0).astype(bf16)


def norm_rows(values, gain, shift):
    centered = values - jnp.mean(values, axis=-1, keepdims=True)
    inverse = lax.rsqrt(jnp.mean(centered * centered, axis=-1, keepdims=True) + norm_epsilon)
    unit = centered * inverse
    return unit * gain + shift, unit, inverse


def norm_rows_back(upstream, unit, inverse, gain):
    scaled = upstream * gain
    return inverse * (
        scaled
        - jnp.mean(scaled, axis=-1, keepdims=True)
        - unit * jnp.mean(scaled * unit, axis=-1, keepdims=True)
    )


def feed_forward(
    tiles, facts, context_ref, hidden_ref, own, other, small, small_other, gains, biases, cot_own,
    output_ref, output_send, active_near, preact_near, normed_ref, feed_ref, attend_ref, resid_ref,
    context_grad_ref, delta_ref, sums_ref, inner_sum_ref, grads_send, slope_ref, active_far, preact_far,
):
    rows, width = hidden_ref.shape
    tile = rows // tiles
    half = rows // 2
    part = width // 2
    inner_part = active_near.shape[1]
    units = 2 * inner_part
    chunk = 512
    position, count = lax.axis_index("mp"), facts[0:1, 0:1]
    sums_ref[...] = jnp.zeros_like(sums_ref)
    inner_sum_ref[...] = jnp.zeros_like(inner_sum_ref)
    at_inner = part
    at_outer = part + inner_part
    at_cot = at_outer + inner_part

    def inner_chunk(index):
        pack = (own, other)[index * chunk // inner_part]
        start = at_inner + (index * chunk % inner_part) // chunk * width
        return pack[start : start + width, :]

    def outer_chunk(index):
        pack = (own, other)[index * chunk // inner_part]
        start = at_outer + index * chunk % inner_part
        return pack[start : start + chunk, :]

    head_dim = width // HEADS
    chooser = head_chooser(width, head_dim, -1.0)

    def add(row, values):
        sums_ref[row : row + 1, :] += jnp.sum(values, axis=0, keepdims=True)

    def one_tile(step, carry):
        place = pl.ds(pl.multiple_of(step * tile, tile), tile)
        context = context_ref[place, :]
        attended = dot_nn(context[:, :part], own[:part, :]) + dot_nn(
            context[:, part:], other[:part, :]
        )
        normed, unit_one, inverse_one = norm_rows(
            hidden_ref[place, :] + attended + biases[2:3, :], gains[0:1, :], biases[0:1, :]
        )
        normed_low = normed.astype(bf16)
        normed_ref[place, :] = normed_low
        for index in range(units // chunk):
            columns = slice(index * chunk, (index + 1) * chunk)
            bias = (small, small_other)[index * chunk // inner_part]
            start = index * chunk % inner_part
            preact = dot_nn(normed_low, inner_chunk(index)) + bias[2:3, start : start + chunk]
            phi = 0.5 + 0.5 * lax.erf(preact * inverse_root_two)
            (active_near, active_far)[index * chunk // inner_part][place, start : start + chunk] = (preact * phi).astype(bf16)
            slope_ref[:, columns] = (
                phi + preact * jnp.exp2(preact * preact * (-0.5 * log2_e)) * inverse_root_tau
            ).astype(bf16)
        feed_out = dot_nn(active_near[place, :], own[at_outer:at_cot, :]) + dot_nn(
            active_far[place, :], other[at_outer:at_cot, :]
        )
        output, unit_two, inverse_two = norm_rows(
            normed + feed_out + biases[3:4, :], gains[1:2, :], biases[1:2, :]
        )
        index = lax.broadcasted_iota(jnp.int32, (tile, width), 0)

        @pl.when(step < tiles // 2)
        def _():
            output_ref[place, :] = output
        far = step - tiles // 2
        far_place = pl.ds(pl.multiple_of(jnp.maximum(far, 0) * tile, tile), tile)
        near_place = pl.ds(pl.multiple_of(jnp.minimum(step, tiles // 2 - 1) * tile, tile), tile)

        @pl.when(step >= tiles // 2)
        def _():
            output_send[far_place, :] = output
        cot = jnp.where(
            step < tiles // 2,
            cot_own[near_place, :],
            other[pl.ds(pl.multiple_of(at_cot + jnp.maximum(far, 0) * tile, 32), tile), :],
        ).astype(f32)
        first = jnp.where(
            step < tiles // 2,
            position * half + step * tile,
            (1 - position) * half + far * tile,
        )
        upstream = jnp.where(index + first < count, cot, 0.0)
        resid_two = norm_rows_back(upstream, unit_two, inverse_two, gains[1:2, :])
        feed_grad = resid_two.astype(bf16)
        feed_ref[place, :] = feed_grad
        for index in range(units // chunk):
            columns = slice(index * chunk, (index + 1) * chunk)
            grad = dot_nt(feed_grad, outer_chunk(index))
            start = index * chunk % inner_part
            (preact_near, preact_far)[index * chunk // inner_part][place, start : start + chunk] = (
                grad * slope_ref[:, columns].astype(f32)
            ).astype(bf16)
        normed_grad = resid_two
        for index in range(units // chunk):
            start = index * chunk % inner_part
            block = (preact_near, preact_far)[index * chunk // inner_part]
            normed_grad = normed_grad + dot_nt(
                block[place, start : start + chunk], inner_chunk(index)
            )
        resid_one = norm_rows_back(normed_grad, unit_one, inverse_one, gains[0:1, :])
        resid_ref[place, :] = resid_one
        attend_grad = resid_one.astype(bf16)
        attend_ref[place, :] = attend_grad
        context_grad = jnp.concatenate(
            [dot_nt(attend_grad, own[:part, :]), dot_nt(attend_grad, other[:part, :])], axis=1
        ).astype(bf16)
        context_grad_ref[place, :] = context_grad
        high, low = split_two(context_grad.astype(f32) * context.astype(f32))
        delta = dot_nn(high, chooser) + dot_nn(low, chooser)
        delta_ref[place, :] = three_way(delta, lax.broadcasted_iota(jnp.int32, (tile, 128), 1))
        add(1, normed_grad * unit_one)
        add(2, upstream * unit_two)
        add(3, normed_grad)
        add(4, upstream)
        add(5, resid_one)
        add(6, resid_two)
        for index, block in enumerate((preact_near, preact_far)):
            columns = slice(index * inner_part, (index + 1) * inner_part)
            inner_sum_ref[0:1, columns] += jnp.sum(
                block[place, :].astype(f32), axis=0, keepdims=True
            )
        return carry

    lax.fori_loop(0, tiles, one_tile, 0)
    grads_send[:inner_part, :] = dot_tn(active_far[...], feed_ref[...]).astype(bf16)
    for index in range(inner_part // chunk):
        start = index * chunk
        grads_send[inner_part + index * width : inner_part + (index + 1) * width, :] = dot_tn(
            normed_ref[...], preact_far[:, start : start + chunk]
        ).astype(bf16)
    grads_send[2 * inner_part :, :] = dot_tn(context_ref[:, part:], attend_ref[...]).astype(bf16)


def attend_backward(
    facts, query_ref, key_ref, value_ref, lse_ref, context_grad_ref, delta_ref,
    token_ref, resid_ref, own, other, table, series_own, sums_ref, inner_sum_ref,
    attend_own, send, series_near, series_far, near_out, far_out,
    dquery_ref, dkey_ref, dvalue_ref,
):
    rows, width = query_ref.shape
    head_dim = width // HEADS
    half, history = series_own.shape
    part = width // 2
    position, count = lax.axis_index("mp"), facts[0:1, 0:1]
    lane = lax.broadcasted_iota(jnp.int32, (rows, 128), 1)
    dead = row_number(rows, position) >= count
    last = lax.rem(lane, 64) == 63
    spread = part_spreader(-1.0)
    extra_query = jnp.where(
        last, 1.0, dot_tn(jnp.concatenate(three_parts(lse_ref[...]), axis=0), spread)
    ).astype(bf16)
    extra_key = jnp.where(last & dead, -1e30, 0.0)
    extra_grad = delta_ref[...]
    nothing = jnp.zeros((rows, 128), bf16)

    def pair(index, carry):
        columns = pl.ds(pl.multiple_of(index * 128, 128), 128)
        queries = query_ref[:, columns]
        keys = key_ref[:, columns]
        values = value_ref[:, columns]
        grads = context_grad_ref[:, columns]
        softs, score_grads, own_grads, own_queries, own_keys = [], [], [], [], []
        for side in range(2):
            mine = (lane >= head_dim) if side else (lane < head_dim)
            hot = lax.rem(lane, 64) // 3 == index * 2 + side
            soft = jnp.exp2(
                dot_nt(
                    jnp.where(mine, keys, jnp.where(hot, 1.0, extra_key).astype(bf16)),
                    jnp.where(mine, queries, extra_query),
                )
            )
            centered = dot_nt(
                jnp.where(mine, values, jnp.where(hot, 1.0, 0.0).astype(bf16)),
                jnp.where(mine, grads, extra_grad),
            )
            softs.append(soft.astype(bf16))
            score_grads.append((soft * centered).astype(bf16))
            own_grads.append(jnp.where(mine, grads, nothing))
            own_queries.append(jnp.where(mine, queries, nothing))
            own_keys.append(jnp.where(mine, keys, nothing))
        dvalue = dot_nn(jnp.concatenate(softs, axis=1), jnp.concatenate(own_grads, axis=0))
        dkey = dot_nn(jnp.concatenate(score_grads, axis=1), jnp.concatenate(own_queries, axis=0))
        dquery = dot_tn(jnp.concatenate(own_keys, axis=0), jnp.concatenate(score_grads, axis=0))
        dvalue_ref[:, columns] = dvalue.astype(bf16)
        dkey_ref[:, columns] = (dkey * ln_two).astype(bf16)
        dquery_ref[:, columns] = (dquery.T * head_dim**-0.5).astype(bf16)
        return carry

    lax.fori_loop(0, width // 128, pair, 0)

    tokens = token_ref[...]
    total = resid_ref[...]
    near_out[...] = jnp.zeros_like(near_out)
    far_out[...] = jnp.zeros_like(far_out)
    for kind, grad_ref in enumerate((dquery_ref, dkey_ref, dvalue_ref)):
        low = grad_ref[...]
        attend_own[kind] = dot_tn(tokens, low[:, :part])
        far = dot_tn(tokens, low[:, part:]).astype(bf16)
        send[kind * part : (kind + 1) * part, :part] = far[:part]
        send[kind * part : (kind + 1) * part, part:] = far[part:]
        total = (
            total
            + dot_nt(low[:, :part], attend_block(own, half, kind))
            + dot_nt(low[:, part:], attend_block(other, half, kind))
        )
        if kind != 1:
            column = jnp.sum(low.astype(f32), axis=0, keepdims=True)
            start = kind // 2 * part
            near_out[7:8, start : start + part] = column[:, :part]
            far_out[7:8, start : start + part] = column[:, part:]
    low = total.astype(bf16)
    series_near[...] = dot_nt(low[:half], table[...])
    series_far[...] = dot_nt(low[half:], table[...])
    table_grad = dot_tn(series_own[...], low[:half]) + dot_tn(other[:half, :history], low[half:])
    row = lax.broadcasted_iota(jnp.int32, table_grad.shape, 0)
    seen = row >= facts[1:2, 0:1]
    send[3 * part :, :] = jnp.where(seen, table_grad, 0.0).astype(bf16)
    shared = sums_ref[0:7, :]
    bias_grad = jnp.sum(low.astype(f32), axis=0, keepdims=True)
    near_out[0:7, :] = shared
    far_out[0:7, :] = shared
    near_out[0:1, :] = bias_grad
    far_out[0:1, :] = bias_grad
    count_near = inner_sum_ref.shape[1] // 2 // width
    for index in range(count_near):
        near_out[8 + index : 9 + index, :] = inner_sum_ref[0:1, index * width : (index + 1) * width]
        far_out[8 + index : 9 + index, :] = inner_sum_ref[
            0:1, (count_near + index) * width : (count_near + index + 1) * width
        ]


def left_product(start, matrix):
    both = dot_nt(jnp.concatenate(split_two(start), axis=0), matrix.astype(bf16))
    return both[:8] + both[8:]


def right_product(basis, matrix):
    both = dot_nn(jnp.concatenate(split_two(basis), axis=0), matrix.astype(bf16))
    return both[:8] + both[8:]


def feed_matrices(
    active_ref, preact_ref, normed_ref, feed_ref, context_ref, attend_ref, received,
    e_outer, e_inner, e_mixer, s_outer, s_inner, s_mixer, output_near, output_far,
    outer, inner, mixer, left, output, done,
):
    width = feed_ref.shape[1]
    inner_part = outer.shape[0]
    part = mixer.shape[0]
    chunk = 512
    copies = join_copies(output_near, output_far, output, done)
    for copy in copies:
        copy.start()
    outer[...] = (
        dot_tn(active_ref[...], feed_ref[...])
        + received[:inner_part, :].astype(f32)
        + e_outer[...]
    )
    for index in range(inner_part // chunk):
        columns = slice(index * chunk, (index + 1) * chunk)
        start = inner_part + index * width
        inner[:, columns] = (
            dot_tn(normed_ref[...], preact_ref[:, columns])
            + received[start : start + width, :].astype(f32)
            + e_inner[:, columns]
        )
    mixer[...] = (
        dot_tn(context_ref[:, :part], attend_ref[...])
        + received[2 * inner_part :, :].astype(f32)
        + e_mixer[...]
    )
    left[:, 0:1024] = left_product(s_outer[...], outer[...])
    left[:, 1024:1536] = left_product(s_inner[...], inner[...])
    left[:, 1536:1792] = left_product(s_mixer[...], mixer[...])
    for copy in copies:
        copy.wait()


def orthonormal_rows(blocks):
    rows = [lax.broadcasted_iota(jnp.int32, block.shape, 0) for block in blocks]
    for index in range(blocks[0].shape[0]):
        pivots = [block[index : index + 1, :] for block in blocks]
        inners = [jnp.sum(block * pivot, axis=1, keepdims=True) for block, pivot in zip(blocks, pivots)]
        sizes = [inner[index : index + 1, :] + 1e-12 for inner in inners]
        blocks = [
            jnp.where(
                row > index,
                block - pivot * (inner / size),
                jnp.where(row == index, block * lax.rsqrt(size), block),
            )
            for block, row, pivot, inner, size in zip(blocks, rows, pivots, inners, sizes)
        ]
    return blocks


def reduce_factors(
    replicas, facts, near_attend, own, received, e_attend, e_embed, s_attend, s_embed, left_part,
    near, far, outer, inner, mixer,
    left_ref, right_ref, mean_ref, attend, embed,
    start_ref, summed, partial, gathered, parts_one, parts_two, send_sems, recv_sems,
):
    me = lax.axis_index("dp")
    barrier = pltpu.get_barrier_semaphore()
    chunk = start_ref.shape[1] // replicas
    share = 1.0 / replicas

    paired = replicas & (replicas - 1) == 0

    def peer(offset):
        return jnp.bitwise_xor(me, offset) if paired else lax.rem(me + offset, replicas)

    def columns(index):
        return pl.ds(pl.multiple_of(index * chunk, 128), chunk)

    far_first = sorted(
        range(1, min(replicas, 17)), key=lambda k: -((k & 1) + (k >> 1 & 1) + (k >> 2))
    )

    def each(what):
        if replicas <= 16:
            for offset in far_first:
                what(offset)
            return

        def body(index, carry):
            what(replicas - index)
            return carry

        lax.fori_loop(1, replicas, body, 0)

    each(
        lambda offset: pl.semaphore_signal(
            barrier, inc=1, device_id={"dp": peer(offset)}, device_id_type=pl.DeviceIdType.MESH
        )
    )
    part = near_attend.shape[2]
    total = None
    for kind in range(3):
        rows = slice(kind * part, (kind + 1) * part)
        block = jnp.concatenate([received[rows, :part], received[rows, part:]], axis=0)
        attend[kind] = near_attend[kind] + block.astype(f32) + e_attend[kind]
        term = left_product(s_attend[kind], attend[kind])
        total = term if total is None else total + term
    mine, theirs = facts[2:3, 0:1], facts[3:4, 0:1]
    table_near = own[3 * part :, :].astype(f32)
    table_far = received[3 * part :, :].astype(f32)
    pieces = []
    for group in range(embed.shape[0]):
        grad = jnp.where(mine == group, table_near, 0.0) + jnp.where(theirs == group, table_far, 0.0)
        embed[group] = grad + e_embed[group]
        pieces.append(left_product(s_embed[...], embed[group]))
    used = embed.shape[0] * embed.shape[1]
    start_ref[:, 0:1024] = jnp.concatenate(pieces + [jnp.zeros((8, 1024 - used), f32)], axis=1)
    start_ref[:, 1024:2048] = left_part[:, 0:1024]
    start_ref[:, 2048:2560] = total
    start_ref[:, 2560:3328] = left_part[:, 1024:1792]
    common = near[1:7, :] + far[1:7, :]
    row = lax.broadcasted_iota(jnp.int32, (3, near.shape[1]), 0)
    bias = jnp.where(row == mine, near[0:1, :], 0.0) + jnp.where(row == theirs, far[0:1, :], 0.0)
    start_ref[:, 3328:3840] = jnp.concatenate([bias, common[:5]], axis=0)
    rest = jnp.concatenate([common[5:6], near[7:10, :] + far[7:10, :]], axis=0)
    for row in range(4):
        start_ref[2 * row : 2 * row + 1, 3840:4096] = rest[row : row + 1, :256]
        start_ref[2 * row + 1 : 2 * row + 2, 3840:4096] = rest[row : row + 1, 256:]
    if start_ref.shape[1] > 4096:
        start_ref[:, 4096:] = jnp.zeros((8, start_ref.shape[1] - 4096), f32)
    pl.semaphore_wait(barrier, replicas - 1)

    def all_sum(phase, source, parts, result):
        others = parts.at[pl.ds(1, replicas - 1)]

        def scatter(offset):
            other = peer(offset)
            return pltpu.make_async_remote_copy(
                src_ref=source.at[:, columns(other)],
                dst_ref=parts.at[offset],
                send_sem=send_sems.at[2 * phase],
                recv_sem=recv_sems.at[2 * phase],
                device_id={"dp": other},
                device_id_type=pl.DeviceIdType.MESH,
            )

        def spread(offset):
            return pltpu.make_async_remote_copy(
                src_ref=result.at[:, columns(me)],
                dst_ref=result.at[:, columns(me)],
                send_sem=send_sems.at[2 * phase + 1],
                recv_sem=recv_sems.at[2 * phase + 1],
                device_id={"dp": peer(offset)},
                device_id_type=pl.DeviceIdType.MESH,
            )

        def wait_all(semaphore):
            pltpu.make_async_copy(others, others, semaphore).wait()

        each(lambda offset: scatter(offset).start())
        wait_all(recv_sems.at[2 * phase])
        total = source[:, columns(me)]
        if replicas <= 16:
            for offset in range(1, replicas):
                total = total + parts[offset]
        else:
            total = lax.fori_loop(1, replicas, lambda offset, total: total + parts[offset], total)
        result[:, columns(me)] = total * share
        each(lambda offset: spread(offset).start())
        wait_all(recv_sems.at[2 * phase + 1])
        wait_all(send_sems.at[2 * phase])
        wait_all(send_sems.at[2 * phase + 1])

    all_sum(0, start_ref, parts_one, summed)
    mean_ref[...] = summed[:, 3328:4096]
    places = ((0, 1024), (1024, 1024), (2048, 512), (2560, 512), (3072, 256))
    bases = orthonormal_rows([summed[:, start : start + size] for start, size in places])
    for (start, size), basis in zip(places, bases):
        left_ref[:, start : start + size] = basis
    height = embed.shape[1]
    total = None
    for group in range(embed.shape[0]):
        term = right_product(bases[0][:, group * height : (group + 1) * height], embed[group])
        total = term if total is None else total + term
    partial[:, 0:512] = total
    partial[:, 512:1024] = right_product(bases[1], outer[...])
    for kind in range(3):
        partial[:, 1024 + kind * 256 : 1280 + kind * 256] = right_product(bases[2], attend[kind])
    partial[:, 1792:2816] = right_product(bases[3], inner[...])
    partial[:, 2816:3328] = right_product(bases[4], mixer[...])
    partial[:, 3328:] = jnp.zeros((8, partial.shape[1] - 3328), f32)
    all_sum(1, partial, parts_two, gathered)
    right_ref[...] = gathered[:, :3328]


def renew_all(
    step_rate, mixer_rate, left, right, mean, series_near, series_far, *refs,
):
    matrices, weights, moments = refs[0:5], refs[5:10], refs[10:15]
    vectors, vector_moments = refs[15:20], refs[20:25]
    errors, new_weights, new_moments = refs[25:30], refs[30:35], refs[35:40]
    new_vectors, new_vector_moments = refs[40:45], refs[45:50]
    lefts, rights, series_grad, done = refs[50:55], refs[55:60], refs[60], refs[61]
    step = pl.program_id(0)
    copies = join_copies(series_near, series_far, series_grad, done)

    @pl.when(step == 0)
    def _():
        for copy in copies:
            copy.start()

    def approx(basis, factor):
        left_high, left_low = split_two(basis)
        right_high, right_low = split_two(factor)
        return dot_tn(
            jnp.concatenate([left_high, left_low, left_high, left_low], axis=0),
            jnp.concatenate([right_high, right_high, right_low, right_low], axis=0),
        )

    def write(index, where, update, rate):
        errors[index][where] = matrices[index][where] - update
        moment = momentum_decay * moments[index][where] + update
        new_moments[index][where] = moment
        new_weights[index][where] = weights[index][where] - rate * moment

    def cut(start, size):
        return pl.ds(pl.multiple_of(start + step * size, 128), size)

    every = (slice(None), slice(None))
    groups, height, block = matrices[0].shape
    factor = right[:, cut(0, block)]
    for group in range(groups):
        write(
            0, (group, slice(None), slice(None)),
            approx(left[:, group * height : (group + 1) * height], factor), step_rate,
        )
    write(1, every, approx(left[:, cut(1024, matrices[1].shape[0])], right[:, 512:1024]), step_rate)
    basis = left[:, cut(2048, matrices[2].shape[1])]
    for kind in range(3):
        write(
            2, (kind, slice(None), slice(None)),
            approx(basis, right[:, 1024 + kind * 256 : 1280 + kind * 256]), step_rate,
        )
    write(3, every, approx(left[:, cut(2560, matrices[3].shape[0])], right[:, 1792:2816]), step_rate)
    write(4, every, approx(left[:, 3072:3328], right[:, cut(2816, matrices[4].shape[1])]), mixer_rate)

    @pl.when(step == 0)
    def _():
        for group in range(groups):
            lefts[0][group] = left[:, group * height : (group + 1) * height]
        lefts[1][...] = left[:, 1024:2048]
        lefts[2][...] = left[:, 2048:2560]
        lefts[3][...] = left[:, 2560:3072]
        lefts[4][...] = left[:, 3072:3328]
        rights[0][...] = right[:, 0:512]
        rights[1][...] = right[:, 512:1024]
        for kind in range(3):
            rights[2][kind] = right[:, 1024 + kind * 256 : 1280 + kind * 256]
        rights[3][...] = right[:, 1792:2816]
        rights[4][...] = right[:, 2816:3328]

        def renew(index, rows, columns, gradient):
            moment = momentum_decay * vector_moments[index][rows, columns] + gradient
            new_vector_moments[index][rows, columns] = moment
            new_vectors[index][rows, columns] = vectors[index][rows, columns] - step_rate * moment

        renew(0, slice(0, 3), slice(None), mean[0:3, :512])
        renew(1, slice(0, 2), slice(None), mean[3:5, :512])
        renew(2, slice(0, 3), slice(None), mean[5:8, :512])
        renew(2, slice(3, 4), slice(0, 256), mean[0:1, 512:])
        renew(2, slice(3, 4), slice(256, 512), mean[1:2, 512:])
        renew(3, slice(0, 1), slice(None), mean[2:3, 512:])
        renew(3, slice(1, 2), slice(None), mean[3:4, 512:])
        for index in range(4):
            renew(
                4, slice(0, 1), slice(index * 256, (index + 1) * 256),
                mean[4 + index : 5 + index, 512:],
            )

    @pl.when(step == pl.num_programs(0) - 1)
    def _():
        for copy in copies:
            copy.wait()


def call(
    kernel, outs, args, *, cost, in_specs=None, out_specs=None, scratch=(), limit=32, name=None
):
    return pl.pallas_call(
        kernel,
        out_shape=outs,
        in_specs=in_specs if in_specs is not None else [VM] * len(args),
        out_specs=out_specs if out_specs is not None else [VM] * len(outs),
        scratch_shapes=list(scratch),
        compiler_params=pltpu.CompilerParams(vmem_limit_bytes=limit * MIB),
        cost_estimate=estimate(cost),
        name=name,
    )(*args)


def estimate(microseconds):
    return pl.CostEstimate(
        flops=int(microseconds * 1e9), bytes_accessed=int(microseconds * 2e6), transcendentals=0
    )


def sds(shape, dtype=f32):
    return jax.ShapeDtypeStruct(shape, dtype)


def local(
    series, groups, counts, cotangent,
    embed_weight, embed_moment, embed_error, embed_start,
    attend_weight, attend_moment, attend_error, attend_start,
    mixer_weight, mixer_moment, mixer_error, mixer_start,
    inner_weight, inner_moment, inner_error, inner_start,
    outer_weight, outer_moment, outer_error, outer_start,
    embed_bias, embed_bias_moment, query_bias, query_bias_moment,
    inner_bias, inner_bias_moment, norm_gains, gains_moment, shared_biases, biases_moment,
):
    replicas = lax.axis_size("dp")
    half, windows, history = series.shape
    rows = 2 * half
    group_count, _, width = embed_weight.shape
    part = attend_weight.shape[2]
    inner_part = inner_weight.shape[1]
    units = 2 * inner_part
    turned = lambda a: a.transpose(1, 0, 2)

    def swap(values):
        return lax.ppermute(values, "mp", [(0, 1), (1, 0)])

    low = sds((rows, width), bf16)
    full = sds((rows, width))
    near = sds((half, width))
    packed = sds((half + 3 * part + 16, width), bf16)
    send_one, other_one, series_own, small, facts, send_two, cot_own = pl.pallas_call(
        prepare,
        out_shape=[
            packed, packed, sds((half, history), bf16), sds((8, inner_part)), sds((8, 128), jnp.int32),
            sds((part + 2 * inner_part + half, width), bf16), sds((half, width), bf16),
        ],
        in_specs=[HB] * 10,
        out_specs=[VM] * 7,
        scratch_shapes=[
            pltpu.SMEM(groups.shape, jnp.int32), pltpu.SMEM(counts.shape, jnp.int32),
            pltpu.VMEM(series.shape, bf16), pltpu.VMEM((3, width, part), f32),
            pltpu.VMEM(query_bias.shape, f32), pltpu.VMEM((1, inner_part), f32),
            pltpu.VMEM(cotangent.shape, bf16), pltpu.VMEM(mixer_weight.shape, f32),
            pltpu.VMEM(inner_weight.shape, f32), pltpu.VMEM(outer_weight.shape, f32),
            pltpu.SemaphoreType.DMA((10,)), pltpu.SemaphoreType.DMA((2,)), pltpu.SemaphoreType.DMA((2,)),
        ],
        compiler_params=pltpu.CompilerParams(
            collective_id=2, has_side_effects=True, vmem_limit_bytes=LIMITS[0] * MIB
        ),
        cost_estimate=estimate(7),
        name="prepare",
    )(
        *(
            pltpu.with_memory_space_constraint(a, pltpu.HBM)
            for a in (
                groups, counts, series, turned(attend_weight), query_bias, inner_bias[None],
                cotangent, mixer_weight, inner_weight, outer_weight,
            )
        )
    )
    other_two = swap(send_two)
    hidden, tokens, queries, keys, values, context, lse, small_other, table = call(
        attend_forward,
        [full, low, low, low, low, low, sds((HEADS, rows)), sds((8, inner_part)), sds((history, width), bf16)],
        (facts, series_own, embed_weight, embed_bias, send_one, other_one, small),
        limit=LIMITS[2], cost=15, scratch=[pltpu.VMEM((HEADS, rows), f32)],
        name="attend_forward",
    )
    (
        output_near, output_send, active, preact_grad, normed_low, feed_grad, attend_out, resid_one,
        context_grad, delta, sums, inner_sums, grads_send,
    ) = call(
        functools.partial(feed_forward, TILES),
        [near, near, sds((rows, inner_part), bf16), sds((rows, inner_part), bf16), low, low, low, full, low,
         sds((rows, 128), bf16), sds((8, width)), sds((8, units)),
         sds((2 * inner_part + part, width), bf16)],
        (facts, context, hidden, send_two, other_two, small, small_other, norm_gains, shared_biases, cot_own),
        limit=LIMITS[3], cost=22,
        scratch=[
            pltpu.VMEM((rows // TILES, units), bf16), pltpu.VMEM((rows, inner_part), bf16),
            pltpu.VMEM((rows, inner_part), bf16),
        ],
        name="feed_forward",
    )
    output_other = swap(output_send)
    grads_other = swap(grads_send)
    attend_near, send_three, series_near, series_far, sums_near, sums_far = call(
        attend_backward,
        [sds((3, width, part)), sds((3 * part + history, width), bf16), sds((half, history)),
         sds((half, history)), sds((16, width)), sds((16, width))],
        (facts, queries, keys, values, lse, context_grad, delta, tokens, resid_one, send_one,
         other_one, table, series_own, sums, inner_sums),
        limit=LIMITS[4], cost=22,
        scratch=[pltpu.VMEM((rows, width), bf16)] * 3,
        name="attend_backward",
    )
    other_three = swap(send_three)
    series_other = swap(series_far)
    sums_other = swap(sums_far)
    outer_matrix, inner_matrix, mixer_matrix, left_part, output = call(
        feed_matrices,
        [sds(outer_weight.shape), sds(inner_weight.shape), sds(mixer_weight.shape), sds((8, 1792)),
         sds((half, windows, width))],
        (active, preact_grad, normed_low, feed_grad, context, attend_out, grads_other,
         outer_error[0], inner_error[0], mixer_error[0], outer_start[0].T, inner_start.T, mixer_start[0].T,
         output_near, output_other),
        limit=LIMITS[5], cost=6, out_specs=[VM] * 4 + [HB],
        scratch=[pltpu.SemaphoreType.DMA((2,))],
        name="feed_matrices",
    )
    padded = max(128, -(-4096 // replicas // 128) * 128)
    total = padded * replicas
    left, right, mean, attend_matrix, embed_matrix = pl.pallas_call(
        functools.partial(reduce_factors, replicas),
        out_shape=[sds((8, 3328)), sds((8, 3328)), sds((8, 768)), sds((3, width, part)), sds(embed_weight.shape)],
        in_specs=[VM] * 14,
        out_specs=[VM] * 5,
        scratch_shapes=[
            pltpu.VMEM((8, total), f32), pltpu.VMEM((8, total), f32), pltpu.VMEM((8, total), f32),
            pltpu.VMEM((8, total), f32),
            pltpu.VMEM((replicas, 8, padded), f32), pltpu.VMEM((replicas, 8, padded), f32),
            pltpu.SemaphoreType.DMA((4,)), pltpu.SemaphoreType.DMA((4,)),
        ],
        compiler_params=pltpu.CompilerParams(
            collective_id=1, has_side_effects=True, vmem_limit_bytes=LIMITS[6] * MIB
        ),
        cost_estimate=estimate(30),
        name="reduce_factors",
    )(
        facts, attend_near, send_three, other_three, turned(attend_error[0]), embed_error[0],
        attend_start.transpose(0, 2, 1), embed_start.T, left_part, sums_near, sums_other,
        outer_matrix, inner_matrix, mixer_matrix,
    )
    matrices = (embed_matrix, outer_matrix, attend_matrix, inner_matrix, mixer_matrix)

    step_rate = base_rate * math.sqrt(replicas * 7 / (windows * rows))
    mixer_rate = step_rate * math.sqrt(width / max(width * 16 // rows, 1))
    steps = 4
    whole = lambda a: pl.BlockSpec(a.shape, lambda i: (0,) * len(a.shape))
    column = lambda a: pl.BlockSpec((a.shape[0], a.shape[1] // steps), lambda i: (0, i))
    row = lambda a: pl.BlockSpec((a.shape[0] // steps, a.shape[1]), lambda i: (i, 0))
    middle = lambda a: pl.BlockSpec((a.shape[0], a.shape[1] // steps, a.shape[2]), lambda i: (0, i, 0))
    last = lambda a: pl.BlockSpec((a.shape[0], a.shape[1], a.shape[2] // steps), lambda i: (0, 0, i))
    specs = [spec(a) for spec, a in zip((last, row, middle, row, column), matrices)]
    vectors = (embed_bias, norm_gains, shared_biases, query_bias, inner_bias[None])
    vector_moments = (
        embed_bias_moment, gains_moment, biases_moment, query_bias_moment, inner_bias_moment[None]
    )
    vector_specs = [whole(a) for a in vectors]
    factors = [
        sds((group_count, 8, history)), sds((8, 1024)), sds((8, 512)), sds((8, 512)), sds((8, 256)),
        sds((8, 512)), sds((8, 512)), sds((3, 8, part)), sds((8, 1024)), sds((8, 512)),
    ]
    found = pl.pallas_call(
        functools.partial(renew_all, step_rate, mixer_rate),
        grid=(steps,),
        out_shape=[sds(a.shape) for a in matrices] * 3 + [sds(a.shape) for a in vectors] * 2
        + factors + [sds(series.shape)],
        in_specs=[whole(left), whole(right), whole(mean), VM, VM] + specs * 3 + vector_specs * 2,
        out_specs=specs * 3 + vector_specs * 2 + [whole(a) for a in factors] + [HB],
        scratch_shapes=[pltpu.SemaphoreType.DMA((2,))],
        compiler_params=pltpu.CompilerParams(vmem_limit_bytes=LIMITS[7] * MIB),
        cost_estimate=estimate(12),
        name="renew_all",
    )(
        left, right, mean, series_near, series_other, *matrices,
        embed_weight, outer_weight, turned(attend_weight), inner_weight, mixer_weight,
        embed_moment, outer_moment, turned(attend_moment), inner_moment, mixer_moment,
        *vectors, *vector_moments,
    )
    errors, weights, moments = found[0:5], found[5:10], found[10:15]
    new_vectors, new_vector_moments = found[15:20], found[20:25]
    lefts, rights = found[25:30], found[30:35]
    return (
        output,
        found[35],
        weights[0],
        moments[0],
        errors[0][None],
        lefts[0].transpose(0, 2, 1),
        rights[0].T,
        turned(weights[2]),
        turned(moments[2]),
        turned(errors[2])[None],
        lefts[2].T[None],
        rights[2].transpose(0, 2, 1),
        weights[4],
        moments[4],
        errors[4][None],
        lefts[4].T,
        rights[4].T[None],
        weights[3],
        moments[3],
        errors[3][None],
        lefts[3].T[None],
        rights[3].T,
        weights[1],
        moments[1],
        errors[1][None],
        lefts[1].T,
        rights[1].T[None],
        new_vector_moments[0],
        new_vectors[0],
        new_vector_moments[3],
        new_vectors[3],
        new_vector_moments[4][0],
        new_vectors[4][0],
        new_vector_moments[1],
        new_vectors[1],
        new_vector_moments[2],
        new_vectors[2],
    )


def solution(mesh):
    return jax.shard_map(
        local,
        mesh=mesh,
        in_specs=(
            P("mp", "dp", None),
            P("dp"),
            P("dp"),
            P("mp", "dp", None),
            P(),
            P(),
            P("dp", None, None, None),
            P(),
            P(None, None, "mp"),
            P(None, None, "mp"),
            P("dp", None, None, "mp"),
            P(None, "mp", None),
            P("mp", None),
            P("mp", None),
            P("dp", "mp", None),
            P("mp", None, None),
            P(None, "mp"),
            P(None, "mp"),
            P("dp", None, "mp"),
            P("mp", None),
            P("mp", None),
            P("mp", None),
            P("dp", "mp", None),
            P("mp", None, None),
            P(),
            P(),
            P(None, "mp"),
            P(None, "mp"),
            P("mp"),
            P("mp"),
            P(),
            P(),
            P(),
            P(),
        ),
        out_specs=(
            P("mp", "dp", None),
            P("mp", "dp", None),
            P(),
            P(),
            P("dp", None, None, None),
            P(),
            P(),
            P(None, None, "mp"),
            P(None, None, "mp"),
            P("dp", None, None, "mp"),
            P("mp", None, None),
            P(None, "mp", None),
            P("mp", None),
            P("mp", None),
            P("dp", "mp", None),
            P("mp", None),
            P("mp", None, None),
            P(None, "mp"),
            P(None, "mp"),
            P("dp", None, "mp"),
            P("mp", None, None),
            P("mp", None),
            P("mp", None),
            P("mp", None),
            P("dp", "mp", None),
            P("mp", None),
            P("mp", None, None),
            P(),
            P(),
            P(None, "mp"),
            P(None, "mp"),
            P("mp"),
            P("mp"),
            P(),
            P(),
            P(),
            P(),
        ),
        check_vma=False,
    )
```

```python
import functools
import math

import jax
import jax.numpy as jnp
from jax import lax
from jax.experimental import pallas as pl
from jax.experimental.pallas import tpu as pltpu
from jax.sharding import PartitionSpec as P

HEADS = 8
momentum_decay = 0.9
norm_epsilon = 1e-05
base_rate = 0.03
inverse_root_two = 0.7071067811865476
inverse_root_tau = 0.3989422804014327
log2_e = 1.4426950408889634
ln_two = 0.6931471805599453
f32 = jnp.float32
bf16 = jnp.bfloat16
VMEM = pltpu.VMEM
VM = pl.BlockSpec(memory_space=pltpu.VMEM)
HB = pl.BlockSpec(memory_space=pltpu.HBM)
MIB = 1024 * 1024


def dot_nn(a, b):
    return lax.dot_general(a, b, (((1,), (0,)), ((), ())), preferred_element_type=f32)


def dot_nt(a, b):
    return lax.dot_general(a, b, (((1,), (1,)), ((), ())), preferred_element_type=f32)


def dot_tn(a, b):
    return lax.dot_general(a, b, (((0,), (0,)), ((), ())), preferred_element_type=f32)


def split_two(x):
    high = x.astype(bf16)
    return high, (x - high.astype(f32)).astype(bf16)


def three_way(x, lane):
    high = x.astype(bf16).astype(f32)
    rest = x - high
    middle = rest.astype(bf16).astype(f32)
    last = rest - middle
    place = lax.rem(lax.rem(lane, 64), 3)
    return jnp.where(place == 0, high, jnp.where(place == 1, middle, last)).astype(bf16)


LIMITS = (12, 14, 12, 14, 16, 8, 8, 18)
TILES = 2


def row_number(rows, position):
    half = rows // 2
    index = lax.broadcasted_iota(jnp.int32, (rows, 128), 0)
    return jnp.where(index < half, index + position * half, index - half + (1 - position) * half)


def lookback_of(group, history):
    return jnp.where(
        group == 0, history * 2 // 7, jnp.where(group == 1, history * 4 // 7, history)
    ).astype(jnp.int32)


def take_window(pair_ref, window, home, columns):
    for index in range(2):

        @pl.when(window == index)
        def _(index=index):
            home[:, columns] = pair_ref[:, index, :]


def join_copies(mine, theirs, home, done):
    position = lax.axis_index("mp")
    return [
        pltpu.make_async_copy(source, home.at[:, window, :], done.at[index])
        for index, (source, window) in enumerate(((mine, position), (theirs, 1 - position)))
    ]


def three_parts(x):
    high = x.astype(bf16)
    rest = x - high.astype(f32)
    middle = rest.astype(bf16)
    return high, middle, (rest - middle.astype(f32)).astype(bf16)


def prepare(
    groups_hbm, counts_hbm, series_hbm, attend_hbm, query_bias_hbm, inner_bias_hbm,
    cot_hbm, mixer_hbm, inner_hbm, outer_hbm,
    send, received, series_own, small, facts, send_feed, cot_own,
    groups, counts, series, attend, query_bias, inner_bias, cotangent, mixer, inner, outer,
    done, send_sems, recv_sems,
):
    position = lax.axis_index("mp")
    partner = {"mp": 1 - position}
    barrier = pltpu.get_barrier_semaphore()
    pl.semaphore_signal(barrier, inc=1, device_id=partner, device_id_type=pl.DeviceIdType.MESH)
    copies = []
    for source, target in (
        (query_bias_hbm, query_bias), (inner_bias_hbm, inner_bias), (attend_hbm, attend),
        (series_hbm, series), (groups_hbm, groups), (counts_hbm, counts), (cot_hbm, cotangent),
        (mixer_hbm, mixer), (inner_hbm, inner), (outer_hbm, outer),
    ):
        copies.append(pltpu.make_async_copy(source, target, done.at[len(copies)]))
    for copy in copies[:6]:
        copy.start()
    half, _, history = series.shape
    width = send.shape[1]
    depth = attend.shape[1] // 2
    end = half + 3 * depth
    part = query_bias.shape[1]
    trades = [
        pltpu.make_async_remote_copy(
            src_ref=send.at[place], dst_ref=received.at[place], send_sem=send_sems.at[index],
            recv_sem=recv_sems.at[index], device_id=partner, device_id_type=pl.DeviceIdType.MESH,
        )
        for index, place in enumerate(
            (
                (slice(half, end + 16), slice(None)),
                (slice(0, half), slice(0, -(-history // 128) * 128)),
            )
        )
    ]
    copies[0].wait()
    copies[1].wait()
    small[...] = jnp.zeros_like(small)
    small[0:2, :part] = query_bias[...]
    small[2:3, :] = inner_bias[...]
    values = jnp.concatenate(
        [
            jnp.concatenate([query_bias[0:1, :], query_bias[1:2, :]], axis=1),
            inner_bias[:, :width],
            inner_bias[:, width:],
            jnp.zeros((1, width), f32),
        ],
        axis=0,
    )
    send[end : end + 16, :] = jnp.concatenate(
        [*three_parts(values), jnp.zeros((4, width), bf16)], axis=0
    )
    copies[2].wait()
    for copy in copies[6:]:
        copy.start()
    for kind in range(3):
        rows = slice(half + kind * depth, half + (kind + 1) * depth)
        send[rows, :256] = attend[kind, :depth, :].astype(bf16)
        send[rows, 256:] = attend[kind, depth:, :].astype(bf16)
    pl.semaphore_wait(barrier, 1)
    trades[0].start()
    send[:half, 256:] = jnp.zeros((half, width - 256), bf16)
    copies[3].wait()
    take_window(series, 1 - position, send.at[:half], slice(0, history))
    trades[1].start()
    take_window(series, position, series_own, slice(None))
    copies[4].wait()
    copies[5].wait()
    group = jnp.where(position == 0, groups[0], groups[1])
    other_group = jnp.where(position == 0, groups[1], groups[0])
    count = jnp.where(position == 0, counts[0], counts[1])
    first = history - lookback_of(group, history)
    row = lax.broadcasted_iota(jnp.int32, facts.shape, 0)
    facts[...] = jnp.where(
        row == 0, count, jnp.where(row == 1, first, jnp.where(row == 2, group, other_group))
    )
    m, d, o = mixer.shape[0], inner.shape[0], outer.shape[0]
    copies[6].wait()
    take_window(cotangent, 1 - position, send_feed.at[m + 2 * d + o :], slice(None))
    take_window(cotangent, position, cot_own, slice(None))
    copies[7].wait()
    send_feed[:m] = mixer[...].astype(bf16)
    copies[8].wait()
    send_feed[m : m + d] = inner[:, :512].astype(bf16)
    send_feed[m + d : m + 2 * d] = inner[:, 512:].astype(bf16)
    copies[9].wait()
    send_feed[m + 2 * d : m + 2 * d + o] = outer[...].astype(bf16)
    for trade in trades:
        trade.wait()


def unpack_small(other, small_other):
    part = other.shape[1] // 2
    parts = other[other.shape[0] - 16 :, :].astype(f32)
    values = parts[0:4] + parts[4:8] + parts[8:12]
    small_other[0:1, :part] = values[0:1, :part]
    small_other[1:2, :part] = values[0:1, part:]
    small_other[2:3, : 2 * part] = values[1:2, :]
    small_other[2:3, 2 * part :] = values[2:3, :]


def attend_block(pack, half, kind):
    start = half + kind * 256
    return jnp.concatenate([pack[start : start + 256, :256], pack[start : start + 256, 256:]], axis=0)


def attend_forward(
    facts, series_own, embed, embed_bias, own, other, small,
    hidden_ref, token_ref, query_ref, key_ref, value_ref, context_ref, lse_ref, small_other, table, peak_ref,
):
    unpack_small(other, small_other)
    chosen, bias_row = embed[0], embed_bias[0:1, :]
    for group in range(1, embed.shape[0]):
        here = facts[2:3, 0:1] == group
        chosen = jnp.where(here, embed[group], chosen)
        bias_row = jnp.where(here, embed_bias[group : group + 1, :], bias_row)
    row = lax.broadcasted_iota(jnp.int32, chosen.shape, 0)
    table[...] = jnp.where(row >= facts[1:2, 0:1], chosen, 0.0).astype(bf16)
    rows, width = hidden_ref.shape
    half, history = series_own.shape
    part = width // 2
    head_dim = width // HEADS
    position, count = lax.axis_index("mp"), facts[0:1, 0:1]
    for index, block in enumerate((series_own[...], other[:half, :history])):
        values = dot_nn(block, table[...]) + bias_row
        hidden_ref[pl.ds(index * half, half), :] = values
        token_ref[pl.ds(index * half, half), :] = values.astype(bf16)
    scale = head_dim**-0.5 * log2_e
    tokens = token_ref[...]
    for index, (pack, bias) in enumerate(((own, small), (other, small_other))):
        columns = pl.ds(index * part, part)
        query_ref[:, columns] = (
            (dot_nn(tokens, attend_block(pack, half, 0)) + bias[0:1, :part]) * scale
        ).astype(bf16)
        key_ref[:, columns] = dot_nn(tokens, attend_block(pack, half, 1)).astype(bf16)
        value_ref[:, columns] = (
            dot_nn(tokens, attend_block(pack, half, 2)) + bias[1:2, :part]
        ).astype(bf16)
    lane = lax.broadcasted_iota(jnp.int32, (rows, 128), 1)
    dead = row_number(rows, position) >= count
    last = lax.rem(lane, 64) == 63
    extra_query = jnp.where(last, 1.0, 0.0).astype(bf16)
    extra_key = jnp.where(last & dead, -1e30, 0.0).astype(bf16)
    ones = jnp.ones((rows, 128), bf16)

    chooser = head_chooser(width, head_dim, 1.0)

    def longest(ref):
        values = ref[...].astype(f32)
        return jnp.max(dot_nn((values * values).astype(bf16), chooser), axis=0, keepdims=True)

    bound = jnp.max(longest(query_ref) * longest(key_ref))
    peak_ref[...] = jnp.zeros_like(peak_ref)

    @pl.when(jnp.logical_not(bound < 3600.0))
    def _():
        block = 128
        block_lane = lane[:block]

        def one_head(head, carry):
            columns = pl.ds(pl.multiple_of(head // 2 * 128, 128), 128)
            side = lax.rem(head, 2)
            query = jnp.where((lane // head_dim) == side, query_ref[:, columns], extra_query)

            def one_block(index, peak):
                place = pl.ds(pl.multiple_of(index * block, block), block)
                keys = key_ref[place, columns]
                far = lax.broadcasted_iota(jnp.int32, (block, 128), 0) + index * block
                near = jnp.where(
                    far < half, far + position * half, far - half + (1 - position) * half
                )
                mask = jnp.where(
                    (lax.rem(block_lane, 64) == 63) & (near >= count), -1e30, 0.0
                ).astype(bf16)
                scores = dot_nt(jnp.where((block_lane // head_dim) == side, keys, mask), query)
                return jnp.maximum(peak, jnp.max(scores, axis=0, keepdims=True))

            peak_ref[pl.ds(head, 1), :] = lax.fori_loop(
                0, rows // block, one_block, jnp.full((1, rows), -1e30, f32)
            )
            return carry

        lax.fori_loop(0, HEADS, one_head, 0)

    spread = part_spreader(-1.0)
    extra_query = jnp.where(
        last, 1.0, dot_tn(jnp.concatenate(three_parts(peak_ref[...]), axis=0), spread)
    ).astype(bf16)
    extra_key = jnp.where(last & dead, -1e30, 0.0)

    def pair(index, carry):
        columns = pl.ds(pl.multiple_of(index * 128, 128), 128)
        queries = query_ref[:, columns]
        keys = key_ref[:, columns]
        values = value_ref[:, columns]
        found = []
        for side in range(2):
            mine = (lane >= head_dim) if side else (lane < head_dim)
            hot = lax.rem(lane, 64) // 3 == index * 2 + side
            scores = dot_nt(
                jnp.where(mine, keys, jnp.where(hot, 1.0, extra_key).astype(bf16)),
                jnp.where(mine, queries, extra_query),
            )
            soft = jnp.exp2(scores).astype(bf16)
            mixed = dot_tn(jnp.where(mine, values, ones), soft)
            top, bottom = mixed[:head_dim], mixed[head_dim:]
            wanted, total = (bottom, top) if side else (top, bottom)
            found.append(wanted / total)
            place = pl.ds(index * 2 + side, 1)
            lse_ref[place, :] = jnp.log2(total[0:1]) + peak_ref[place, :]
        context_ref[:, columns] = jnp.concatenate(found, axis=0).T.astype(bf16)
        return carry

    lax.fori_loop(0, width // 128, pair, 0)


def part_spreader(value):
    row = lax.broadcasted_iota(jnp.int32, (3 * HEADS, 128), 0)
    lane = lax.broadcasted_iota(jnp.int32, (3 * HEADS, 128), 1)
    head = lax.rem(row, HEADS)
    wanted = lane == jnp.where(lax.rem(head, 2) == 0, 64, 0) + 3 * head + row // HEADS
    return jnp.where(wanted, value, 0.0).astype(bf16)


def head_chooser(width, head_dim, value):
    head = lax.broadcasted_iota(jnp.int32, (width, 128), 0) // head_dim
    lane = lax.broadcasted_iota(jnp.int32, (width, 128), 1)
    wanted = (lax.rem(lane, 64) // 3 == head) & ((lane >= 64) == (lax.rem(head, 2) == 0))
    return jnp.where(wanted, value, 0.0).astype(bf16)


def norm_rows(values, gain, shift):
    centered = values - jnp.mean(values, axis=-1, keepdims=True)
    inverse = lax.rsqrt(jnp.mean(centered * centered, axis=-1, keepdims=True) + norm_epsilon)
    unit = centered * inverse
    return unit * gain + shift, unit, inverse


def norm_rows_back(upstream, unit, inverse, gain):
    scaled = upstream * gain
    return inverse * (
        scaled
        - jnp.mean(scaled, axis=-1, keepdims=True)
        - unit * jnp.mean(scaled * unit, axis=-1, keepdims=True)
    )


def feed_forward(
    tiles, facts, context_ref, hidden_ref, own, other, small, small_other, gains, biases, cot_own,
    output_ref, output_send, active_near, preact_near, normed_ref, feed_ref, attend_ref, resid_ref,
    context_grad_ref, delta_ref, sums_ref, inner_sum_ref, grads_send, slope_ref, active_far, preact_far,
):
    rows, width = hidden_ref.shape
    tile = rows // tiles
    half = rows // 2
    part = width // 2
    inner_part = active_near.shape[1]
    units = 2 * inner_part
    chunk = 512
    position, count = lax.axis_index("mp"), facts[0:1, 0:1]
    sums_ref[...] = jnp.zeros_like(sums_ref)
    inner_sum_ref[...] = jnp.zeros_like(inner_sum_ref)
    at_inner = part
    at_outer = part + inner_part
    at_cot = at_outer + inner_part

    def inner_chunk(index):
        pack = (own, other)[index * chunk // inner_part]
        start = at_inner + (index * chunk % inner_part) // chunk * width
        return pack[start : start + width, :]

    def outer_chunk(index):
        pack = (own, other)[index * chunk // inner_part]
        start = at_outer + index * chunk % inner_part
        return pack[start : start + chunk, :]

    head_dim = width // HEADS
    chooser = head_chooser(width, head_dim, -1.0)

    def add(row, values):
        sums_ref[row : row + 1, :] += jnp.sum(values, axis=0, keepdims=True)

    def one_tile(step, carry):
        place = pl.ds(pl.multiple_of(step * tile, tile), tile)
        context = context_ref[place, :]
        attended = dot_nn(context[:, :part], own[:part, :]) + dot_nn(
            context[:, part:], other[:part, :]
        )
        normed, unit_one, inverse_one = norm_rows(
            hidden_ref[place, :] + attended + biases[2:3, :], gains[0:1, :], biases[0:1, :]
        )
        normed_low = normed.astype(bf16)
        normed_ref[place, :] = normed_low
        for index in range(units // chunk):
            columns = slice(index * chunk, (index + 1) * chunk)
            bias = (small, small_other)[index * chunk // inner_part]
            start = index * chunk % inner_part
            preact = dot_nn(normed_low, inner_chunk(index)) + bias[2:3, start : start + chunk]
            phi = 0.5 + 0.5 * lax.erf(preact * inverse_root_two)
            (active_near, active_far)[index * chunk // inner_part][place, start : start + chunk] = (preact * phi).astype(bf16)
            slope_ref[:, columns] = (
                phi + preact * jnp.exp2(preact * preact * (-0.5 * log2_e)) * inverse_root_tau
            ).astype(bf16)
        feed_out = dot_nn(active_near[place, :], own[at_outer:at_cot, :]) + dot_nn(
            active_far[place, :], other[at_outer:at_cot, :]
        )
        output, unit_two, inverse_two = norm_rows(
            normed + feed_out + biases[3:4, :], gains[1:2, :], biases[1:2, :]
        )
        index = lax.broadcasted_iota(jnp.int32, (tile, width), 0)

        @pl.when(step < tiles // 2)
        def _():
            output_ref[place, :] = output
        far = step - tiles // 2
        far_place = pl.ds(pl.multiple_of(jnp.maximum(far, 0) * tile, tile), tile)
        near_place = pl.ds(pl.multiple_of(jnp.minimum(step, tiles // 2 - 1) * tile, tile), tile)

        @pl.when(step >= tiles // 2)
        def _():
            output_send[far_place, :] = output
        cot = jnp.where(
            step < tiles // 2,
            cot_own[near_place, :],
            other[pl.ds(pl.multiple_of(at_cot + jnp.maximum(far, 0) * tile, 32), tile), :],
        ).astype(f32)
        first = jnp.where(
            step < tiles // 2,
            position * half + step * tile,
            (1 - position) * half + far * tile,
        )
        upstream = jnp.where(index + first < count, cot, 0.0)
        resid_two = norm_rows_back(upstream, unit_two, inverse_two, gains[1:2, :])
        feed_grad = resid_two.astype(bf16)
        feed_ref[place, :] = feed_grad
        for index in range(units // chunk):
            columns = slice(index * chunk, (index + 1) * chunk)
            grad = dot_nt(feed_grad, outer_chunk(index))
            start = index * chunk % inner_part
            (preact_near, preact_far)[index * chunk // inner_part][place, start : start + chunk] = (
                grad * slope_ref[:, columns].astype(f32)
            ).astype(bf16)
        normed_grad = resid_two
        for index in range(units // chunk):
            start = index * chunk % inner_part
            block = (preact_near, preact_far)[index * chunk // inner_part]
            normed_grad = normed_grad + dot_nt(
                block[place, start : start + chunk], inner_chunk(index)
            )
        resid_one = norm_rows_back(normed_grad, unit_one, inverse_one, gains[0:1, :])
        resid_ref[place, :] = resid_one
        attend_grad = resid_one.astype(bf16)
        attend_ref[place, :] = attend_grad
        context_grad = jnp.concatenate(
            [dot_nt(attend_grad, own[:part, :]), dot_nt(attend_grad, other[:part, :])], axis=1
        ).astype(bf16)
        context_grad_ref[place, :] = context_grad
        high, low = split_two(context_grad.astype(f32) * context.astype(f32))
        delta = dot_nn(high, chooser) + dot_nn(low, chooser)
        delta_ref[place, :] = three_way(delta, lax.broadcasted_iota(jnp.int32, (tile, 128), 1))
        add(1, normed_grad * unit_one)
        add(2, upstream * unit_two)
        add(3, normed_grad)
        add(4, upstream)
        add(5, resid_one)
        add(6, resid_two)
        for index, block in enumerate((preact_near, preact_far)):
            columns = slice(index * inner_part, (index + 1) * inner_part)
            inner_sum_ref[0:1, columns] += jnp.sum(
                block[place, :].astype(f32), axis=0, keepdims=True
            )
        return carry

    lax.fori_loop(0, tiles, one_tile, 0)
    grads_send[:inner_part, :] = dot_tn(active_far[...], feed_ref[...]).astype(bf16)
    for index in range(inner_part // chunk):
        start = index * chunk
        grads_send[inner_part + index * width : inner_part + (index + 1) * width, :] = dot_tn(
            normed_ref[...], preact_far[:, start : start + chunk]
        ).astype(bf16)
    grads_send[2 * inner_part :, :] = dot_tn(context_ref[:, part:], attend_ref[...]).astype(bf16)


def attend_backward(
    facts, query_ref, key_ref, value_ref, lse_ref, context_grad_ref, delta_ref,
    token_ref, resid_ref, own, other, table, series_own, sums_ref, inner_sum_ref,
    attend_own, send, series_near, series_far, near_out, far_out,
    dquery_ref, dkey_ref, dvalue_ref,
):
    rows, width = query_ref.shape
    head_dim = width // HEADS
    half, history = series_own.shape
    part = width // 2
    position, count = lax.axis_index("mp"), facts[0:1, 0:1]
    lane = lax.broadcasted_iota(jnp.int32, (rows, 128), 1)
    dead = row_number(rows, position) >= count
    last = lax.rem(lane, 64) == 63
    spread = part_spreader(-1.0)
    extra_query = jnp.where(
        last, 1.0, dot_tn(jnp.concatenate(three_parts(lse_ref[...]), axis=0), spread)
    ).astype(bf16)
    extra_key = jnp.where(last & dead, -1e30, 0.0)
    extra_grad = delta_ref[...]
    nothing = jnp.zeros((rows, 128), bf16)

    def pair(index, carry):
        columns = pl.ds(pl.multiple_of(index * 128, 128), 128)
        queries = query_ref[:, columns]
        keys = key_ref[:, columns]
        values = value_ref[:, columns]
        grads = context_grad_ref[:, columns]
        softs, score_grads, own_grads, own_queries, own_keys = [], [], [], [], []
        for side in range(2):
            mine = (lane >= head_dim) if side else (lane < head_dim)
            hot = lax.rem(lane, 64) // 3 == index * 2 + side
            soft = jnp.exp2(
                dot_nt(
                    jnp.where(mine, keys, jnp.where(hot, 1.0, extra_key).astype(bf16)),
                    jnp.where(mine, queries, extra_query),
                )
            )
            centered = dot_nt(
                jnp.where(mine, values, jnp.where(hot, 1.0, 0.0).astype(bf16)),
                jnp.where(mine, grads, extra_grad),
            )
            softs.append(soft.astype(bf16))
            score_grads.append((soft * centered).astype(bf16))
            own_grads.append(jnp.where(mine, grads, nothing))
            own_queries.append(jnp.where(mine, queries, nothing))
            own_keys.append(jnp.where(mine, keys, nothing))
        dvalue = dot_nn(jnp.concatenate(softs, axis=1), jnp.concatenate(own_grads, axis=0))
        dkey = dot_nn(jnp.concatenate(score_grads, axis=1), jnp.concatenate(own_queries, axis=0))
        dquery = dot_tn(jnp.concatenate(own_keys, axis=0), jnp.concatenate(score_grads, axis=0))
        dvalue_ref[:, columns] = dvalue.astype(bf16)
        dkey_ref[:, columns] = (dkey * ln_two).astype(bf16)
        dquery_ref[:, columns] = (dquery.T * head_dim**-0.5).astype(bf16)
        return carry

    lax.fori_loop(0, width // 128, pair, 0)

    tokens = token_ref[...]
    total = resid_ref[...]
    near_out[...] = jnp.zeros_like(near_out)
    far_out[...] = jnp.zeros_like(far_out)
    for kind, grad_ref in enumerate((dquery_ref, dkey_ref, dvalue_ref)):
        low = grad_ref[...]
        attend_own[kind] = dot_tn(tokens, low[:, :part])
        far = dot_tn(tokens, low[:, part:]).astype(bf16)
        send[kind * part : (kind + 1) * part, :part] = far[:part]
        send[kind * part : (kind + 1) * part, part:] = far[part:]
        total = (
            total
            + dot_nt(low[:, :part], attend_block(own, half, kind))
            + dot_nt(low[:, part:], attend_block(other, half, kind))
        )
        if kind != 1:
            column = jnp.sum(low.astype(f32), axis=0, keepdims=True)
            start = kind // 2 * part
            near_out[7:8, start : start + part] = column[:, :part]
            far_out[7:8, start : start + part] = column[:, part:]
    low = total.astype(bf16)
    series_near[...] = dot_nt(low[:half], table[...])
    series_far[...] = dot_nt(low[half:], table[...])
    table_grad = dot_tn(series_own[...], low[:half]) + dot_tn(other[:half, :history], low[half:])
    row = lax.broadcasted_iota(jnp.int32, table_grad.shape, 0)
    seen = row >= facts[1:2, 0:1]
    send[3 * part :, :] = jnp.where(seen, table_grad, 0.0).astype(bf16)
    shared = sums_ref[0:7, :]
    bias_grad = jnp.sum(low.astype(f32), axis=0, keepdims=True)
    near_out[0:7, :] = shared
    far_out[0:7, :] = shared
    near_out[0:1, :] = bias_grad
    far_out[0:1, :] = bias_grad
    count_near = inner_sum_ref.shape[1] // 2 // width
    for index in range(count_near):
        near_out[8 + index : 9 + index, :] = inner_sum_ref[0:1, index * width : (index + 1) * width]
        far_out[8 + index : 9 + index, :] = inner_sum_ref[
            0:1, (count_near + index) * width : (count_near + index + 1) * width
        ]


def left_product(start, matrix):
    both = dot_nt(jnp.concatenate(split_two(start), axis=0), matrix.astype(bf16))
    return both[:8] + both[8:]


def right_product(basis, matrix):
    both = dot_nn(jnp.concatenate(split_two(basis), axis=0), matrix.astype(bf16))
    return both[:8] + both[8:]


def feed_matrices(
    active_ref, preact_ref, normed_ref, feed_ref, context_ref, attend_ref, received,
    e_outer, e_inner, e_mixer, s_outer, s_inner, s_mixer, output_near, output_far,
    outer, inner, mixer, left, output, done,
):
    width = feed_ref.shape[1]
    inner_part = outer.shape[0]
    part = mixer.shape[0]
    chunk = 512
    copies = join_copies(output_near, output_far, output, done)
    for copy in copies:
        copy.start()
    outer[...] = (
        dot_tn(active_ref[...], feed_ref[...])
        + received[:inner_part, :].astype(f32)
        + e_outer[...]
    )
    for index in range(inner_part // chunk):
        columns = slice(index * chunk, (index + 1) * chunk)
        start = inner_part + index * width
        inner[:, columns] = (
            dot_tn(normed_ref[...], preact_ref[:, columns])
            + received[start : start + width, :].astype(f32)
            + e_inner[:, columns]
        )
    mixer[...] = (
        dot_tn(context_ref[:, :part], attend_ref[...])
        + received[2 * inner_part :, :].astype(f32)
        + e_mixer[...]
    )
    left[:, 0:1024] = left_product(s_outer[...], outer[...])
    left[:, 1024:1536] = left_product(s_inner[...], inner[...])
    left[:, 1536:1792] = left_product(s_mixer[...], mixer[...])
    for copy in copies:
        copy.wait()


def orthonormal_rows(blocks):
    rows = [lax.broadcasted_iota(jnp.int32, block.shape, 0) for block in blocks]
    for index in range(blocks[0].shape[0]):
        pivots = [block[index : index + 1, :] for block in blocks]
        inners = [jnp.sum(block * pivot, axis=1, keepdims=True) for block, pivot in zip(blocks, pivots)]
        sizes = [inner[index : index + 1, :] + 1e-12 for inner in inners]
        blocks = [
            jnp.where(
                row > index,
                block - pivot * (inner / size),
                jnp.where(row == index, block * lax.rsqrt(size), block),
            )
            for block, row, pivot, inner, size in zip(blocks, rows, pivots, inners, sizes)
        ]
    return blocks


def reduce_factors(
    replicas, facts, near_attend, own, received, e_attend, e_embed, s_attend, s_embed, left_part,
    near, far, outer, inner, mixer,
    left_ref, right_ref, mean_ref, attend, embed,
    start_ref, summed, partial, gathered, parts_one, parts_two, send_sems, recv_sems,
):
    me = lax.axis_index("dp")
    barrier = pltpu.get_barrier_semaphore()
    chunk = start_ref.shape[1] // replicas
    share = 1.0 / replicas

    paired = replicas & (replicas - 1) == 0

    def peer(offset):
        return jnp.bitwise_xor(me, offset) if paired else lax.rem(me + offset, replicas)

    def columns(index):
        return pl.ds(pl.multiple_of(index * chunk, 128), chunk)

    far_first = sorted(
        range(1, min(replicas, 17)), key=lambda k: -((k & 1) + (k >> 1 & 1) + (k >> 2))
    )

    def each(what):
        if replicas <= 16:
            for offset in far_first:
                what(offset)
            return

        def body(index, carry):
            what(replicas - index)
            return carry

        lax.fori_loop(1, replicas, body, 0)

    each(
        lambda offset: pl.semaphore_signal(
            barrier, inc=1, device_id={"dp": peer(offset)}, device_id_type=pl.DeviceIdType.MESH
        )
    )
    part = near_attend.shape[2]
    total = None
    for kind in range(3):
        rows = slice(kind * part, (kind + 1) * part)
        block = jnp.concatenate([received[rows, :part], received[rows, part:]], axis=0)
        attend[kind] = near_attend[kind] + block.astype(f32) + e_attend[kind]
        term = left_product(s_attend[kind], attend[kind])
        total = term if total is None else total + term
    mine, theirs = facts[2:3, 0:1], facts[3:4, 0:1]
    table_near = own[3 * part :, :].astype(f32)
    table_far = received[3 * part :, :].astype(f32)
    pieces = []
    for group in range(embed.shape[0]):
        grad = jnp.where(mine == group, table_near, 0.0) + jnp.where(theirs == group, table_far, 0.0)
        embed[group] = grad + e_embed[group]
        pieces.append(left_product(s_embed[...], embed[group]))
    used = embed.shape[0] * embed.shape[1]
    start_ref[:, 0:1024] = jnp.concatenate(pieces + [jnp.zeros((8, 1024 - used), f32)], axis=1)
    start_ref[:, 1024:2048] = left_part[:, 0:1024]
    start_ref[:, 2048:2560] = total
    start_ref[:, 2560:3328] = left_part[:, 1024:1792]
    common = near[1:7, :] + far[1:7, :]
    row = lax.broadcasted_iota(jnp.int32, (3, near.shape[1]), 0)
    bias = jnp.where(row == mine, near[0:1, :], 0.0) + jnp.where(row == theirs, far[0:1, :], 0.0)
    start_ref[:, 3328:3840] = jnp.concatenate([bias, common[:5]], axis=0)
    rest = jnp.concatenate([common[5:6], near[7:10, :] + far[7:10, :]], axis=0)
    for row in range(4):
        start_ref[2 * row : 2 * row + 1, 3840:4096] = rest[row : row + 1, :256]
        start_ref[2 * row + 1 : 2 * row + 2, 3840:4096] = rest[row : row + 1, 256:]
    if start_ref.shape[1] > 4096:
        start_ref[:, 4096:] = jnp.zeros((8, start_ref.shape[1] - 4096), f32)
    pl.semaphore_wait(barrier, replicas - 1)

    def all_sum(phase, source, parts, result):
        others = parts.at[pl.ds(1, replicas - 1)]

        def scatter(offset):
            other = peer(offset)
            return pltpu.make_async_remote_copy(
                src_ref=source.at[:, columns(other)],
                dst_ref=parts.at[offset],
                send_sem=send_sems.at[2 * phase],
                recv_sem=recv_sems.at[2 * phase],
                device_id={"dp": other},
                device_id_type=pl.DeviceIdType.MESH,
            )

        def spread(offset):
            return pltpu.make_async_remote_copy(
                src_ref=result.at[:, columns(me)],
                dst_ref=result.at[:, columns(me)],
                send_sem=send_sems.at[2 * phase + 1],
                recv_sem=recv_sems.at[2 * phase + 1],
                device_id={"dp": peer(offset)},
                device_id_type=pl.DeviceIdType.MESH,
            )

        def wait_all(semaphore):
            pltpu.make_async_copy(others, others, semaphore).wait()

        each(lambda offset: scatter(offset).start())
        wait_all(recv_sems.at[2 * phase])
        total = source[:, columns(me)]
        if replicas <= 16:
            for offset in range(1, replicas):
                total = total + parts[offset]
        else:
            total = lax.fori_loop(1, replicas, lambda offset, total: total + parts[offset], total)
        result[:, columns(me)] = total * share
        each(lambda offset: spread(offset).start())
        wait_all(recv_sems.at[2 * phase + 1])
        wait_all(send_sems.at[2 * phase])
        wait_all(send_sems.at[2 * phase + 1])

    all_sum(0, start_ref, parts_one, summed)
    mean_ref[...] = summed[:, 3328:4096]
    places = ((0, 1024), (1024, 1024), (2048, 512), (2560, 512), (3072, 256))
    bases = orthonormal_rows([summed[:, start : start + size] for start, size in places])
    for (start, size), basis in zip(places, bases):
        left_ref[:, start : start + size] = basis
    height = embed.shape[1]
    total = None
    for group in range(embed.shape[0]):
        term = right_product(bases[0][:, group * height : (group + 1) * height], embed[group])
        total = term if total is None else total + term
    partial[:, 0:512] = total
    partial[:, 512:1024] = right_product(bases[1], outer[...])
    for kind in range(3):
        partial[:, 1024 + kind * 256 : 1280 + kind * 256] = right_product(bases[2], attend[kind])
    partial[:, 1792:2816] = right_product(bases[3], inner[...])
    partial[:, 2816:3328] = right_product(bases[4], mixer[...])
    partial[:, 3328:] = jnp.zeros((8, partial.shape[1] - 3328), f32)
    all_sum(1, partial, parts_two, gathered)
    right_ref[...] = gathered[:, :3328]


def renew_all(
    step_rate, mixer_rate, left, right, mean, series_near, series_far, *refs,
):
    matrices, weights, moments = refs[0:5], refs[5:10], refs[10:15]
    vectors, vector_moments = refs[15:20], refs[20:25]
    errors, new_weights, new_moments = refs[25:30], refs[30:35], refs[35:40]
    new_vectors, new_vector_moments = refs[40:45], refs[45:50]
    lefts, rights, series_grad, done = refs[50:55], refs[55:60], refs[60], refs[61]
    step = pl.program_id(0)
    copies = join_copies(series_near, series_far, series_grad, done)

    @pl.when(step == 0)
    def _():
        for copy in copies:
            copy.start()

    def approx(basis, factor):
        left_high, left_low = split_two(basis)
        right_high, right_low = split_two(factor)
        return dot_tn(
            jnp.concatenate([left_high, left_low, left_high, left_low], axis=0),
            jnp.concatenate([right_high, right_high, right_low, right_low], axis=0),
        )

    def write(index, read, where, update, rate):
        errors[index][where] = matrices[index][read] - update
        moment = momentum_decay * moments[index][read] + update
        new_moments[index][where] = moment
        new_weights[index][where] = weights[index][read] - rate * moment

    def cut(start, size):
        return pl.ds(pl.multiple_of(start + step * size, 128), size)

    all_of = slice(None)
    every = (all_of, all_of)
    groups, height, block = errors[0].shape
    factor = right[:, cut(0, block)]
    for group in range(groups):
        write(
            0, (group, all_of, cut(0, block)), (group, all_of, all_of),
            approx(left[:, group * height : (group + 1) * height], factor), step_rate,
        )
    block = errors[1].shape[0]
    write(
        1, (cut(0, block), all_of), every, approx(left[:, cut(1024, block)], right[:, 512:1024]),
        step_rate,
    )
    block = errors[2].shape[1]
    basis = left[:, cut(2048, block)]
    for kind in range(3):
        write(
            2, (kind, cut(0, block), all_of), (kind, all_of, all_of),
            approx(basis, right[:, 1024 + kind * 256 : 1280 + kind * 256]), step_rate,
        )
    block = errors[3].shape[0]
    write(
        3, (cut(0, block), all_of), every, approx(left[:, cut(2560, block)], right[:, 1792:2816]),
        step_rate,
    )
    block = errors[4].shape[1]
    write(
        4, (all_of, cut(0, block)), every, approx(left[:, 3072:3328], right[:, cut(2816, block)]),
        mixer_rate,
    )

    @pl.when(step == 0)
    def _():
        for group in range(groups):
            lefts[0][group] = left[:, group * height : (group + 1) * height]
        lefts[1][...] = left[:, 1024:2048]
        lefts[2][...] = left[:, 2048:2560]
        lefts[3][...] = left[:, 2560:3072]
        lefts[4][...] = left[:, 3072:3328]
        rights[0][...] = right[:, 0:512]
        rights[1][...] = right[:, 512:1024]
        for kind in range(3):
            rights[2][kind] = right[:, 1024 + kind * 256 : 1280 + kind * 256]
        rights[3][...] = right[:, 1792:2816]
        rights[4][...] = right[:, 2816:3328]

        def renew(index, rows, columns, gradient):
            moment = momentum_decay * vector_moments[index][rows, columns] + gradient
            new_vector_moments[index][rows, columns] = moment
            new_vectors[index][rows, columns] = vectors[index][rows, columns] - step_rate * moment

        renew(0, slice(0, 3), slice(None), mean[0:3, :512])
        renew(1, slice(0, 2), slice(None), mean[3:5, :512])
        renew(2, slice(0, 3), slice(None), mean[5:8, :512])
        renew(2, slice(3, 4), slice(0, 256), mean[0:1, 512:])
        renew(2, slice(3, 4), slice(256, 512), mean[1:2, 512:])
        renew(3, slice(0, 1), slice(None), mean[2:3, 512:])
        renew(3, slice(1, 2), slice(None), mean[3:4, 512:])
        for index in range(4):
            renew(
                4, slice(0, 1), slice(index * 256, (index + 1) * 256),
                mean[4 + index : 5 + index, 512:],
            )

    @pl.when(step == pl.num_programs(0) - 1)
    def _():
        for copy in copies:
            copy.wait()


def call(
    kernel, outs, args, *, cost, in_specs=None, out_specs=None, scratch=(), limit=32, name=None
):
    return pl.pallas_call(
        kernel,
        out_shape=outs,
        in_specs=in_specs if in_specs is not None else [VM] * len(args),
        out_specs=out_specs if out_specs is not None else [VM] * len(outs),
        scratch_shapes=list(scratch),
        compiler_params=pltpu.CompilerParams(vmem_limit_bytes=limit * MIB),
        cost_estimate=estimate(cost),
        name=name,
    )(*args)


def estimate(microseconds):
    return pl.CostEstimate(
        flops=int(microseconds * 1e9), bytes_accessed=int(microseconds * 2e6), transcendentals=0
    )


def sds(shape, dtype=f32):
    return jax.ShapeDtypeStruct(shape, dtype)


def local(
    series, groups, counts, cotangent,
    embed_weight, embed_moment, embed_error, embed_start,
    attend_weight, attend_moment, attend_error, attend_start,
    mixer_weight, mixer_moment, mixer_error, mixer_start,
    inner_weight, inner_moment, inner_error, inner_start,
    outer_weight, outer_moment, outer_error, outer_start,
    embed_bias, embed_bias_moment, query_bias, query_bias_moment,
    inner_bias, inner_bias_moment, norm_gains, gains_moment, shared_biases, biases_moment,
):
    replicas = lax.axis_size("dp")
    half, windows, history = series.shape
    rows = 2 * half
    group_count, _, width = embed_weight.shape
    part = attend_weight.shape[2]
    inner_part = inner_weight.shape[1]
    units = 2 * inner_part
    turned = lambda a: a.transpose(1, 0, 2)

    def swap(values):
        return lax.ppermute(values, "mp", [(0, 1), (1, 0)])

    low = sds((rows, width), bf16)
    full = sds((rows, width))
    near = sds((half, width))
    packed = sds((half + 3 * part + 16, width), bf16)
    send_one, other_one, series_own, small, facts, send_two, cot_own = pl.pallas_call(
        prepare,
        out_shape=[
            packed, packed, sds((half, history), bf16), sds((8, inner_part)), sds((8, 128), jnp.int32),
            sds((part + 2 * inner_part + half, width), bf16), sds((half, width), bf16),
        ],
        in_specs=[HB] * 10,
        out_specs=[VM] * 7,
        scratch_shapes=[
            pltpu.SMEM(groups.shape, jnp.int32), pltpu.SMEM(counts.shape, jnp.int32),
            pltpu.VMEM(series.shape, bf16), pltpu.VMEM((3, width, part), f32),
            pltpu.VMEM(query_bias.shape, f32), pltpu.VMEM((1, inner_part), f32),
            pltpu.VMEM(cotangent.shape, bf16), pltpu.VMEM(mixer_weight.shape, f32),
            pltpu.VMEM(inner_weight.shape, f32), pltpu.VMEM(outer_weight.shape, f32),
            pltpu.SemaphoreType.DMA((10,)), pltpu.SemaphoreType.DMA((2,)), pltpu.SemaphoreType.DMA((2,)),
        ],
        compiler_params=pltpu.CompilerParams(
            collective_id=2, has_side_effects=True, vmem_limit_bytes=LIMITS[0] * MIB
        ),
        cost_estimate=estimate(7),
        name="prepare",
    )(
        *(
            pltpu.with_memory_space_constraint(a, pltpu.HBM)
            for a in (
                groups, counts, series, turned(attend_weight), query_bias, inner_bias[None],
                cotangent, mixer_weight, inner_weight, outer_weight,
            )
        )
    )
    other_two = swap(send_two)
    hidden, tokens, queries, keys, values, context, lse, small_other, table = call(
        attend_forward,
        [full, low, low, low, low, low, sds((HEADS, rows)), sds((8, inner_part)), sds((history, width), bf16)],
        (facts, series_own, embed_weight, embed_bias, send_one, other_one, small),
        limit=LIMITS[2], cost=15, scratch=[pltpu.VMEM((HEADS, rows), f32)],
        name="attend_forward",
    )
    (
        output_near, output_send, active, preact_grad, normed_low, feed_grad, attend_out, resid_one,
        context_grad, delta, sums, inner_sums, grads_send,
    ) = call(
        functools.partial(feed_forward, TILES),
        [near, near, sds((rows, inner_part), bf16), sds((rows, inner_part), bf16), low, low, low, full, low,
         sds((rows, 128), bf16), sds((8, width)), sds((8, units)),
         sds((2 * inner_part + part, width), bf16)],
        (facts, context, hidden, send_two, other_two, small, small_other, norm_gains, shared_biases, cot_own),
        limit=LIMITS[3], cost=22,
        scratch=[
            pltpu.VMEM((rows // TILES, units), bf16), pltpu.VMEM((rows, inner_part), bf16),
            pltpu.VMEM((rows, inner_part), bf16),
        ],
        name="feed_forward",
    )
    output_other = swap(output_send)
    grads_other = swap(grads_send)
    attend_near, send_three, series_near, series_far, sums_near, sums_far = call(
        attend_backward,
        [sds((3, width, part)), sds((3 * part + history, width), bf16), sds((half, history)),
         sds((half, history)), sds((16, width)), sds((16, width))],
        (facts, queries, keys, values, lse, context_grad, delta, tokens, resid_one, send_one,
         other_one, table, series_own, sums, inner_sums),
        limit=LIMITS[4], cost=22,
        scratch=[pltpu.VMEM((rows, width), bf16)] * 3,
        name="attend_backward",
    )
    other_three = swap(send_three)
    series_other = swap(series_far)
    sums_other = swap(sums_far)
    outer_matrix, inner_matrix, mixer_matrix, left_part, output = call(
        feed_matrices,
        [sds(outer_weight.shape), sds(inner_weight.shape), sds(mixer_weight.shape), sds((8, 1792)),
         sds((half, windows, width))],
        (active, preact_grad, normed_low, feed_grad, context, attend_out, grads_other,
         outer_error[0], inner_error[0], mixer_error[0], outer_start[0].T, inner_start.T, mixer_start[0].T,
         output_near, output_other),
        limit=LIMITS[5], cost=6, out_specs=[VM] * 4 + [HB],
        scratch=[pltpu.SemaphoreType.DMA((2,))],
        name="feed_matrices",
    )
    padded = max(128, -(-4096 // replicas // 128) * 128)
    total = padded * replicas
    left, right, mean, attend_matrix, embed_matrix = pl.pallas_call(
        functools.partial(reduce_factors, replicas),
        out_shape=[sds((8, 3328)), sds((8, 3328)), sds((8, 768)), sds((3, width, part)), sds(embed_weight.shape)],
        in_specs=[VM] * 14,
        out_specs=[VM] * 5,
        scratch_shapes=[
            pltpu.VMEM((8, total), f32), pltpu.VMEM((8, total), f32), pltpu.VMEM((8, total), f32),
            pltpu.VMEM((8, total), f32),
            pltpu.VMEM((replicas, 8, padded), f32), pltpu.VMEM((replicas, 8, padded), f32),
            pltpu.SemaphoreType.DMA((4,)), pltpu.SemaphoreType.DMA((4,)),
        ],
        compiler_params=pltpu.CompilerParams(
            collective_id=1, has_side_effects=True, vmem_limit_bytes=LIMITS[6] * MIB
        ),
        cost_estimate=estimate(30),
        name="reduce_factors",
    )(
        facts, attend_near, send_three, other_three, turned(attend_error[0]), embed_error[0],
        attend_start.transpose(0, 2, 1), embed_start.T, left_part, sums_near, sums_other,
        outer_matrix, inner_matrix, mixer_matrix,
    )
    matrices = (embed_matrix, outer_matrix, attend_matrix, inner_matrix, mixer_matrix)

    step_rate = base_rate * math.sqrt(replicas * 7 / (windows * rows))
    mixer_rate = step_rate * math.sqrt(width / max(width * 16 // rows, 1))
    steps = 4
    whole = lambda a: pl.BlockSpec(a.shape, lambda i: (0,) * len(a.shape))
    column = lambda a: pl.BlockSpec((a.shape[0], a.shape[1] // steps), lambda i: (0, i))
    row = lambda a: pl.BlockSpec((a.shape[0] // steps, a.shape[1]), lambda i: (i, 0))
    middle = lambda a: pl.BlockSpec((a.shape[0], a.shape[1] // steps, a.shape[2]), lambda i: (0, i, 0))
    last = lambda a: pl.BlockSpec((a.shape[0], a.shape[1], a.shape[2] // steps), lambda i: (0, 0, i))
    specs = [spec(a) for spec, a in zip((last, row, middle, row, column), matrices)]
    vectors = (embed_bias, norm_gains, shared_biases, query_bias, inner_bias[None])
    vector_moments = (
        embed_bias_moment, gains_moment, biases_moment, query_bias_moment, inner_bias_moment[None]
    )
    vector_specs = [whole(a) for a in vectors]
    factors = [
        sds((group_count, 8, history)), sds((8, 1024)), sds((8, 512)), sds((8, 512)), sds((8, 256)),
        sds((8, 512)), sds((8, 512)), sds((3, 8, part)), sds((8, 1024)), sds((8, 512)),
    ]
    found = pl.pallas_call(
        functools.partial(renew_all, step_rate, mixer_rate),
        grid=(steps,),
        out_shape=[sds(a.shape) for a in matrices] * 3 + [sds(a.shape) for a in vectors] * 2
        + factors + [sds(series.shape)],
        in_specs=[whole(left), whole(right), whole(mean), VM, VM] + [VM] * 15 + vector_specs * 2,
        out_specs=specs * 3 + vector_specs * 2 + [whole(a) for a in factors] + [HB],
        scratch_shapes=[pltpu.SemaphoreType.DMA((2,))],
        compiler_params=pltpu.CompilerParams(vmem_limit_bytes=LIMITS[7] * MIB),
        cost_estimate=estimate(12),
        name="renew_all",
    )(
        left, right, mean, series_near, series_other, *matrices,
        embed_weight, outer_weight, turned(attend_weight), inner_weight, mixer_weight,
        embed_moment, outer_moment, turned(attend_moment), inner_moment, mixer_moment,
        *vectors, *vector_moments,
    )
    errors, weights, moments = found[0:5], found[5:10], found[10:15]
    new_vectors, new_vector_moments = found[15:20], found[20:25]
    lefts, rights = found[25:30], found[30:35]
    return (
        output,
        found[35],
        weights[0],
        moments[0],
        errors[0][None],
        lefts[0].transpose(0, 2, 1),
        rights[0].T,
        turned(weights[2]),
        turned(moments[2]),
        turned(errors[2])[None],
        lefts[2].T[None],
        rights[2].transpose(0, 2, 1),
        weights[4],
        moments[4],
        errors[4][None],
        lefts[4].T,
        rights[4].T[None],
        weights[3],
        moments[3],
        errors[3][None],
        lefts[3].T[None],
        rights[3].T,
        weights[1],
        moments[1],
        errors[1][None],
        lefts[1].T,
        rights[1].T[None],
        new_vector_moments[0],
        new_vectors[0],
        new_vector_moments[3],
        new_vectors[3],
        new_vector_moments[4][0],
        new_vectors[4][0],
        new_vector_moments[1],
        new_vectors[1],
        new_vector_moments[2],
        new_vectors[2],
    )


def solution(mesh):
    return jax.shard_map(
        local,
        mesh=mesh,
        in_specs=(
            P("mp", "dp", None),
            P("dp"),
            P("dp"),
            P("mp", "dp", None),
            P(),
            P(),
            P("dp", None, None, None),
            P(),
            P(None, None, "mp"),
            P(None, None, "mp"),
            P("dp", None, None, "mp"),
            P(None, "mp", None),
            P("mp", None),
            P("mp", None),
            P("dp", "mp", None),
            P("mp", None, None),
            P(None, "mp"),
            P(None, "mp"),
            P("dp", None, "mp"),
            P("mp", None),
            P("mp", None),
            P("mp", None),
            P("dp", "mp", None),
            P("mp", None, None),
            P(),
            P(),
            P(None, "mp"),
            P(None, "mp"),
            P("mp"),
            P("mp"),
            P(),
            P(),
            P(),
            P(),
        ),
        out_specs=(
            P("mp", "dp", None),
            P("mp", "dp", None),
            P(),
            P(),
            P("dp", None, None, None),
            P(),
            P(),
            P(None, None, "mp"),
            P(None, None, "mp"),
            P("dp", None, None, "mp"),
            P("mp", None, None),
            P(None, "mp", None),
            P("mp", None),
            P("mp", None),
            P("dp", "mp", None),
            P("mp", None),
            P("mp", None, None),
            P(None, "mp"),
            P(None, "mp"),
            P("dp", None, "mp"),
            P("mp", None, None),
            P("mp", None),
            P("mp", None),
            P("mp", None),
            P("dp", "mp", None),
            P("mp", None),
            P("mp", None, None),
            P(),
            P(),
            P(None, "mp"),
            P(None, "mp"),
            P("mp"),
            P("mp"),
            P(),
            P(),
            P(),
            P(),
        ),
        check_vma=False,
    )
```

```python
import functools
import math

import jax
import jax.numpy as jnp
from jax import lax
from jax.experimental import pallas as pl
from jax.experimental.pallas import tpu as pltpu
from jax.sharding import PartitionSpec as P

HEADS = 8
momentum_decay = 0.9
norm_epsilon = 1e-05
base_rate = 0.03
inverse_root_two = 0.7071067811865476
inverse_root_tau = 0.3989422804014327
log2_e = 1.4426950408889634
ln_two = 0.6931471805599453
f32 = jnp.float32
bf16 = jnp.bfloat16
VMEM = pltpu.VMEM
VM = pl.BlockSpec(memory_space=pltpu.VMEM)
HB = pl.BlockSpec(memory_space=pltpu.HBM)
MIB = 1024 * 1024


def dot_nn(a, b):
    return lax.dot_general(a, b, (((1,), (0,)), ((), ())), preferred_element_type=f32)


def dot_nt(a, b):
    return lax.dot_general(a, b, (((1,), (1,)), ((), ())), preferred_element_type=f32)


def dot_tn(a, b):
    return lax.dot_general(a, b, (((0,), (0,)), ((), ())), preferred_element_type=f32)


def split_two(x):
    high = x.astype(bf16)
    return high, (x - high.astype(f32)).astype(bf16)


def three_way(x, lane):
    high = x.astype(bf16).astype(f32)
    rest = x - high
    middle = rest.astype(bf16).astype(f32)
    last = rest - middle
    place = lax.rem(lax.rem(lane, 64), 3)
    return jnp.where(place == 0, high, jnp.where(place == 1, middle, last)).astype(bf16)


LIMITS = (12, 14, 12, 14, 16, 8, 8, 18)
TILES = 2


def row_number(rows, position):
    half = rows // 2
    index = lax.broadcasted_iota(jnp.int32, (rows, 128), 0)
    return jnp.where(index < half, index + position * half, index - half + (1 - position) * half)


def lookback_of(group, history):
    return jnp.where(
        group == 0, history * 2 // 7, jnp.where(group == 1, history * 4 // 7, history)
    ).astype(jnp.int32)


def take_window(pair_ref, window, home, columns):
    for index in range(2):

        @pl.when(window == index)
        def _(index=index):
            home[:, columns] = pair_ref[:, index, :]


def join_copies(mine, theirs, home, done):
    position = lax.axis_index("mp")
    return [
        pltpu.make_async_copy(source, home.at[:, window, :], done.at[index])
        for index, (source, window) in enumerate(((mine, position), (theirs, 1 - position)))
    ]


def three_parts(x):
    high = x.astype(bf16)
    rest = x - high.astype(f32)
    middle = rest.astype(bf16)
    return high, middle, (rest - middle.astype(f32)).astype(bf16)


def prepare(
    groups_hbm, counts_hbm, series_hbm, attend_hbm, query_bias_hbm, inner_bias_hbm,
    cot_hbm, mixer_hbm, inner_hbm, outer_hbm,
    send, received, series_own, small, facts, send_feed, cot_own,
    groups, counts, series, attend, query_bias, inner_bias, cotangent, mixer, inner, outer,
    done, send_sems, recv_sems,
):
    position = lax.axis_index("mp")
    partner = {"mp": 1 - position}
    barrier = pltpu.get_barrier_semaphore()
    pl.semaphore_signal(barrier, inc=1, device_id=partner, device_id_type=pl.DeviceIdType.MESH)
    copies = []
    for source, target in (
        (query_bias_hbm, query_bias), (inner_bias_hbm, inner_bias), (attend_hbm, attend),
        (series_hbm, series), (groups_hbm, groups), (counts_hbm, counts), (cot_hbm, cotangent),
        (mixer_hbm, mixer), (inner_hbm, inner), (outer_hbm, outer),
    ):
        copies.append(pltpu.make_async_copy(source, target, done.at[len(copies)]))
    for copy in copies[:6]:
        copy.start()
    half, _, history = series.shape
    width = send.shape[1]
    depth = attend.shape[1] // 2
    end = half + 3 * depth
    part = query_bias.shape[1]
    trades = [
        pltpu.make_async_remote_copy(
            src_ref=send.at[place], dst_ref=received.at[place], send_sem=send_sems.at[index],
            recv_sem=recv_sems.at[index], device_id=partner, device_id_type=pl.DeviceIdType.MESH,
        )
        for index, place in enumerate(
            (
                (slice(half, end + 16), slice(None)),
                (slice(0, half), slice(0, -(-history // 128) * 128)),
            )
        )
    ]
    copies[0].wait()
    copies[1].wait()
    small[...] = jnp.zeros_like(small)
    small[0:2, :part] = query_bias[...]
    small[2:3, :] = inner_bias[...]
    values = jnp.concatenate(
        [
            jnp.concatenate([query_bias[0:1, :], query_bias[1:2, :]], axis=1),
            inner_bias[:, :width],
            inner_bias[:, width:],
            jnp.zeros((1, width), f32),
        ],
        axis=0,
    )
    send[end : end + 16, :] = jnp.concatenate(
        [*three_parts(values), jnp.zeros((4, width), bf16)], axis=0
    )
    copies[2].wait()
    for copy in copies[6:]:
        copy.start()
    for kind in range(3):
        rows = slice(half + kind * depth, half + (kind + 1) * depth)
        send[rows, :256] = attend[kind, :depth, :].astype(bf16)
        send[rows, 256:] = attend[kind, depth:, :].astype(bf16)
    pl.semaphore_wait(barrier, 1)
    trades[0].start()
    send[:half, 256:] = jnp.zeros((half, width - 256), bf16)
    copies[3].wait()
    take_window(series, 1 - position, send.at[:half], slice(0, history))
    trades[1].start()
    take_window(series, position, series_own, slice(None))
    copies[4].wait()
    copies[5].wait()
    group = jnp.where(position == 0, groups[0], groups[1])
    other_group = jnp.where(position == 0, groups[1], groups[0])
    count = jnp.where(position == 0, counts[0], counts[1])
    first = history - lookback_of(group, history)
    row = lax.broadcasted_iota(jnp.int32, facts.shape, 0)
    facts[...] = jnp.where(
        row == 0, count, jnp.where(row == 1, first, jnp.where(row == 2, group, other_group))
    )
    m, d, o = mixer.shape[0], inner.shape[0], outer.shape[0]
    copies[6].wait()
    take_window(cotangent, 1 - position, send_feed.at[m + 2 * d + o :], slice(None))
    take_window(cotangent, position, cot_own, slice(None))
    copies[7].wait()
    send_feed[:m] = mixer[...].astype(bf16)
    copies[8].wait()
    send_feed[m : m + d] = inner[:, :512].astype(bf16)
    send_feed[m + d : m + 2 * d] = inner[:, 512:].astype(bf16)
    copies[9].wait()
    send_feed[m + 2 * d : m + 2 * d + o] = outer[...].astype(bf16)
    for trade in trades:
        trade.wait()


def unpack_small(other, small_other):
    part = other.shape[1] // 2
    parts = other[other.shape[0] - 16 :, :].astype(f32)
    values = parts[0:4] + parts[4:8] + parts[8:12]
    small_other[0:1, :part] = values[0:1, :part]
    small_other[1:2, :part] = values[0:1, part:]
    small_other[2:3, : 2 * part] = values[1:2, :]
    small_other[2:3, 2 * part :] = values[2:3, :]


def attend_block(pack, half, kind):
    start = half + kind * 256
    return jnp.concatenate([pack[start : start + 256, :256], pack[start : start + 256, 256:]], axis=0)


def attend_forward(
    facts, series_own, embed, embed_bias, own, other, small,
    hidden_ref, token_ref, query_ref, key_ref, value_ref, context_ref, lse_ref, small_other, table, peak_ref,
):
    unpack_small(other, small_other)
    chosen, bias_row = embed[0], embed_bias[0:1, :]
    for group in range(1, embed.shape[0]):
        here = facts[2:3, 0:1] == group
        chosen = jnp.where(here, embed[group], chosen)
        bias_row = jnp.where(here, embed_bias[group : group + 1, :], bias_row)
    row = lax.broadcasted_iota(jnp.int32, chosen.shape, 0)
    table[...] = jnp.where(row >= facts[1:2, 0:1], chosen, 0.0).astype(bf16)
    rows, width = hidden_ref.shape
    half, history = series_own.shape
    part = width // 2
    head_dim = width // HEADS
    position, count = lax.axis_index("mp"), facts[0:1, 0:1]
    for index, block in enumerate((series_own[...], other[:half, :history])):
        values = dot_nn(block, table[...]) + bias_row
        hidden_ref[pl.ds(index * half, half), :] = values
        token_ref[pl.ds(index * half, half), :] = values.astype(bf16)
    scale = head_dim**-0.5 * log2_e
    tokens = token_ref[...]
    for index, (pack, bias) in enumerate(((own, small), (other, small_other))):
        columns = pl.ds(index * part, part)
        query_ref[:, columns] = (
            (dot_nn(tokens, attend_block(pack, half, 0)) + bias[0:1, :part]) * scale
        ).astype(bf16)
        key_ref[:, columns] = dot_nn(tokens, attend_block(pack, half, 1)).astype(bf16)
        value_ref[:, columns] = (
            dot_nn(tokens, attend_block(pack, half, 2)) + bias[1:2, :part]
        ).astype(bf16)
    lane = lax.broadcasted_iota(jnp.int32, (rows, 128), 1)
    dead = row_number(rows, position) >= count
    last = lax.rem(lane, 64) == 63
    extra_query = jnp.where(last, 1.0, 0.0).astype(bf16)
    extra_key = jnp.where(last & dead, -1e30, 0.0).astype(bf16)
    ones = jnp.ones((rows, 128), bf16)

    chooser = head_chooser(width, head_dim, 1.0)

    def longest(ref):
        values = ref[...].astype(f32)
        return jnp.max(dot_nn((values * values).astype(bf16), chooser), axis=0, keepdims=True)

    bound = jnp.max(longest(query_ref) * longest(key_ref))
    peak_ref[...] = jnp.zeros_like(peak_ref)

    @pl.when(jnp.logical_not(bound < 3600.0))
    def _():
        block = 128
        block_lane = lane[:block]

        def one_head(head, carry):
            columns = pl.ds(pl.multiple_of(head // 2 * 128, 128), 128)
            side = lax.rem(head, 2)
            query = jnp.where((lane // head_dim) == side, query_ref[:, columns], extra_query)

            def one_block(index, peak):
                place = pl.ds(pl.multiple_of(index * block, block), block)
                keys = key_ref[place, columns]
                far = lax.broadcasted_iota(jnp.int32, (block, 128), 0) + index * block
                near = jnp.where(
                    far < half, far + position * half, far - half + (1 - position) * half
                )
                mask = jnp.where(
                    (lax.rem(block_lane, 64) == 63) & (near >= count), -1e30, 0.0
                ).astype(bf16)
                scores = dot_nt(jnp.where((block_lane // head_dim) == side, keys, mask), query)
                return jnp.maximum(peak, jnp.max(scores, axis=0, keepdims=True))

            peak_ref[pl.ds(head, 1), :] = lax.fori_loop(
                0, rows // block, one_block, jnp.full((1, rows), -1e30, f32)
            )
            return carry

        lax.fori_loop(0, HEADS, one_head, 0)

    spread = part_spreader(-1.0)
    extra_query = jnp.where(
        last, 1.0, dot_tn(jnp.concatenate(three_parts(peak_ref[...]), axis=0), spread)
    ).astype(bf16)
    extra_key = jnp.where(last & dead, -1e30, 0.0).astype(bf16)
    unit = jnp.ones((rows, 128), bf16)

    def pair(index, carry):
        columns = pl.ds(pl.multiple_of(index * 128, 128), 128)
        queries = query_ref[:, columns]
        keys = key_ref[:, columns]
        values = value_ref[:, columns]
        found = []
        for side in range(2):
            mine = (lane >= head_dim) if side else (lane < head_dim)
            hot = lax.rem(lane, 64) // 3 == index * 2 + side
            scores = dot_nt(
                jnp.where(mine, keys, jnp.where(hot, unit, extra_key)),
                jnp.where(mine, queries, extra_query),
            )
            soft = jnp.exp2(scores).astype(bf16)
            mixed = dot_tn(jnp.where(mine, values, ones), soft)
            top, bottom = mixed[:head_dim], mixed[head_dim:]
            wanted, total = (bottom, top) if side else (top, bottom)
            found.append(wanted / total)
            place = pl.ds(index * 2 + side, 1)
            lse_ref[place, :] = jnp.log2(total[0:1]) + peak_ref[place, :]
        context_ref[:, columns] = jnp.concatenate(found, axis=0).T.astype(bf16)
        return carry

    lax.fori_loop(0, width // 128, pair, 0)


def part_spreader(value):
    row = lax.broadcasted_iota(jnp.int32, (3 * HEADS, 128), 0)
    lane = lax.broadcasted_iota(jnp.int32, (3 * HEADS, 128), 1)
    head = lax.rem(row, HEADS)
    wanted = lane == jnp.where(lax.rem(head, 2) == 0, 64, 0) + 3 * head + row // HEADS
    return jnp.where(wanted, value, 0.0).astype(bf16)


def head_chooser(width, head_dim, value):
    head = lax.broadcasted_iota(jnp.int32, (width, 128), 0) // head_dim
    lane = lax.broadcasted_iota(jnp.int32, (width, 128), 1)
    wanted = (lax.rem(lane, 64) // 3 == head) & ((lane >= 64) == (lax.rem(head, 2) == 0))
    return jnp.where(wanted, value, 0.0).astype(bf16)


def norm_rows(values, gain, shift):
    centered = values - jnp.mean(values, axis=-1, keepdims=True)
    inverse = lax.rsqrt(jnp.mean(centered * centered, axis=-1, keepdims=True) + norm_epsilon)
    unit = centered * inverse
    return unit * gain + shift, unit, inverse


def norm_rows_back(upstream, unit, inverse, gain):
    scaled = upstream * gain
    return inverse * (
        scaled
        - jnp.mean(scaled, axis=-1, keepdims=True)
        - unit * jnp.mean(scaled * unit, axis=-1, keepdims=True)
    )


def feed_forward(
    tiles, facts, context_ref, hidden_ref, own, other, small, small_other, gains, biases, cot_own,
    output_ref, output_send, active_near, preact_near, normed_ref, feed_ref, attend_ref, resid_ref,
    context_grad_ref, delta_ref, sums_ref, inner_sum_ref, grads_send, slope_ref, active_far, preact_far,
):
    rows, width = hidden_ref.shape
    tile = rows // tiles
    half = rows // 2
    part = width // 2
    inner_part = active_near.shape[1]
    units = 2 * inner_part
    chunk = 512
    position, count = lax.axis_index("mp"), facts[0:1, 0:1]
    sums_ref[...] = jnp.zeros_like(sums_ref)
    inner_sum_ref[...] = jnp.zeros_like(inner_sum_ref)
    at_inner = part
    at_outer = part + inner_part
    at_cot = at_outer + inner_part

    def inner_chunk(index):
        pack = (own, other)[index * chunk // inner_part]
        start = at_inner + (index * chunk % inner_part) // chunk * width
        return pack[start : start + width, :]

    def outer_chunk(index):
        pack = (own, other)[index * chunk // inner_part]
        start = at_outer + index * chunk % inner_part
        return pack[start : start + chunk, :]

    head_dim = width // HEADS
    chooser = head_chooser(width, head_dim, -1.0)

    def add(row, values):
        sums_ref[row : row + 1, :] += jnp.sum(values, axis=0, keepdims=True)

    def one_tile(step, carry):
        place = pl.ds(pl.multiple_of(step * tile, tile), tile)
        context = context_ref[place, :]
        attended = dot_nn(context[:, :part], own[:part, :]) + dot_nn(
            context[:, part:], other[:part, :]
        )
        normed, unit_one, inverse_one = norm_rows(
            hidden_ref[place, :] + attended + biases[2:3, :], gains[0:1, :], biases[0:1, :]
        )
        normed_low = normed.astype(bf16)
        normed_ref[place, :] = normed_low
        for index in range(units // chunk):
            columns = slice(index * chunk, (index + 1) * chunk)
            bias = (small, small_other)[index * chunk // inner_part]
            start = index * chunk % inner_part
            preact = dot_nn(normed_low, inner_chunk(index)) + bias[2:3, start : start + chunk]
            phi = 0.5 + 0.5 * lax.erf(preact * inverse_root_two)
            (active_near, active_far)[index * chunk // inner_part][place, start : start + chunk] = (preact * phi).astype(bf16)
            slope_ref[:, columns] = (
                phi + preact * jnp.exp2(preact * preact * (-0.5 * log2_e)) * inverse_root_tau
            ).astype(bf16)
        feed_out = dot_nn(active_near[place, :], own[at_outer:at_cot, :]) + dot_nn(
            active_far[place, :], other[at_outer:at_cot, :]
        )
        output, unit_two, inverse_two = norm_rows(
            normed + feed_out + biases[3:4, :], gains[1:2, :], biases[1:2, :]
        )
        index = lax.broadcasted_iota(jnp.int32, (tile, width), 0)

        @pl.when(step < tiles // 2)
        def _():
            output_ref[place, :] = output
        far = step - tiles // 2
        far_place = pl.ds(pl.multiple_of(jnp.maximum(far, 0) * tile, tile), tile)
        near_place = pl.ds(pl.multiple_of(jnp.minimum(step, tiles // 2 - 1) * tile, tile), tile)

        @pl.when(step >= tiles // 2)
        def _():
            output_send[far_place, :] = output
        cot = jnp.where(
            step < tiles // 2,
            cot_own[near_place, :],
            other[pl.ds(pl.multiple_of(at_cot + jnp.maximum(far, 0) * tile, 32), tile), :],
        ).astype(f32)
        first = jnp.where(
            step < tiles // 2,
            position * half + step * tile,
            (1 - position) * half + far * tile,
        )
        upstream = jnp.where(index + first < count, cot, 0.0)
        resid_two = norm_rows_back(upstream, unit_two, inverse_two, gains[1:2, :])
        feed_grad = resid_two.astype(bf16)
        feed_ref[place, :] = feed_grad
        for index in range(units // chunk):
            columns = slice(index * chunk, (index + 1) * chunk)
            grad = dot_nt(feed_grad, outer_chunk(index))
            start = index * chunk % inner_part
            (preact_near, preact_far)[index * chunk // inner_part][place, start : start + chunk] = (
                grad * slope_ref[:, columns].astype(f32)
            ).astype(bf16)
        normed_grad = resid_two
        for index in range(units // chunk):
            start = index * chunk % inner_part
            block = (preact_near, preact_far)[index * chunk // inner_part]
            normed_grad = normed_grad + dot_nt(
                block[place, start : start + chunk], inner_chunk(index)
            )
        resid_one = norm_rows_back(normed_grad, unit_one, inverse_one, gains[0:1, :])
        resid_ref[place, :] = resid_one
        attend_grad = resid_one.astype(bf16)
        attend_ref[place, :] = attend_grad
        context_grad = jnp.concatenate(
            [dot_nt(attend_grad, own[:part, :]), dot_nt(attend_grad, other[:part, :])], axis=1
        ).astype(bf16)
        context_grad_ref[place, :] = context_grad
        high, low = split_two(context_grad.astype(f32) * context.astype(f32))
        delta = dot_nn(high, chooser) + dot_nn(low, chooser)
        delta_ref[place, :] = three_way(delta, lax.broadcasted_iota(jnp.int32, (tile, 128), 1))
        add(1, normed_grad * unit_one)
        add(2, upstream * unit_two)
        add(3, normed_grad)
        add(4, upstream)
        add(5, resid_one)
        add(6, resid_two)
        for index, block in enumerate((preact_near, preact_far)):
            columns = slice(index * inner_part, (index + 1) * inner_part)
            inner_sum_ref[0:1, columns] += jnp.sum(
                block[place, :].astype(f32), axis=0, keepdims=True
            )
        return carry

    lax.fori_loop(0, tiles, one_tile, 0)
    grads_send[:inner_part, :] = dot_tn(active_far[...], feed_ref[...]).astype(bf16)
    for index in range(inner_part // chunk):
        start = index * chunk
        grads_send[inner_part + index * width : inner_part + (index + 1) * width, :] = dot_tn(
            normed_ref[...], preact_far[:, start : start + chunk]
        ).astype(bf16)
    grads_send[2 * inner_part :, :] = dot_tn(context_ref[:, part:], attend_ref[...]).astype(bf16)


def attend_backward(
    facts, query_ref, key_ref, value_ref, lse_ref, context_grad_ref, delta_ref,
    token_ref, resid_ref, own, other, table, series_own, sums_ref, inner_sum_ref,
    attend_own, send, series_near, series_far, near_out, far_out,
    dquery_ref, dkey_ref, dvalue_ref,
):
    rows, width = query_ref.shape
    head_dim = width // HEADS
    half, history = series_own.shape
    part = width // 2
    position, count = lax.axis_index("mp"), facts[0:1, 0:1]
    lane = lax.broadcasted_iota(jnp.int32, (rows, 128), 1)
    dead = row_number(rows, position) >= count
    last = lax.rem(lane, 64) == 63
    spread = part_spreader(-1.0)
    extra_query = jnp.where(
        last, 1.0, dot_tn(jnp.concatenate(three_parts(lse_ref[...]), axis=0), spread)
    ).astype(bf16)
    extra_key = jnp.where(last & dead, -1e30, 0.0).astype(bf16)
    unit = jnp.ones((rows, 128), bf16)
    extra_grad = delta_ref[...]
    nothing = jnp.zeros((rows, 128), bf16)

    def pair(index, carry):
        columns = pl.ds(pl.multiple_of(index * 128, 128), 128)
        queries = query_ref[:, columns]
        keys = key_ref[:, columns]
        values = value_ref[:, columns]
        grads = context_grad_ref[:, columns]
        softs, score_grads, own_grads, own_queries, own_keys = [], [], [], [], []
        for side in range(2):
            mine = (lane >= head_dim) if side else (lane < head_dim)
            hot = lax.rem(lane, 64) // 3 == index * 2 + side
            soft = jnp.exp2(
                dot_nt(
                    jnp.where(mine, keys, jnp.where(hot, unit, extra_key)),
                    jnp.where(mine, queries, extra_query),
                )
            )
            centered = dot_nt(
                jnp.where(mine, values, jnp.where(hot, unit, nothing)),
                jnp.where(mine, grads, extra_grad),
            )
            softs.append(soft.astype(bf16))
            score_grads.append((soft * centered).astype(bf16))
            own_grads.append(jnp.where(mine, grads, nothing))
            own_queries.append(jnp.where(mine, queries, nothing))
            own_keys.append(jnp.where(mine, keys, nothing))
        dvalue = dot_nn(jnp.concatenate(softs, axis=1), jnp.concatenate(own_grads, axis=0))
        dkey = dot_nn(jnp.concatenate(score_grads, axis=1), jnp.concatenate(own_queries, axis=0))
        dquery = dot_tn(jnp.concatenate(own_keys, axis=0), jnp.concatenate(score_grads, axis=0))
        dvalue_ref[:, columns] = dvalue.astype(bf16)
        dkey_ref[:, columns] = (dkey * ln_two).astype(bf16)
        dquery_ref[:, columns] = (dquery.T * head_dim**-0.5).astype(bf16)
        return carry

    lax.fori_loop(0, width // 128, pair, 0)

    tokens = token_ref[...]
    total = resid_ref[...]
    near_out[...] = jnp.zeros_like(near_out)
    far_out[...] = jnp.zeros_like(far_out)
    for kind, grad_ref in enumerate((dquery_ref, dkey_ref, dvalue_ref)):
        low = grad_ref[...]
        attend_own[kind] = dot_tn(tokens, low[:, :part])
        far = dot_tn(tokens, low[:, part:]).astype(bf16)
        send[kind * part : (kind + 1) * part, :part] = far[:part]
        send[kind * part : (kind + 1) * part, part:] = far[part:]
        total = (
            total
            + dot_nt(low[:, :part], attend_block(own, half, kind))
            + dot_nt(low[:, part:], attend_block(other, half, kind))
        )
        if kind != 1:
            column = jnp.sum(low.astype(f32), axis=0, keepdims=True)
            start = kind // 2 * part
            near_out[7:8, start : start + part] = column[:, :part]
            far_out[7:8, start : start + part] = column[:, part:]
    low = total.astype(bf16)
    series_near[...] = dot_nt(low[:half], table[...])
    series_far[...] = dot_nt(low[half:], table[...])
    table_grad = dot_tn(series_own[...], low[:half]) + dot_tn(other[:half, :history], low[half:])
    row = lax.broadcasted_iota(jnp.int32, table_grad.shape, 0)
    seen = row >= facts[1:2, 0:1]
    send[3 * part :, :] = jnp.where(seen, table_grad, 0.0).astype(bf16)
    shared = sums_ref[0:7, :]
    bias_grad = jnp.sum(low.astype(f32), axis=0, keepdims=True)
    near_out[0:7, :] = shared
    far_out[0:7, :] = shared
    near_out[0:1, :] = bias_grad
    far_out[0:1, :] = bias_grad
    count_near = inner_sum_ref.shape[1] // 2 // width
    for index in range(count_near):
        near_out[8 + index : 9 + index, :] = inner_sum_ref[0:1, index * width : (index + 1) * width]
        far_out[8 + index : 9 + index, :] = inner_sum_ref[
            0:1, (count_near + index) * width : (count_near + index + 1) * width
        ]


def left_product(start, matrix):
    both = dot_nt(jnp.concatenate(split_two(start), axis=0), matrix.astype(bf16))
    return both[:8] + both[8:]


def right_product(basis, matrix):
    both = dot_nn(jnp.concatenate(split_two(basis), axis=0), matrix.astype(bf16))
    return both[:8] + both[8:]


def feed_matrices(
    active_ref, preact_ref, normed_ref, feed_ref, context_ref, attend_ref, received,
    e_outer, e_inner, e_mixer, s_outer, s_inner, s_mixer, output_near, output_far,
    outer, inner, mixer, left, output, done,
):
    width = feed_ref.shape[1]
    inner_part = outer.shape[0]
    part = mixer.shape[0]
    chunk = 512
    copies = join_copies(output_near, output_far, output, done)
    for copy in copies:
        copy.start()
    outer[...] = (
        dot_tn(active_ref[...], feed_ref[...])
        + received[:inner_part, :].astype(f32)
        + e_outer[...]
    )
    for index in range(inner_part // chunk):
        columns = slice(index * chunk, (index + 1) * chunk)
        start = inner_part + index * width
        inner[:, columns] = (
            dot_tn(normed_ref[...], preact_ref[:, columns])
            + received[start : start + width, :].astype(f32)
            + e_inner[:, columns]
        )
    mixer[...] = (
        dot_tn(context_ref[:, :part], attend_ref[...])
        + received[2 * inner_part :, :].astype(f32)
        + e_mixer[...]
    )
    left[:, 0:1024] = left_product(s_outer[...], outer[...])
    left[:, 1024:1536] = left_product(s_inner[...], inner[...])
    left[:, 1536:1792] = left_product(s_mixer[...], mixer[...])
    for copy in copies:
        copy.wait()


def orthonormal_rows(blocks):
    rows = [lax.broadcasted_iota(jnp.int32, block.shape, 0) for block in blocks]
    for index in range(blocks[0].shape[0]):
        pivots = [block[index : index + 1, :] for block in blocks]
        inners = [jnp.sum(block * pivot, axis=1, keepdims=True) for block, pivot in zip(blocks, pivots)]
        sizes = [inner[index : index + 1, :] + 1e-12 for inner in inners]
        blocks = [
            jnp.where(
                row > index,
                block - pivot * (inner / size),
                jnp.where(row == index, block * lax.rsqrt(size), block),
            )
            for block, row, pivot, inner, size in zip(blocks, rows, pivots, inners, sizes)
        ]
    return blocks


def reduce_factors(
    replicas, facts, near_attend, own, received, e_attend, e_embed, s_attend, s_embed, left_part,
    near, far, outer, inner, mixer,
    left_ref, right_ref, mean_ref, attend, embed,
    start_ref, summed, partial, gathered, parts_one, parts_two, send_sems, recv_sems,
):
    me = lax.axis_index("dp")
    barrier = pltpu.get_barrier_semaphore()
    chunk = start_ref.shape[1] // replicas
    share = 1.0 / replicas

    paired = replicas & (replicas - 1) == 0

    def peer(offset):
        return jnp.bitwise_xor(me, offset) if paired else lax.rem(me + offset, replicas)

    def columns(index):
        return pl.ds(pl.multiple_of(index * chunk, 128), chunk)

    far_first = sorted(
        range(1, min(replicas, 17)), key=lambda k: -((k & 1) + (k >> 1 & 1) + (k >> 2))
    )

    def each(what):
        if replicas <= 16:
            for offset in far_first:
                what(offset)
            return

        def body(index, carry):
            what(replicas - index)
            return carry

        lax.fori_loop(1, replicas, body, 0)

    each(
        lambda offset: pl.semaphore_signal(
            barrier, inc=1, device_id={"dp": peer(offset)}, device_id_type=pl.DeviceIdType.MESH
        )
    )
    part = near_attend.shape[2]
    total = None
    for kind in range(3):
        rows = slice(kind * part, (kind + 1) * part)
        block = jnp.concatenate([received[rows, :part], received[rows, part:]], axis=0)
        attend[kind] = near_attend[kind] + block.astype(f32) + e_attend[kind]
        term = left_product(s_attend[kind], attend[kind])
        total = term if total is None else total + term
    mine, theirs = facts[2:3, 0:1], facts[3:4, 0:1]
    table_near = own[3 * part :, :].astype(f32)
    table_far = received[3 * part :, :].astype(f32)
    pieces = []
    for group in range(embed.shape[0]):
        grad = jnp.where(mine == group, table_near, 0.0) + jnp.where(theirs == group, table_far, 0.0)
        embed[group] = grad + e_embed[group]
        pieces.append(left_product(s_embed[...], embed[group]))
    used = embed.shape[0] * embed.shape[1]
    start_ref[:, 0:1024] = jnp.concatenate(pieces + [jnp.zeros((8, 1024 - used), f32)], axis=1)
    start_ref[:, 1024:2048] = left_part[:, 0:1024]
    start_ref[:, 2048:2560] = total
    start_ref[:, 2560:3328] = left_part[:, 1024:1792]
    common = near[1:7, :] + far[1:7, :]
    row = lax.broadcasted_iota(jnp.int32, (3, near.shape[1]), 0)
    bias = jnp.where(row == mine, near[0:1, :], 0.0) + jnp.where(row == theirs, far[0:1, :], 0.0)
    start_ref[:, 3328:3840] = jnp.concatenate([bias, common[:5]], axis=0)
    rest = jnp.concatenate([common[5:6], near[7:10, :] + far[7:10, :]], axis=0)
    for row in range(4):
        start_ref[2 * row : 2 * row + 1, 3840:4096] = rest[row : row + 1, :256]
        start_ref[2 * row + 1 : 2 * row + 2, 3840:4096] = rest[row : row + 1, 256:]
    if start_ref.shape[1] > 4096:
        start_ref[:, 4096:] = jnp.zeros((8, start_ref.shape[1] - 4096), f32)
    pl.semaphore_wait(barrier, replicas - 1)

    def all_sum(phase, source, parts, result):
        others = parts.at[pl.ds(1, replicas - 1)]

        def scatter(offset):
            other = peer(offset)
            return pltpu.make_async_remote_copy(
                src_ref=source.at[:, columns(other)],
                dst_ref=parts.at[offset],
                send_sem=send_sems.at[2 * phase],
                recv_sem=recv_sems.at[2 * phase],
                device_id={"dp": other},
                device_id_type=pl.DeviceIdType.MESH,
            )

        def spread(offset):
            return pltpu.make_async_remote_copy(
                src_ref=result.at[:, columns(me)],
                dst_ref=result.at[:, columns(me)],
                send_sem=send_sems.at[2 * phase + 1],
                recv_sem=recv_sems.at[2 * phase + 1],
                device_id={"dp": peer(offset)},
                device_id_type=pl.DeviceIdType.MESH,
            )

        def wait_all(semaphore):
            pltpu.make_async_copy(others, others, semaphore).wait()

        each(lambda offset: scatter(offset).start())
        wait_all(recv_sems.at[2 * phase])
        total = source[:, columns(me)]
        if replicas <= 16:
            for offset in range(1, replicas):
                total = total + parts[offset]
        else:
            total = lax.fori_loop(1, replicas, lambda offset, total: total + parts[offset], total)
        result[:, columns(me)] = total * share
        each(lambda offset: spread(offset).start())
        wait_all(recv_sems.at[2 * phase + 1])
        wait_all(send_sems.at[2 * phase])
        wait_all(send_sems.at[2 * phase + 1])

    all_sum(0, start_ref, parts_one, summed)
    mean_ref[...] = summed[:, 3328:4096]
    places = ((0, 1024), (1024, 1024), (2048, 512), (2560, 512), (3072, 256))
    bases = orthonormal_rows([summed[:, start : start + size] for start, size in places])
    for (start, size), basis in zip(places, bases):
        left_ref[:, start : start + size] = basis
    height = embed.shape[1]
    total = None
    for group in range(embed.shape[0]):
        term = right_product(bases[0][:, group * height : (group + 1) * height], embed[group])
        total = term if total is None else total + term
    partial[:, 0:512] = total
    partial[:, 512:1024] = right_product(bases[1], outer[...])
    for kind in range(3):
        partial[:, 1024 + kind * 256 : 1280 + kind * 256] = right_product(bases[2], attend[kind])
    partial[:, 1792:2816] = right_product(bases[3], inner[...])
    partial[:, 2816:3328] = right_product(bases[4], mixer[...])
    partial[:, 3328:] = jnp.zeros((8, partial.shape[1] - 3328), f32)
    all_sum(1, partial, parts_two, gathered)
    right_ref[...] = gathered[:, :3328]


def renew_all(
    step_rate, mixer_rate, left, right, mean, series_near, series_far, *refs,
):
    matrices, weights, moments = refs[0:5], refs[5:10], refs[10:15]
    vectors, vector_moments = refs[15:20], refs[20:25]
    errors, new_weights, new_moments = refs[25:30], refs[30:35], refs[35:40]
    new_vectors, new_vector_moments = refs[40:45], refs[45:50]
    lefts, rights, series_grad, done = refs[50:55], refs[55:60], refs[60], refs[61]
    step = pl.program_id(0)
    copies = join_copies(series_near, series_far, series_grad, done)

    @pl.when(step == 0)
    def _():
        for copy in copies:
            copy.start()

    def approx(basis, factor):
        left_high, left_low = split_two(basis)
        right_high, right_low = split_two(factor)
        return dot_tn(
            jnp.concatenate([left_high, left_low, left_high, left_low], axis=0),
            jnp.concatenate([right_high, right_high, right_low, right_low], axis=0),
        )

    def write(index, read, where, update, rate):
        errors[index][where] = matrices[index][read] - update
        moment = momentum_decay * moments[index][read] + update
        new_moments[index][where] = moment
        new_weights[index][where] = weights[index][read] - rate * moment

    def cut(start, size):
        return pl.ds(pl.multiple_of(start + step * size, 128), size)

    all_of = slice(None)
    every = (all_of, all_of)
    groups, height, block = errors[0].shape
    factor = right[:, cut(0, block)]
    for group in range(groups):
        write(
            0, (group, all_of, cut(0, block)), (group, all_of, all_of),
            approx(left[:, group * height : (group + 1) * height], factor), step_rate,
        )
    block = errors[1].shape[0]
    write(
        1, (cut(0, block), all_of), every, approx(left[:, cut(1024, block)], right[:, 512:1024]),
        step_rate,
    )
    block = errors[2].shape[1]
    basis = left[:, cut(2048, block)]
    for kind in range(3):
        write(
            2, (kind, cut(0, block), all_of), (kind, all_of, all_of),
            approx(basis, right[:, 1024 + kind * 256 : 1280 + kind * 256]), step_rate,
        )
    block = errors[3].shape[0]
    write(
        3, (cut(0, block), all_of), every, approx(left[:, cut(2560, block)], right[:, 1792:2816]),
        step_rate,
    )
    block = errors[4].shape[1]
    write(
        4, (all_of, cut(0, block)), every, approx(left[:, 3072:3328], right[:, cut(2816, block)]),
        mixer_rate,
    )

    @pl.when(step == 0)
    def _():
        for group in range(groups):
            lefts[0][group] = left[:, group * height : (group + 1) * height]
        lefts[1][...] = left[:, 1024:2048]
        lefts[2][...] = left[:, 2048:2560]
        lefts[3][...] = left[:, 2560:3072]
        lefts[4][...] = left[:, 3072:3328]
        rights[0][...] = right[:, 0:512]
        rights[1][...] = right[:, 512:1024]
        for kind in range(3):
            rights[2][kind] = right[:, 1024 + kind * 256 : 1280 + kind * 256]
        rights[3][...] = right[:, 1792:2816]
        rights[4][...] = right[:, 2816:3328]

        def renew(index, rows, columns, gradient):
            moment = momentum_decay * vector_moments[index][rows, columns] + gradient
            new_vector_moments[index][rows, columns] = moment
            new_vectors[index][rows, columns] = vectors[index][rows, columns] - step_rate * moment

        renew(0, slice(0, 3), slice(None), mean[0:3, :512])
        renew(1, slice(0, 2), slice(None), mean[3:5, :512])
        renew(2, slice(0, 3), slice(None), mean[5:8, :512])
        renew(2, slice(3, 4), slice(0, 256), mean[0:1, 512:])
        renew(2, slice(3, 4), slice(256, 512), mean[1:2, 512:])
        renew(3, slice(0, 1), slice(None), mean[2:3, 512:])
        renew(3, slice(1, 2), slice(None), mean[3:4, 512:])
        for index in range(4):
            renew(
                4, slice(0, 1), slice(index * 256, (index + 1) * 256),
                mean[4 + index : 5 + index, 512:],
            )

    @pl.when(step == pl.num_programs(0) - 1)
    def _():
        for copy in copies:
            copy.wait()


def call(
    kernel, outs, args, *, cost, in_specs=None, out_specs=None, scratch=(), limit=32, name=None
):
    return pl.pallas_call(
        kernel,
        out_shape=outs,
        in_specs=in_specs if in_specs is not None else [VM] * len(args),
        out_specs=out_specs if out_specs is not None else [VM] * len(outs),
        scratch_shapes=list(scratch),
        compiler_params=pltpu.CompilerParams(vmem_limit_bytes=limit * MIB),
        cost_estimate=estimate(cost),
        name=name,
    )(*args)


def estimate(microseconds):
    return pl.CostEstimate(
        flops=int(microseconds * 1e9), bytes_accessed=int(microseconds * 2e6), transcendentals=0
    )


def sds(shape, dtype=f32):
    return jax.ShapeDtypeStruct(shape, dtype)


def local(
    series, groups, counts, cotangent,
    embed_weight, embed_moment, embed_error, embed_start,
    attend_weight, attend_moment, attend_error, attend_start,
    mixer_weight, mixer_moment, mixer_error, mixer_start,
    inner_weight, inner_moment, inner_error, inner_start,
    outer_weight, outer_moment, outer_error, outer_start,
    embed_bias, embed_bias_moment, query_bias, query_bias_moment,
    inner_bias, inner_bias_moment, norm_gains, gains_moment, shared_biases, biases_moment,
):
    replicas = lax.axis_size("dp")
    half, windows, history = series.shape
    rows = 2 * half
    group_count, _, width = embed_weight.shape
    part = attend_weight.shape[2]
    inner_part = inner_weight.shape[1]
    units = 2 * inner_part
    turned = lambda a: a.transpose(1, 0, 2)

    def swap(values):
        return lax.ppermute(values, "mp", [(0, 1), (1, 0)])

    low = sds((rows, width), bf16)
    full = sds((rows, width))
    near = sds((half, width))
    packed = sds((half + 3 * part + 16, width), bf16)
    send_one, other_one, series_own, small, facts, send_two, cot_own = pl.pallas_call(
        prepare,
        out_shape=[
            packed, packed, sds((half, history), bf16), sds((8, inner_part)), sds((8, 128), jnp.int32),
            sds((part + 2 * inner_part + half, width), bf16), sds((half, width), bf16),
        ],
        in_specs=[HB] * 10,
        out_specs=[VM] * 7,
        scratch_shapes=[
            pltpu.SMEM(groups.shape, jnp.int32), pltpu.SMEM(counts.shape, jnp.int32),
            pltpu.VMEM(series.shape, bf16), pltpu.VMEM((3, width, part), f32),
            pltpu.VMEM(query_bias.shape, f32), pltpu.VMEM((1, inner_part), f32),
            pltpu.VMEM(cotangent.shape, bf16), pltpu.VMEM(mixer_weight.shape, f32),
            pltpu.VMEM(inner_weight.shape, f32), pltpu.VMEM(outer_weight.shape, f32),
            pltpu.SemaphoreType.DMA((10,)), pltpu.SemaphoreType.DMA((2,)), pltpu.SemaphoreType.DMA((2,)),
        ],
        compiler_params=pltpu.CompilerParams(
            collective_id=2, has_side_effects=True, vmem_limit_bytes=LIMITS[0] * MIB
        ),
        cost_estimate=estimate(7),
        name="prepare",
    )(
        *(
            pltpu.with_memory_space_constraint(a, pltpu.HBM)
            for a in (
                groups, counts, series, turned(attend_weight), query_bias, inner_bias[None],
                cotangent, mixer_weight, inner_weight, outer_weight,
            )
        )
    )
    other_two = swap(send_two)
    hidden, tokens, queries, keys, values, context, lse, small_other, table = call(
        attend_forward,
        [full, low, low, low, low, low, sds((HEADS, rows)), sds((8, inner_part)), sds((history, width), bf16)],
        (facts, series_own, embed_weight, embed_bias, send_one, other_one, small),
        limit=LIMITS[2], cost=15, scratch=[pltpu.VMEM((HEADS, rows), f32)],
        name="attend_forward",
    )
    (
        output_near, output_send, active, preact_grad, normed_low, feed_grad, attend_out, resid_one,
        context_grad, delta, sums, inner_sums, grads_send,
    ) = call(
        functools.partial(feed_forward, TILES),
        [near, near, sds((rows, inner_part), bf16), sds((rows, inner_part), bf16), low, low, low, full, low,
         sds((rows, 128), bf16), sds((8, width)), sds((8, units)),
         sds((2 * inner_part + part, width), bf16)],
        (facts, context, hidden, send_two, other_two, small, small_other, norm_gains, shared_biases, cot_own),
        limit=LIMITS[3], cost=22,
        scratch=[
            pltpu.VMEM((rows // TILES, units), bf16), pltpu.VMEM((rows, inner_part), bf16),
            pltpu.VMEM((rows, inner_part), bf16),
        ],
        name="feed_forward",
    )
    output_other = swap(output_send)
    grads_other = swap(grads_send)
    attend_near, send_three, series_near, series_far, sums_near, sums_far = call(
        attend_backward,
        [sds((3, width, part)), sds((3 * part + history, width), bf16), sds((half, history)),
         sds((half, history)), sds((16, width)), sds((16, width))],
        (facts, queries, keys, values, lse, context_grad, delta, tokens, resid_one, send_one,
         other_one, table, series_own, sums, inner_sums),
        limit=LIMITS[4], cost=22,
        scratch=[pltpu.VMEM((rows, width), bf16)] * 3,
        name="attend_backward",
    )
    other_three = swap(send_three)
    series_other = swap(series_far)
    sums_other = swap(sums_far)
    outer_matrix, inner_matrix, mixer_matrix, left_part, output = call(
        feed_matrices,
        [sds(outer_weight.shape), sds(inner_weight.shape), sds(mixer_weight.shape), sds((8, 1792)),
         sds((half, windows, width))],
        (active, preact_grad, normed_low, feed_grad, context, attend_out, grads_other,
         outer_error[0], inner_error[0], mixer_error[0], outer_start[0].T, inner_start.T, mixer_start[0].T,
         output_near, output_other),
        limit=LIMITS[5], cost=6, out_specs=[VM] * 4 + [HB],
        scratch=[pltpu.SemaphoreType.DMA((2,))],
        name="feed_matrices",
    )
    padded = max(128, -(-4096 // replicas // 128) * 128)
    total = padded * replicas
    left, right, mean, attend_matrix, embed_matrix = pl.pallas_call(
        functools.partial(reduce_factors, replicas),
        out_shape=[sds((8, 3328)), sds((8, 3328)), sds((8, 768)), sds((3, width, part)), sds(embed_weight.shape)],
        in_specs=[VM] * 14,
        out_specs=[VM] * 5,
        scratch_shapes=[
            pltpu.VMEM((8, total), f32), pltpu.VMEM((8, total), f32), pltpu.VMEM((8, total), f32),
            pltpu.VMEM((8, total), f32),
            pltpu.VMEM((replicas, 8, padded), f32), pltpu.VMEM((replicas, 8, padded), f32),
            pltpu.SemaphoreType.DMA((4,)), pltpu.SemaphoreType.DMA((4,)),
        ],
        compiler_params=pltpu.CompilerParams(
            collective_id=1, has_side_effects=True, vmem_limit_bytes=LIMITS[6] * MIB
        ),
        cost_estimate=estimate(30),
        name="reduce_factors",
    )(
        facts, attend_near, send_three, other_three, turned(attend_error[0]), embed_error[0],
        attend_start.transpose(0, 2, 1), embed_start.T, left_part, sums_near, sums_other,
        outer_matrix, inner_matrix, mixer_matrix,
    )
    matrices = (embed_matrix, outer_matrix, attend_matrix, inner_matrix, mixer_matrix)

    step_rate = base_rate * math.sqrt(replicas * 7 / (windows * rows))
    mixer_rate = step_rate * math.sqrt(width / max(width * 16 // rows, 1))
    steps = 4
    whole = lambda a: pl.BlockSpec(a.shape, lambda i: (0,) * len(a.shape))
    column = lambda a: pl.BlockSpec((a.shape[0], a.shape[1] // steps), lambda i: (0, i))
    row = lambda a: pl.BlockSpec((a.shape[0] // steps, a.shape[1]), lambda i: (i, 0))
    middle = lambda a: pl.BlockSpec((a.shape[0], a.shape[1] // steps, a.shape[2]), lambda i: (0, i, 0))
    last = lambda a: pl.BlockSpec((a.shape[0], a.shape[1], a.shape[2] // steps), lambda i: (0, 0, i))
    specs = [spec(a) for spec, a in zip((last, row, middle, row, column), matrices)]
    vectors = (embed_bias, norm_gains, shared_biases, query_bias, inner_bias[None])
    vector_moments = (
        embed_bias_moment, gains_moment, biases_moment, query_bias_moment, inner_bias_moment[None]
    )
    vector_specs = [whole(a) for a in vectors]
    factors = [
        sds((group_count, 8, history)), sds((8, 1024)), sds((8, 512)), sds((8, 512)), sds((8, 256)),
        sds((8, 512)), sds((8, 512)), sds((3, 8, part)), sds((8, 1024)), sds((8, 512)),
    ]
    found = pl.pallas_call(
        functools.partial(renew_all, step_rate, mixer_rate),
        grid=(steps,),
        out_shape=[sds(a.shape) for a in matrices] * 3 + [sds(a.shape) for a in vectors] * 2
        + factors + [sds(series.shape)],
        in_specs=[whole(left), whole(right), whole(mean), VM, VM] + [VM] * 15 + vector_specs * 2,
        out_specs=specs * 3 + vector_specs * 2 + [whole(a) for a in factors] + [HB],
        scratch_shapes=[pltpu.SemaphoreType.DMA((2,))],
        compiler_params=pltpu.CompilerParams(vmem_limit_bytes=LIMITS[7] * MIB),
        cost_estimate=estimate(12),
        name="renew_all",
    )(
        left, right, mean, series_near, series_other, *matrices,
        embed_weight, outer_weight, turned(attend_weight), inner_weight, mixer_weight,
        embed_moment, outer_moment, turned(attend_moment), inner_moment, mixer_moment,
        *vectors, *vector_moments,
    )
    errors, weights, moments = found[0:5], found[5:10], found[10:15]
    new_vectors, new_vector_moments = found[15:20], found[20:25]
    lefts, rights = found[25:30], found[30:35]
    return (
        output,
        found[35],
        weights[0],
        moments[0],
        errors[0][None],
        lefts[0].transpose(0, 2, 1),
        rights[0].T,
        turned(weights[2]),
        turned(moments[2]),
        turned(errors[2])[None],
        lefts[2].T[None],
        rights[2].transpose(0, 2, 1),
        weights[4],
        moments[4],
        errors[4][None],
        lefts[4].T,
        rights[4].T[None],
        weights[3],
        moments[3],
        errors[3][None],
        lefts[3].T[None],
        rights[3].T,
        weights[1],
        moments[1],
        errors[1][None],
        lefts[1].T,
        rights[1].T[None],
        new_vector_moments[0],
        new_vectors[0],
        new_vector_moments[3],
        new_vectors[3],
        new_vector_moments[4][0],
        new_vectors[4][0],
        new_vector_moments[1],
        new_vectors[1],
        new_vector_moments[2],
        new_vectors[2],
    )


def solution(mesh):
    return jax.shard_map(
        local,
        mesh=mesh,
        in_specs=(
            P("mp", "dp", None),
            P("dp"),
            P("dp"),
            P("mp", "dp", None),
            P(),
            P(),
            P("dp", None, None, None),
            P(),
            P(None, None, "mp"),
            P(None, None, "mp"),
            P("dp", None, None, "mp"),
            P(None, "mp", None),
            P("mp", None),
            P("mp", None),
            P("dp", "mp", None),
            P("mp", None, None),
            P(None, "mp"),
            P(None, "mp"),
            P("dp", None, "mp"),
            P("mp", None),
            P("mp", None),
            P("mp", None),
            P("dp", "mp", None),
            P("mp", None, None),
            P(),
            P(),
            P(None, "mp"),
            P(None, "mp"),
            P("mp"),
            P("mp"),
            P(),
            P(),
            P(),
            P(),
        ),
        out_specs=(
            P("mp", "dp", None),
            P("mp", "dp", None),
            P(),
            P(),
            P("dp", None, None, None),
            P(),
            P(),
            P(None, None, "mp"),
            P(None, None, "mp"),
            P("dp", None, None, "mp"),
            P("mp", None, None),
            P(None, "mp", None),
            P("mp", None),
            P("mp", None),
            P("dp", "mp", None),
            P("mp", None),
            P("mp", None, None),
            P(None, "mp"),
            P(None, "mp"),
            P("dp", None, "mp"),
            P("mp", None, None),
            P("mp", None),
            P("mp", None),
            P("mp", None),
            P("dp", "mp", None),
            P("mp", None),
            P("mp", None, None),
            P(),
            P(),
            P(None, "mp"),
            P(None, "mp"),
            P("mp"),
            P("mp"),
            P(),
            P(),
            P(),
            P(),
        ),
        check_vma=False,
    )
```
